256 devices in a mesh: img: 2 (over y_lo), slab: 128 (over y_hi, x, z, core).
Axes of the slice: x: 4, y: 4 (y_hi: 2, y_lo: 2; y = y_hi * 2 + y_lo), z: 8, core: 2. Of those that a mesh axis runs over, the one named last changes fastest.
Arguments:
- images: float32 [16384, 128, 128], P(('img', 'slab')), may hold values from 0.05 to 5
- orient: int32 [16384], P(('img', 'slab')), may hold values from 0 to 511, as said below
- sharp: float32 [16384], P(('img', 'slab')), may hold values from 0.05 to 2
- density: bfloat16 [512, 512, 512], P('slab', None, 'img'), may hold values from -6 to 6
- support: int32 [512, 512, 512], P('slab', None, 'img'), may hold values 0 or 1
Outputs:
- updated: float32 [512, 512, 512], P('slab', None, 'img')
The draws below stay inside these ranges and needn't reach their ends.
Inputs may be any that keep to these rules, and one draw needn't show every extreme that they name: `orient`: snapshot n's centre plane lies among the 4 planes that begin at 4 times ((n // 64) mod the number of slabs); the first snapshot's centre is plane 0 and the last one's plane 512 - 1.
All inputs are finite; a program needn't handle non-finite values. No bound on the sum of `support` on one device may be relied on, other than what follows from the above.
Results may differ from the reference program's by a relative error of at most 0.0075.
The reference program's roundings to bfloat16 on the way (of `amplitude`) count: a program that leaves them out, or rounds other values in their place, can miss the bound.
Values may be sent and summed in bfloat16 or wider, within the bound.
A program may use at most 64 MiB of HBM per device.

```python
import math
import jax
import jax.numpy as jnp
from jax import lax

GZ = 512
GY = 512
GX = 512
P_SIZE = 128
NS = 64
NSNAP = 16384
ZL = 4
HALF = 4


def draw_orient(key, part):
    key = jax.random.fold_in(key, 11)
    number = jnp.arange(NSNAP, dtype=jnp.int32)
    block = number // NS % (GZ // ZL)
    offset = jax.random.randint(key, (NSNAP,), 0, ZL, dtype=jnp.int32)
    offset = offset.at[0].set(0)
    offset = offset.at[NSNAP - 1].set(ZL - 1)
    return (block * ZL + offset).astype(jnp.int32)


def plant(drawn, stream_key, low, top_value):
    index_at = [jax.random.randint(jax.random.fold_in(stream_key, axis), (), 0, length) for axis, length in enumerate(drawn.shape)]
    longest = drawn.shape.index(max(drawn.shape))
    beside = index_at[:longest] + [(index_at[longest] + 1) % drawn.shape[longest]] + index_at[longest + 1:]
    return drawn.at[tuple(index_at)].set(low).at[tuple(beside)].set(top_value)


def block_scale(stream_key, dims, shards, low, top_value):
    factor_of = 1.0
    for axis_at, parts in shards:
        heights = jax.random.uniform(jax.random.fold_in(jax.random.fold_in(stream_key, 6), axis_at), (parts,), jnp.float32, low / len(shards), top_value / len(shards))
        factor_of = factor_of * jnp.repeat(jnp.exp(heights), dims[axis_at] // parts).reshape((-1,) + (1,) * (len(dims) - 1 - axis_at))
    return factor_of


def scatter_about(rng, shape, width, bound, split=(), kind=jnp.bfloat16):
    array = jax.random.normal(rng, shape, jnp.float32) * width
    if len(split) > 0:
        array = block_scale(rng, shape, split, -0.22, 0.18) * array
    return jnp.clip(array, min=-bound, max=bound).astype(kind)


def setup_inputs(seed: int = 0) -> dict:
    arg_keys = jax.random.split(jax.random.key(seed), 6)
    return {
        "images": jnp.clip(jnp.exp(math.log(5.0) - 4.6051702 * jax.random.uniform(arg_keys[0], (NSNAP, P_SIZE, P_SIZE), jnp.float32) ** block_scale(arg_keys[0], (NSNAP, P_SIZE, P_SIZE), ((0, 256),), -0.2, 0.2)), 0.05, 5.0),
        "orient": draw_orient(jax.random.fold_in(arg_keys[5], 71), 0),
        "sharp": jnp.clip(jnp.exp(math.log(2.0) - 3.6888794 * jax.random.uniform(arg_keys[2], (NSNAP,), jnp.float32) ** block_scale(arg_keys[2], (NSNAP,), ((0, 256),), -0.2, 0.2)), 0.05, 2.0),
        "density": scatter_about(arg_keys[3], (GZ, GY, GX), 1.0, 6.0, ((0, 128), (2, 2))),
        "support": plant((jax.random.randint(arg_keys[4], (GZ, GY, GX), 0, 2) < 1).astype(jnp.int32), jax.random.fold_in(arg_keys[4], 1), 0, 1),
    }


least_modulus = 0.5
feedback = 0.9

def dft_tables(length):
    index = jnp.arange(length, dtype=jnp.int32)
    product = index[:, None] * index[None, :] % length
    angles = product.astype(jnp.float32) * (2.0 * math.pi / length)
    factor = 1.0 / math.sqrt(length)
    return ((jnp.cos(angles) * factor).astype(jnp.bfloat16), (jnp.sin(angles) * factor).astype(jnp.bfloat16))

def interpolation(cells, pixels):
    grid = jnp.arange(cells, dtype=jnp.float32)
    detector = jnp.arange(pixels, dtype=jnp.float32)
    position = (grid + 0.5) * (pixels / cells) - 0.5
    return jnp.maximum(0.0, 1.0 - jnp.abs(position[:, None] - detector[None, :]))

def band_weights(sharp, reach):
    offsets = jnp.arange(-reach, reach + 1).astype(jnp.float32)
    raw = jnp.exp(-sharp[:, None] * (offsets * offsets)[None, :])
    return raw / lax.optimization_barrier(jnp.sum(raw, axis=1, keepdims=True))

def section(form, first, second):
    return jnp.einsum(form, first.astype(jnp.float32), second.astype(jnp.float32))

def reference(images, orient, sharp, density, support):
    weights = band_weights(sharp, HALF)
    flat = images.reshape(NSNAP, P_SIZE * P_SIZE)
    planes = jnp.zeros((GZ + 2 * HALF, P_SIZE * P_SIZE), jnp.float32)
    for offset in range(2 * HALF + 1):
        planes = planes + jax.ops.segment_sum(weights[:, offset, None] * flat, (orient + offset).astype(jnp.int32), num_segments=GZ + 2 * HALF)
    merged = planes[HALF:HALF + GZ].reshape(GZ, P_SIZE, P_SIZE)
    across_y = interpolation(GY, P_SIZE)
    across_x = interpolation(GX, P_SIZE)
    rows = jnp.einsum('yp,zpq->zyq', across_y, merged, precision=lax.Precision.HIGHEST)
    intensity = GZ / NSNAP * jnp.einsum('zyq,xq->zyx', rows, across_x, precision=lax.Precision.HIGHEST)
    amplitude = jnp.sqrt(intensity).astype(jnp.bfloat16)
    cos_y, sin_y = dft_tables(GY)
    cos_x, sin_x = dft_tables(GX)
    cos_z, sin_z = dft_tables(GZ)
    real_y = section('jy,zyx->zjx', cos_y, density).astype(jnp.bfloat16)
    imag_y = (-section('jy,zyx->zjx', sin_y, density)).astype(jnp.bfloat16)
    real_x = (section('zyx,kx->zyk', real_y, cos_x) + section('zyx,kx->zyk', imag_y, sin_x)).astype(jnp.bfloat16)
    imag_x = (section('zyx,kx->zyk', imag_y, cos_x) - section('zyx,kx->zyk', real_y, sin_x)).astype(jnp.bfloat16)
    real_z = section('kz,zyx->kyx', cos_z, real_x) + section('kz,zyx->kyx', sin_z, imag_x)
    imag_z = section('kz,zyx->kyx', cos_z, imag_x) - section('kz,zyx->kyx', sin_z, real_x)
    modulus = jnp.sqrt(real_z * real_z + imag_z * imag_z)
    factor = amplitude.astype(jnp.float32) / jnp.maximum(modulus, least_modulus)
    proj_real = (real_z * factor).astype(jnp.bfloat16)
    proj_imag = (imag_z * factor).astype(jnp.bfloat16)
    back_real = (section('kz,zyx->kyx', cos_z, proj_real) - section('kz,zyx->kyx', sin_z, proj_imag)).astype(jnp.bfloat16)
    back_imag = (section('kz,zyx->kyx', cos_z, proj_imag) + section('kz,zyx->kyx', sin_z, proj_real)).astype(jnp.bfloat16)
    out_real = (section('zyx,kx->zyk', back_real, cos_x) - section('zyx,kx->zyk', back_imag, sin_x)).astype(jnp.bfloat16)
    out_imag = (section('zyx,kx->zyk', back_imag, cos_x) + section('zyx,kx->zyk', back_real, sin_x)).astype(jnp.bfloat16)
    projected = section('jy,zyx->zjx', cos_y, out_real) - section('jy,zyx->zjx', sin_y, out_imag)
    previous = density.astype(jnp.float32)
    return jnp.where(support == 1, projected, previous - feedback * projected)
```

```python
import math

import jax
import jax.numpy as jnp
import ml_dtypes
import numpy as np
from jax import lax
from jax.sharding import PartitionSpec as P

GZ = 512
GY = 512
GX = 512
PIX = 128
REACH = 4

least_modulus = 0.5
feedback = 0.9


def dft_tables(length):
    index = np.arange(length, dtype=np.int64)
    product = (index[:, None] * index[None, :]) % length
    angles = product.astype(np.float32) * np.float32(2.0 * math.pi / length)
    factor = np.float32(1.0 / math.sqrt(length))
    return (
        (np.cos(angles) * factor).astype(ml_dtypes.bfloat16),
        (np.sin(angles) * factor).astype(ml_dtypes.bfloat16),
    )


def interpolation(cells, pixels):
    grid = np.arange(cells, dtype=np.float32)
    detector = np.arange(pixels, dtype=np.float32)
    position = (grid + np.float32(0.5)) * np.float32(pixels / cells) - np.float32(0.5)
    return np.maximum(
        np.float32(0.0), np.float32(1.0) - np.abs(position[:, None] - detector[None, :])
    )


def bf(table):
    return np.asarray(table).astype(ml_dtypes.bfloat16)


COS, SIN = dft_tables(GY)
HALF = GY // 2
FORWARD_Y = np.stack([COS[:HALF], np.concatenate([COS[HALF : HALF + 1], -SIN[1:HALF]])])
_two = 2.0 * COS[:, :HALF].astype(np.float32)
_two[:, 0] = COS[:, 0]
_sin = -2.0 * SIN[:, :HALF].astype(np.float32)
_sin[:, 0] = COS[:, HALF]
BACK_Y = np.stack([bf(_two), bf(_sin)])
COS_X = np.concatenate([COS, SIN], axis=0)
FORWARD_X = np.concatenate(
    [np.concatenate([COS, -SIN], axis=1), np.concatenate([SIN, COS], axis=1)], axis=0
)
BACK_X = np.concatenate(
    [np.concatenate([COS, SIN], axis=1), np.concatenate([-SIN, COS], axis=1)], axis=0
)
_across = interpolation(GY, PIX)
_mirror = (-np.arange(GY)) % GY
_partner = _mirror[:HALF].copy()
_partner[0] = HALF
ACROSS_Y = bf(np.stack([_across[:HALF], _across[_partner]]))
ACROSS_X = bf(_across)
ACROSS_X_MIRROR = bf(_across[_mirror])
MIRROR = bf(np.eye(GZ, dtype=np.float32)[_mirror])


def band_weights(sharp, reach):
    offsets = jnp.arange(-reach, reach + 1).astype(jnp.float32)
    raw = jnp.exp(-sharp[:, None] * (offsets * offsets)[None, :])
    return raw / jnp.sum(raw, axis=1, keepdims=True)


def dot(first, second):
    return jnp.dot(first, second, preferred_element_type=jnp.float32)


def own_planes(planes, images, slabs, image_index, depth):
    axes = ("img", "slab")
    share = depth // images
    total = lax.dynamic_slice_in_dim(planes, depth + image_index * share, share, 0)
    for shift in (-1, 0, 1):
        for turn in range(images):
            if shift == 0 and turn == 0:
                continue
            target = (image_index + turn) % images
            piece = lax.dynamic_slice_in_dim(
                planes, (1 + shift) * depth + target * share, share, 0
            )
            pairs = [
                (i * slabs + s, (i + turn) % images * slabs + s + shift)
                for i in range(images)
                for s in range(slabs)
                if 0 <= s + shift < slabs
            ]
            total = total + lax.ppermute(piece, axes, pairs)
    return total


def amplitudes(rows, across, scale):
    return jnp.sqrt(scale * dot(rows, across.T)).astype(jnp.bfloat16).astype(jnp.float32)


def project(real_x, imag_x, amplitude):
    real_z = dot(COS, real_x) + dot(SIN, imag_x)
    imag_z = dot(COS, imag_x) - dot(SIN, real_x)
    modulus = jnp.sqrt(real_z * real_z + imag_z * imag_z)
    factor = amplitude / jnp.maximum(modulus, least_modulus)
    proj_real = (real_z * factor).astype(jnp.bfloat16)
    proj_imag = (imag_z * factor).astype(jnp.bfloat16)
    back_real = (dot(COS, proj_real) - dot(SIN, proj_imag)).astype(jnp.bfloat16)
    back_imag = (dot(COS, proj_imag) + dot(SIN, proj_real)).astype(jnp.bfloat16)
    return back_real, back_imag


def body(images, orient, sharp, density, support):
    depth, rows_all, width_own = density.shape
    count = images.shape[0]
    image_count = lax.axis_size("img")
    slabs = lax.axis_size("slab")
    devices = image_count * slabs
    slab_index = lax.axis_index("slab")
    image_index = lax.axis_index("img")
    axes = ("img", "slab")
    scale = depth / (count * image_count)

    weights = band_weights(sharp, REACH)
    local = orient - slab_index * depth
    plane_ids = jnp.arange(depth + 2 * REACH, dtype=jnp.int32)
    offsets = jnp.arange(2 * REACH + 1, dtype=jnp.int32)
    hits = plane_ids[:, None, None] == local[None, :, None] + offsets[None, None, :]
    mixing = jnp.sum(jnp.where(hits, weights[None, :, :], 0.0), axis=2)
    planes = jnp.dot(
        mixing,
        images.reshape(count, PIX * PIX),
        precision=lax.Precision.HIGH,
        preferred_element_type=jnp.float32,
    )
    mine = own_planes(planes, image_count, slabs, image_index, depth)
    share = mine.shape[0]
    mine = mine.reshape(share, PIX, PIX).astype(jnp.bfloat16)
    expanded = jnp.einsum(
        "ejp,zpq->jezq", ACROSS_Y, mine, preferred_element_type=jnp.float32
    ).astype(jnp.bfloat16)
    expanded = lax.all_to_all(
        expanded.reshape(devices, 2 * share, PIX), axes, split_axis=0, concat_axis=0, tiled=True
    )
    expanded = (
        expanded.reshape(image_count, slabs, 2, share, PIX)
        .transpose(2, 1, 0, 3, 4)
        .reshape(2, GZ, PIX)
    )

    spectrum = jnp.einsum(
        "cjy,zyx->jczx", FORWARD_Y, density, preferred_element_type=jnp.float32
    ).astype(jnp.bfloat16)
    lines = lax.all_to_all(
        spectrum.reshape(devices, 2 * depth, width_own), axes, split_axis=0, concat_axis=0, tiled=True
    )
    lines = (
        lines.reshape(image_count, slabs, 2, depth, width_own)
        .transpose(1, 3, 2, 0, 4)
        .reshape(GZ, 2 * GX)
    )
    first, second = expanded[0], expanded[1]
    first_mirror = dot(MIRROR, first).astype(jnp.bfloat16)
    second_mirror = dot(MIRROR, second).astype(jnp.bfloat16)

    def usual(lines, first, second, first_mirror, second_mirror):
        both = dot(lines, FORWARD_X).astype(jnp.bfloat16)
        amplitude = 0.5 * (
            amplitudes(first, ACROSS_X, scale) + amplitudes(second_mirror, ACROSS_X_MIRROR, scale)
        )
        back_real, back_imag = project(both[:, :GX], both[:, GX:], amplitude)
        return dot(jnp.concatenate([back_real, back_imag], axis=1), BACK_X).astype(jnp.bfloat16)

    def real_rows(lines, first, second, first_mirror, second_mirror):
        out = []
        for part, near, far in ((0, first, first_mirror), (1, second, second_mirror)):
            line = lines[:, part * GX : (part + 1) * GX]
            both = dot(line, FORWARD_X[:GX]).astype(jnp.bfloat16)
            amplitude = 0.5 * (
                amplitudes(near, ACROSS_X, scale) + amplitudes(far, ACROSS_X_MIRROR, scale)
            )
            back_real, back_imag = project(both[:, :GX], both[:, GX:], amplitude)
            out.append(
                dot(jnp.concatenate([back_real, back_imag], axis=1), BACK_X[:, :GX]).astype(
                    jnp.bfloat16
                )
            )
        return jnp.concatenate(out, axis=1)

    special = jnp.logical_and(slab_index == 0, image_index == 0)
    out = lax.cond(
        special, real_rows, usual, lines, first, second, first_mirror, second_mirror
    )
    out = (
        out.reshape(slabs, depth, 2, image_count, width_own)
        .transpose(3, 0, 2, 1, 4)
        .reshape(devices, 2 * depth, width_own)
    )
    out = lax.all_to_all(out, axes, split_axis=0, concat_axis=0, tiled=True)
    out = out.reshape(devices, 2, depth, width_own)
    projected = jnp.einsum("cyj,jczx->zyx", BACK_Y, out, preferred_element_type=jnp.float32)
    previous = density.astype(jnp.float32)
    return jnp.where(support == 1, projected, previous - feedback * projected)


def solution(mesh):
    placed = (
        P(("img", "slab"), None, None),
        P(("img", "slab")),
        P(("img", "slab")),
        P("slab", None, "img"),
        P("slab", None, "img"),
    )
    return jax.shard_map(
        body, mesh=mesh, in_specs=placed, out_specs=P("slab", None, "img"), check_vma=False
    )
```

```python
import functools
import math

import jax
import jax.numpy as jnp
import ml_dtypes
import numpy as np
from jax import lax
from jax.experimental import pallas as pl
from jax.experimental.pallas import tpu as pltpu
from jax.sharding import PartitionSpec as P

GZ = 512
GY = 512
GX = 512
PIX = 128

least_modulus = 0.5
feedback = 0.9


def dft_tables(length):
    index = np.arange(length, dtype=np.int64)
    product = (index[:, None] * index[None, :]) % length
    angles = product.astype(np.float32) * np.float32(2.0 * math.pi / length)
    factor = np.float32(1.0 / math.sqrt(length))
    return (
        (np.cos(angles) * factor).astype(ml_dtypes.bfloat16),
        (np.sin(angles) * factor).astype(ml_dtypes.bfloat16),
    )


def interpolation(cells, pixels):
    grid = np.arange(cells, dtype=np.float32)
    detector = np.arange(pixels, dtype=np.float32)
    position = (grid + np.float32(0.5)) * np.float32(pixels / cells) - np.float32(0.5)
    return np.maximum(
        np.float32(0.0), np.float32(1.0) - np.abs(position[:, None] - detector[None, :])
    )


def bf(table):
    return np.asarray(table).astype(ml_dtypes.bfloat16)


COS, SIN = dft_tables(GY)
HALF = GY // 2
_y, _x, _z, _c = np.meshgrid(np.arange(4), np.arange(4), np.arange(8), np.arange(2), indexing="ij")
ROW_OF = 32 * _z + 8 * _y + 2 * _x + _c
_imag = np.concatenate([COS[HALF : HALF + 1], -SIN[1:HALF]])
FORWARD_Y = np.stack(
    [COS[:HALF][ROW_OF.reshape(4, 64)], _imag[ROW_OF.reshape(4, 64)]], axis=1
).reshape(4, 128, GY)
_two = 2.0 * COS[:, :HALF].astype(np.float32)
_two[:, 0] = COS[:, 0]
_sin = -2.0 * SIN[:, :HALF].astype(np.float32)
_sin[:, 0] = COS[:, HALF]
BACK_Y = np.stack(
    [bf(t.reshape(GY, 8, 32).transpose(0, 2, 1).reshape(GY, HALF)) for t in (_two, _sin)]
)
FORWARD_X = np.concatenate(
    [np.concatenate([COS, -SIN], axis=1), np.concatenate([SIN, COS], axis=1)], axis=0
)
BACK_X = np.concatenate(
    [np.concatenate([COS, SIN], axis=1), np.concatenate([-SIN, COS], axis=1)], axis=0
)
_across = interpolation(GY, PIX)
_mirror = (-np.arange(GY)) % GY
ACROSS_X = bf(_across)
ACROSS_X_MIRROR = bf(_across[_mirror])
_yh, _xx, _cc, _zz, _z4 = np.meshgrid(
    np.arange(2), np.arange(4), np.arange(2), np.arange(8), np.arange(4), indexing="ij"
)
Z_ORDER = (4 * (64 * _yh + 16 * _xx + 2 * _zz + _cc) + _z4).reshape(-1)
_yh, _yl, _xx, _cc, _zz, _p2 = np.meshgrid(
    np.arange(2), np.arange(2), np.arange(4), np.arange(2), np.arange(8), np.arange(2), indexing="ij"
)
K_ORDER = (4 * (64 * _yh + 16 * _xx + 2 * _zz + _cc) + 2 * _yl + _p2).reshape(-1)
COS_Z = COS[K_ORDER][:, Z_ORDER]
SIN_Z = SIN[K_ORDER][:, Z_ORDER]
COS_B = COS[:, K_ORDER]
SIN_B = SIN[:, K_ORDER]
MIRROR = bf(K_ORDER[None, :] == _mirror[K_ORDER][:, None])
WINDOWS = np.zeros((2, 32, 2, 2, 16), np.float32)
for _m in range(32):
    for _r in range(16):
        WINDOWS[:, _m, 0, 0, _r] = max(0.0, 1.0 - abs(_m / 4 + 3.625 - _r))
        WINDOWS[:, _m, 1, 1, _r] = max(0.0, 1.0 - abs(11.625 - _m / 4 - _r))
WINDOWS[1, 0, 1, 1, :] = 0.0
WINDOWS[1, 0, 1, 1, 0:2] = (0.375, 0.625)
WINDOWS = bf(WINDOWS.reshape(2, 64, 32))

MESH = pl.DeviceIdType.MESH


def dot(first, second):
    return jnp.dot(first, second, preferred_element_type=jnp.float32)


def place():
    slab = lax.axis_index("slab")
    return (slab // 64) * 2 + lax.axis_index("img"), (slab // 16) % 4, (slab // 2) % 8, slab % 2


def device(y, x, z, c):
    return (y % 2, (y // 2) * 64 + x * 16 + z * 2 + c)


def greet(others):
    barrier = pltpu.get_barrier_semaphore()
    for other in others:
        pl.semaphore_signal(barrier, inc=1, device_id=other, device_id_type=MESH)
    return lambda: pl.semaphore_wait(barrier, len(others))


class Exchange:
    def __init__(self, x_ref, a_ref, r_ref, sems):
        self.x_ref, self.a_ref, self.r_ref = x_ref, a_ref, r_ref
        self.local, self.z_send, self.z_recv, self.p_send, self.p_recv, self.own = sems
        self.y, self.x, self.z, self.c = place()
        self.m = (self.y * 4 + self.x) * 2 + self.c

    def along_z(self, k, step):
        row, depth = (self.y + k) % 4, (self.z + step) % 8
        return pltpu.make_async_remote_copy(
            src_ref=self.x_ref.at[row, :, depth],
            dst_ref=self.a_ref.at[row, :, self.z],
            send_sem=self.z_send.at[k],
            recv_sem=self.z_recv.at[k],
            device_id=device(self.y, self.x, depth, self.c),
            device_id_type=MESH,
        )

    def keep(self, k):
        row = (self.y + k) % 4
        return pltpu.make_async_copy(
            self.x_ref.at[row, :, self.z], self.a_ref.at[row, :, self.z], self.local.at[k]
        )

    def whole(self, k):
        row = (self.y + k) % 4
        return pltpu.make_async_remote_copy(
            src_ref=self.x_ref.at[row, :, pl.ds(0, 7)],
            dst_ref=self.a_ref.at[row, :, pl.ds(0, 7)],
            send_sem=self.z_send.at[k],
            recv_sem=self.z_recv.at[k],
            device_id=device(self.y, self.x, (self.z + 1) % 8, self.c),
            device_id_type=MESH,
        )

    def start(self, k):
        for step in (4, 1, 7, 2, 6, 3, 5):
            self.along_z(k, step).start()
        self.keep(k).start()

    def spread(self, k):
        self.keep(k).wait()
        self.whole(k).wait_recv()
        row = (self.y + k) % 4
        for dx in (2, 1, 3, 0):
            for dc in (0, 1):
                if (k, dx, dc) == (0, 0, 0):
                    self.mine().start()
                    continue
                column, core = (self.x + dx) % 4, (self.c + dc) % 2
                pltpu.make_async_remote_copy(
                    src_ref=self.a_ref.at[row, column, :, core],
                    dst_ref=self.r_ref.at[self.m],
                    send_sem=self.p_send,
                    recv_sem=self.p_recv,
                    device_id=device(row, column, self.z, core),
                    device_id_type=MESH,
                ).start()

    def mine(self):
        return pltpu.make_async_copy(
            self.a_ref.at[self.y, self.x, :, self.c], self.r_ref.at[self.m], self.own
        )

    def finish(self):
        for k in range(4):
            self.whole(k).wait_send()
        self.mine().wait()
        rest = pltpu.make_async_remote_copy(
            src_ref=self.r_ref.at[pl.ds(0, 31)],
            dst_ref=self.r_ref.at[pl.ds(0, 31)],
            send_sem=self.p_send,
            recv_sem=self.p_recv,
            device_id=device(self.y, self.x, (self.z + 1) % 8, self.c),
            device_id_type=MESH,
        )
        rest.wait_send()
        rest.wait_recv()


EXCHANGE_SEMS = [pltpu.SemaphoreType.DMA((4,))] * 3 + [pltpu.SemaphoreType.DMA] * 3
BLOCKS = (4, 4, 8, 2, 16, 128)
ORDER = (1, 2, 3, 0)


def partners():
    y, x, z, c = place()
    return [device(y, x, (z + d) % 8, c) for d in range(1, 8)] + [
        device((y + d // 8) % 4, (x + d // 2 % 4) % 4, z, (c + d) % 2) for d in range(1, 32)
    ]


def back_kernel(x_ref, r_ref, a_ref, *sems):
    entered = greet(partners())
    exchange = Exchange(x_ref, a_ref, r_ref, sems)
    entered()
    for k in ORDER:
        exchange.start(k)
    for k in ORDER:
        exchange.spread(k)
    exchange.finish()


def back_exchange(blocks):
    return pl.pallas_call(
        back_kernel,
        out_shape=jax.ShapeDtypeStruct((32, 8, 16, 128), jnp.bfloat16),
        in_specs=[pl.BlockSpec(memory_space=pltpu.VMEM)],
        out_specs=pl.BlockSpec(memory_space=pltpu.VMEM),
        scratch_shapes=[pltpu.VMEM(BLOCKS, jnp.bfloat16)] + EXCHANGE_SEMS,
        compiler_params=pltpu.CompilerParams(
            collective_id=2, has_side_effects=True, vmem_limit_bytes=16 << 20
        ),
    )(blocks)


def forward_kernel(
    density, table, windows, orient, sharp, images,
    r_ref, e_ref,
    x_ref, a_ref, stage, held, parts, sent, got, padded, g_ref, h_ref, made, whole_rows,
    load, c_send, c_recv, g_send, g_recv, g_own, e_send, e_recv, e_own, *sems,
):
    y, x, z, c = place()
    image = lax.axis_index("img")
    slab = lax.axis_index("slab")
    m = (y * 4 + x) * 2 + c

    def beside(shift, turn):
        return ((image + turn) % 2, (slab + shift + 128) % 128)

    moves = [(shift, turn) for shift in (-1, 0, 1) for turn in (0, 1) if (shift, turn) != (0, 0)]
    entered = greet(partners() + [beside(*move) for move in moves])
    fetch = pltpu.make_async_copy(images, held, load)
    fetch.start()
    exchange = Exchange(x_ref, a_ref, r_ref, sems)

    def transform(k):
        row = (y + k) % 4
        for plane in range(4):
            out = dot(table[row], density[plane])
            for part in range(2):
                for side in range(2):
                    stage[pl.ds(plane * 4 + part * 2 + side, 64, stride=16), :] = out[
                        part * 64 : part * 64 + 64, side * 128 : side * 128 + 128
                    ]
        x_ref[row] = stage[...].astype(jnp.bfloat16).reshape(4, 8, 2, 16, 128)

    transform(1)
    entered()
    exchange.start(1)
    for k in (2, 3):
        transform(k)
        exchange.start(k)
    transform(0)

    near = orient[...] - slab * 4
    steps = lax.broadcasted_iota(jnp.int32, (16, 64), 0) - 4 - near
    squares = (steps * steps).astype(jnp.float32)
    raw = jnp.exp(-sharp[...] * squares)
    total = 1.0 + 2.0 * (
        jnp.exp(-sharp[...])
        + jnp.exp(-4.0 * sharp[...])
        + jnp.exp(-9.0 * sharp[...])
        + jnp.exp(-16.0 * sharp[...])
    )
    mixing = jnp.where(jnp.abs(steps) <= 4, raw / total, 0.0)
    high = mixing.astype(jnp.bfloat16)
    low = (mixing - high.astype(jnp.float32)).astype(jnp.bfloat16)
    factors = jnp.concatenate(
        [
            jnp.concatenate([high, high], axis=1),
            jnp.concatenate([low, jnp.zeros_like(low)], axis=1),
        ],
        axis=0,
    )
    fetch.wait()

    def mix(index, carry):
        at = index * 2
        rows = jnp.concatenate(
            [held[pl.ds(at, 64, stride=128), :], held[pl.ds(at + 1, 64, stride=128), :]], axis=1
        )
        upper = rows.astype(jnp.bfloat16)
        lower = (rows - upper.astype(jnp.float32)).astype(jnp.bfloat16)
        out = dot(factors, jnp.concatenate([upper, lower], axis=0))
        out = out[:16] + out[16:]
        parts[pl.ds(at, 16, stride=128), :] = out[:, :128]
        parts[pl.ds(at + 1, 16, stride=128), :] = out[:, 128:]
        return carry

    lax.fori_loop(0, 64, mix, 0)
    sent[...] = parts[...].astype(jnp.bfloat16).reshape(16, 128, 128)

    def gift(index, shift, turn):
        first = 4 + 4 * shift + 2 * ((image + turn) % 2)
        return pltpu.make_async_remote_copy(
            src_ref=sent.at[pl.ds(first, 2)],
            dst_ref=got.at[index],
            send_sem=c_send.at[index],
            recv_sem=c_recv.at[index],
            device_id=beside(shift, turn),
            device_id_type=MESH,
        )

    gifts = [gift(index, *move) for index, move in enumerate(moves)]
    for copy in gifts:
        copy.start()
    exchange.spread(1)
    for copy in gifts:
        copy.wait()
    padded[...] = jnp.zeros_like(padded)
    for plane in range(2):
        own = sent[4 + 2 * image + plane].astype(jnp.float32)
        for index, (shift, turn) in enumerate(moves):
            piece = got[index, plane].astype(jnp.float32)
            if shift:
                source = slab - shift
                piece = jnp.where(jnp.logical_and(source >= 0, source < 128), piece, 0.0)
            own = own + piece
        padded[plane, pl.ds(16, 128), :] = own
        for depth in range(8):
            g_ref[depth, plane, pl.ds(0, 16), :] = padded[
                plane, pl.ds(16 + 8 * depth - 4, 16), :
            ].astype(jnp.bfloat16)
            mirrored = padded[plane, pl.ds(16 + 116 - 8 * depth, 16), :]
            if depth == 0:
                mirrored = jnp.concatenate([own[63:65], mirrored[2:]], axis=0)
            g_ref[depth, plane, pl.ds(16, 16), :] = mirrored.astype(jnp.bfloat16)

    def window(step):
        depth = (z + step) % 8
        return pltpu.make_async_remote_copy(
            src_ref=g_ref.at[depth],
            dst_ref=h_ref.at[z],
            send_sem=g_send,
            recv_sem=g_recv,
            device_id=device(y, x, depth, c),
            device_id_type=MESH,
        )

    for step in (4, 1, 7, 2, 6, 3, 5):
        window(step).start()
    stay = pltpu.make_async_copy(g_ref.at[z], h_ref.at[z], g_own)
    stay.start()
    exchange.start(0)
    exchange.spread(2)
    stay.wait()
    seven = pltpu.make_async_remote_copy(
        src_ref=g_ref.at[pl.ds(0, 7)],
        dst_ref=h_ref.at[pl.ds(0, 7)],
        send_sem=g_send,
        recv_sem=g_recv,
        device_id=device(y, x, (z + 1) % 8, c),
        device_id_type=MESH,
    )
    seven.wait_send()
    seven.wait_recv()
    weights = windows[jnp.where(z == 0, 1, 0)]
    for source in range(8):
        for plane in range(2):
            made[pl.ds(source * 2 + plane, 64, stride=16), :] = dot(weights, h_ref[source, plane])
    whole_rows[...] = made[...].astype(jnp.bfloat16).reshape(32, 2, 16, 128)
    for d in range(1, 32):
        row, column, core = (y + d // 8) % 4, (x + d // 2 % 4) % 4, (c + d) % 2
        pltpu.make_async_remote_copy(
            src_ref=whole_rows.at[(row * 4 + column) * 2 + core],
            dst_ref=e_ref.at[m],
            send_sem=e_send,
            recv_sem=e_recv,
            device_id=device(row, column, z, core),
            device_id_type=MESH,
        ).start()
    kept = pltpu.make_async_copy(whole_rows.at[m], e_ref.at[m], e_own)
    kept.start()
    exchange.spread(3)
    exchange.spread(0)
    kept.wait()
    others = pltpu.make_async_remote_copy(
        src_ref=whole_rows.at[pl.ds(0, 31)],
        dst_ref=e_ref.at[pl.ds(0, 31)],
        send_sem=e_send,
        recv_sem=e_recv,
        device_id=device(y, x, (z + 1) % 8, c),
        device_id_type=MESH,
    )
    others.wait_send()
    others.wait_recv()
    exchange.finish()


def forward_exchange(density, orient, sharp, images):
    vmem = pl.BlockSpec(memory_space=pltpu.VMEM)
    bfloat, single = jnp.bfloat16, jnp.float32
    one = pltpu.SemaphoreType.DMA
    return pl.pallas_call(
        forward_kernel,
        out_shape=[
            jax.ShapeDtypeStruct((32, 8, 16, 128), bfloat),
            jax.ShapeDtypeStruct((32, 2, 16, 128), bfloat),
        ],
        in_specs=[vmem] * 5 + [pl.BlockSpec(memory_space=pl.ANY)],
        out_specs=[vmem] * 2,
        scratch_shapes=[
            pltpu.VMEM(BLOCKS, bfloat),
            pltpu.VMEM(BLOCKS, bfloat),
            pltpu.VMEM((1024, 128), single),
            pltpu.VMEM((64 * 128, 128), single),
            pltpu.VMEM((16 * 128, 128), single),
            pltpu.VMEM((16, 128, 128), bfloat),
            pltpu.VMEM((5, 2, 128, 128), bfloat),
            pltpu.VMEM((2, 160, 128), single),
            pltpu.VMEM((8, 2, 32, 128), bfloat),
            pltpu.VMEM((8, 2, 32, 128), bfloat),
            pltpu.VMEM((1024, 128), single),
            pltpu.VMEM((32, 2, 16, 128), bfloat),
            one, one((5,)), one((5,)), one, one, one, one, one, one,
        ]
        + EXCHANGE_SEMS,
        compiler_params=pltpu.CompilerParams(
            collective_id=1, has_side_effects=True, vmem_limit_bytes=32 << 20
        ),
    )(
        density,
        FORWARD_Y,
        WINDOWS,
        orient.reshape(1, -1),
        sharp.reshape(1, -1),
        images.reshape(-1, PIX),
    )


def amplitudes(rows, across, scale):
    return jnp.sqrt(scale * dot(rows, across.T)).astype(jnp.bfloat16).astype(jnp.float32)


def project(real_x, imag_x, amplitude):
    real_z = dot(COS_Z, real_x) + dot(SIN_Z, imag_x)
    imag_z = dot(COS_Z, imag_x) - dot(SIN_Z, real_x)
    modulus = jnp.sqrt(real_z * real_z + imag_z * imag_z)
    factor = amplitude / jnp.maximum(modulus, least_modulus)
    proj_real = (real_z * factor).astype(jnp.bfloat16)
    proj_imag = (imag_z * factor).astype(jnp.bfloat16)
    back_real = (dot(COS_B, proj_real) - dot(SIN_B, proj_imag)).astype(jnp.bfloat16)
    back_imag = (dot(COS_B, proj_imag) + dot(SIN_B, proj_real)).astype(jnp.bfloat16)
    return back_real, back_imag


def body(images, orient, sharp, density, support):
    depth, rows_all, width_own = density.shape
    count = images.shape[0]
    image_count = lax.axis_size("img")
    slab_index = lax.axis_index("slab")
    image_index = lax.axis_index("img")
    scale = depth / (count * image_count)

    lines, expanded = forward_exchange(density, orient, sharp, images)
    lines = (
        lines.reshape(2, 2, 4, 2, 8, 4, 2, 2, 128)
        .transpose(0, 2, 3, 4, 5, 6, 1, 7, 8)
        .reshape(GZ, 2 * GX)
    )
    expanded = expanded.reshape(32, 2, 16, PIX).transpose(1, 0, 2, 3).reshape(2, GZ, PIX)
    first, second = expanded[0], expanded[1]
    first_mirror = dot(MIRROR, first).astype(jnp.bfloat16)
    second_mirror = dot(MIRROR, second).astype(jnp.bfloat16)

    def usual(lines, first, second, first_mirror, second_mirror):
        both = dot(lines, FORWARD_X).astype(jnp.bfloat16)
        amplitude = 0.5 * (
            amplitudes(first, ACROSS_X, scale) + amplitudes(second_mirror, ACROSS_X_MIRROR, scale)
        )
        back_real, back_imag = project(both[:, :GX], both[:, GX:], amplitude)
        return dot(jnp.concatenate([back_real, back_imag], axis=1), BACK_X).astype(jnp.bfloat16)

    def real_rows(lines, first, second, first_mirror, second_mirror):
        out = []
        for part, near, far in ((0, first, first_mirror), (1, second, second_mirror)):
            line = lines[:, part * GX : (part + 1) * GX]
            both = dot(line, FORWARD_X[:GX]).astype(jnp.bfloat16)
            amplitude = 0.5 * (
                amplitudes(near, ACROSS_X, scale) + amplitudes(far, ACROSS_X_MIRROR, scale)
            )
            back_real, back_imag = project(both[:, :GX], both[:, GX:], amplitude)
            out.append(
                dot(jnp.concatenate([back_real, back_imag], axis=1), BACK_X[:, :GX]).astype(
                    jnp.bfloat16
                )
            )
        return jnp.concatenate(out, axis=1)

    special = jnp.logical_and(slab_index == 0, image_index == 0)
    out = lax.cond(
        special, real_rows, usual, lines, first, second, first_mirror, second_mirror
    )
    blocks = out.reshape(2, 4, 8, 2, depth, 2, 2, 2, 128).transpose(0, 6, 1, 2, 3, 4, 5, 7, 8)
    out = back_exchange(blocks.reshape(BLOCKS))
    projected = jnp.einsum(
        "cyj,jzchl->zyhl",
        BACK_Y,
        out.reshape(HALF, depth, 2, 2, 128),
        preferred_element_type=jnp.float32,
    ).reshape(depth, GY, width_own)
    previous = density.astype(jnp.float32)
    return jnp.where(support == 1, projected, previous - feedback * projected)


def solution(mesh):
    placed = (
        P(("img", "slab"), None, None),
        P(("img", "slab")),
        P(("img", "slab")),
        P("slab", None, "img"),
        P("slab", None, "img"),
    )
    return jax.shard_map(
        body, mesh=mesh, in_specs=placed, out_specs=P("slab", None, "img"), check_vma=False
    )
```

```python
import functools
import math

import jax
import jax.numpy as jnp
import ml_dtypes
import numpy as np
from jax import lax
from jax.experimental import pallas as pl
from jax.experimental.pallas import tpu as pltpu
from jax.sharding import PartitionSpec as P

GZ = 512
GY = 512
GX = 512
PIX = 128

least_modulus = 0.5
feedback = 0.9


def dft_tables(length):
    index = np.arange(length, dtype=np.int64)
    product = (index[:, None] * index[None, :]) % length
    angles = product.astype(np.float32) * np.float32(2.0 * math.pi / length)
    factor = np.float32(1.0 / math.sqrt(length))
    return (
        (np.cos(angles) * factor).astype(ml_dtypes.bfloat16),
        (np.sin(angles) * factor).astype(ml_dtypes.bfloat16),
    )


def interpolation(cells, pixels):
    grid = np.arange(cells, dtype=np.float32)
    detector = np.arange(pixels, dtype=np.float32)
    position = (grid + np.float32(0.5)) * np.float32(pixels / cells) - np.float32(0.5)
    return np.maximum(
        np.float32(0.0), np.float32(1.0) - np.abs(position[:, None] - detector[None, :])
    )


def bf(table):
    return np.asarray(table).astype(ml_dtypes.bfloat16)


COS, SIN = dft_tables(GY)
HALF = GY // 2
_y, _x, _z, _c = np.meshgrid(np.arange(4), np.arange(4), np.arange(8), np.arange(2), indexing="ij")
ROW_OF = 32 * _z + 8 * _y + 2 * _x + _c
_imag = np.concatenate([COS[HALF : HALF + 1], -SIN[1:HALF]])
FORWARD_Y = np.stack(
    [COS[:HALF][ROW_OF.reshape(4, 64)], _imag[ROW_OF.reshape(4, 64)]], axis=1
).reshape(4, 128, GY)
_two = 2.0 * COS[:, :HALF].astype(np.float32)
_two[:, 0] = COS[:, 0]
_sin = -2.0 * SIN[:, :HALF].astype(np.float32)
_sin[:, 0] = COS[:, HALF]
BACK_Y = np.stack(
    [bf(t.reshape(GY, 8, 32).transpose(0, 2, 1).reshape(GY, HALF)) for t in (_two, _sin)]
)
BACK_Y = np.concatenate([BACK_Y[0], BACK_Y[1]], axis=1)
COS_X, SIN_X = COS.reshape(2, 256, GX), SIN.reshape(2, 256, GX)
COS_R, SIN_R = (t.reshape(GX, 2, 256).transpose(1, 0, 2) for t in (COS, SIN))
_across = interpolation(GY, PIX)
_mirror = (-np.arange(GY)) % GY
ACROSS_X = np.stack([bf(_across.T), bf(_across[_mirror].T)])
EDGE_IN = np.zeros((2, GX, 128), np.float32)
EDGE_OUT = np.zeros((2, 128, GX), np.float32)
EDGE_ACROSS = np.zeros((2, PIX, 128), np.float32)
for _e in range(2):
    EDGE_IN[_e, :, _e] = COS[:, GX // 2].astype(np.float32)
    EDGE_OUT[_e, _e, :] = COS[GX // 2].astype(np.float32)
    EDGE_ACROSS[_e, :, _e] = _across[GX // 2]
EDGE_IN = bf(EDGE_IN.reshape(2, 2, 256, 128))
EDGE_OUT = bf(EDGE_OUT.reshape(2, 128, 2, 256).transpose(0, 2, 1, 3))
EDGE_ACROSS = bf(EDGE_ACROSS)
_yh, _xx, _cc, _zz, _z4 = np.meshgrid(
    np.arange(2), np.arange(4), np.arange(2), np.arange(8), np.arange(4), indexing="ij"
)
Z_ORDER = (4 * (64 * _yh + 16 * _xx + 2 * _zz + _cc) + _z4).reshape(-1)
_yh, _yl, _xx, _cc, _zz, _p2 = np.meshgrid(
    np.arange(2), np.arange(2), np.arange(4), np.arange(2), np.arange(8), np.arange(2), indexing="ij"
)
K_ORDER = (4 * (64 * _yh + 16 * _xx + 2 * _zz + _cc) + 2 * _yl + _p2).reshape(-1)
COS_Z = COS[K_ORDER][:, Z_ORDER].reshape(4, 128, GZ)
SIN_Z = SIN[K_ORDER][:, Z_ORDER].reshape(4, 128, GZ)
COS_B = COS[:, K_ORDER].reshape(2, 256, GZ)
SIN_B = SIN[:, K_ORDER].reshape(2, 256, GZ)
MIRROR = bf(K_ORDER[None, :] == _mirror[K_ORDER][:, None])
WINDOWS = np.zeros((2, 32, 2, 2, 16), np.float32)
for _m in range(32):
    for _r in range(16):
        WINDOWS[:, _m, 0, 0, _r] = max(0.0, 1.0 - abs(_m / 4 + 3.625 - _r))
        WINDOWS[:, _m, 1, 1, _r] = max(0.0, 1.0 - abs(11.625 - _m / 4 - _r))
WINDOWS[1, 0, 1, 1, :] = 0.0
WINDOWS[1, 0, 1, 1, 0:2] = (0.375, 0.625)
WINDOWS = bf(WINDOWS.reshape(2, 64, 32))

MESH = pl.DeviceIdType.MESH


def dot(first, second):
    return jnp.dot(first, second, preferred_element_type=jnp.float32)


def place():
    slab = lax.axis_index("slab")
    return (slab // 64) * 2 + lax.axis_index("img"), (slab // 16) % 4, (slab // 2) % 8, slab % 2


def device(y, x, z, c):
    return (y % 2, (y // 2) * 64 + x * 16 + z * 2 + c)


def greet(others):
    barrier = pltpu.get_barrier_semaphore()
    for other in others:
        pl.semaphore_signal(barrier, inc=1, device_id=other, device_id_type=MESH)
    return lambda: pl.semaphore_wait(barrier, len(others))


class Exchange:
    def __init__(self, x_ref, a_ref, r_ref, sems):
        self.x_ref, self.a_ref, self.r_ref = x_ref, a_ref, r_ref
        self.local, self.z_send, self.z_recv, self.p_send, self.p_recv, self.own = sems
        self.y, self.x, self.z, self.c = place()
        self.m = (self.y * 4 + self.x) * 2 + self.c

    def along_z(self, k, step):
        row, depth = (self.y + k) % 4, (self.z + step) % 8
        return pltpu.make_async_remote_copy(
            src_ref=self.x_ref.at[row, :, depth],
            dst_ref=self.a_ref.at[row, :, self.z],
            send_sem=self.z_send.at[k],
            recv_sem=self.z_recv.at[k],
            device_id=device(self.y, self.x, depth, self.c),
            device_id_type=MESH,
        )

    def keep(self, k):
        row = (self.y + k) % 4
        return pltpu.make_async_copy(
            self.x_ref.at[row, :, self.z], self.a_ref.at[row, :, self.z], self.local.at[k]
        )

    def whole(self, k):
        row = (self.y + k) % 4
        return pltpu.make_async_remote_copy(
            src_ref=self.x_ref.at[row, :, pl.ds(0, 7)],
            dst_ref=self.a_ref.at[row, :, pl.ds(0, 7)],
            send_sem=self.z_send.at[k],
            recv_sem=self.z_recv.at[k],
            device_id=device(self.y, self.x, (self.z + 1) % 8, self.c),
            device_id_type=MESH,
        )

    def start(self, k):
        for step in (4, 1, 7, 2, 6, 3, 5):
            self.along_z(k, step).start()
        self.keep(k).start()

    def spread(self, k):
        self.keep(k).wait()
        self.whole(k).wait_recv()
        row = (self.y + k) % 4
        for dx in (2, 1, 3, 0):
            for dc in (0, 1):
                if (k, dx, dc) == (0, 0, 0):
                    self.mine().start()
                    continue
                column, core = (self.x + dx) % 4, (self.c + dc) % 2
                pltpu.make_async_remote_copy(
                    src_ref=self.a_ref.at[row, column, :, core],
                    dst_ref=self.r_ref.at[self.m],
                    send_sem=self.p_send,
                    recv_sem=self.p_recv.at[k],
                    device_id=device(row, column, self.z, core),
                    device_id_type=MESH,
                ).start()

    def mine(self):
        return pltpu.make_async_copy(
            self.a_ref.at[self.y, self.x, :, self.c], self.r_ref.at[self.m], self.own
        )

    def arrived(self, k):
        count = 8 if k else 7
        if not k:
            self.mine().wait()
        pltpu.make_async_remote_copy(
            src_ref=self.r_ref.at[pl.ds(0, count)],
            dst_ref=self.r_ref.at[pl.ds(0, count)],
            send_sem=self.p_send,
            recv_sem=self.p_recv.at[k],
            device_id=device(self.y, self.x, (self.z + 1) % 8, self.c),
            device_id_type=MESH,
        ).wait_recv()
        return (self.y + 4 - k) % 4

    def finish(self):
        for k in range(4):
            self.whole(k).wait_send()
        pltpu.make_async_remote_copy(
            src_ref=self.r_ref.at[pl.ds(0, 31)],
            dst_ref=self.r_ref.at[pl.ds(0, 31)],
            send_sem=self.p_send,
            recv_sem=self.p_recv.at[0],
            device_id=device(self.y, self.x, (self.z + 1) % 8, self.c),
            device_id_type=MESH,
        ).wait_send()


EXCHANGE_SEMS = [
    pltpu.SemaphoreType.DMA((4,)),
    pltpu.SemaphoreType.DMA((4,)),
    pltpu.SemaphoreType.DMA((4,)),
    pltpu.SemaphoreType.DMA,
    pltpu.SemaphoreType.DMA((4,)),
    pltpu.SemaphoreType.DMA,
]
BLOCKS = (4, 4, 8, 2, 16, 128)
ORDER = (1, 2, 3, 0)


def partners():
    y, x, z, c = place()
    return [device(y, x, (z + d) % 8, c) for d in range(1, 8)] + [
        device((y + d // 8) % 4, (x + d // 2 % 4) % 4, z, (c + d) % 2) for d in range(1, 32)
    ]


TABLES = (
    FORWARD_Y, COS_X, SIN_X, MIRROR, ACROSS_X, COS_Z, SIN_Z, COS_B, SIN_B, COS_R, SIN_R,
    EDGE_IN, EDGE_OUT, EDGE_ACROSS,
)


def step_kernel(scale, windows, orient, sharp, density_in, images, *rest):
    count = len(TABLES)
    sources, (out_ref,), rest = rest[:count], rest[count : count + 1], rest[count + 1 :]
    tables, rest = rest[:count], rest[count:]
    (
        density, r_ref, e_ref,
        x_ref, a_ref, stage, held, parts, sent, got, padded, g_ref, h_ref, made, whole_rows,
        x_back, a_back, sum_re, sum_im, sum_edge, line_re, line_im, line_edge, amplitude, amplitude_edge,
        proj_re, proj_im, edge_re, edge_im, back_re, back_im, back_edge,
        d_load, t_load, load, c_send, c_recv, g_send, g_recv, g_own, e_send, e_recv, e_own, *sems,
    ) = rest
    (
        table, cos_x, sin_x, mirror, across_x, cos_z, sin_z, cos_b, sin_b, cos_r, sin_r,
        edge_in, edge_out, edge_across,
    ) = tables
    y, x, z, c = place()
    image = lax.axis_index("img")
    slab = lax.axis_index("slab")
    m = (y * 4 + x) * 2 + c
    both_real = jnp.logical_and(slab == 0, image == 0)
    usual = jnp.logical_not(both_real)

    def beside(shift, turn):
        return ((image + turn) % 2, (slab + shift + 128) % 128)

    moves = [(shift, turn) for shift in (-1, 0, 1) for turn in (0, 1) if (shift, turn) != (0, 0)]
    entered = greet(partners() + [beside(*move) for move in moves])
    fills = [
        pltpu.make_async_copy(sources[i], tables[i], t_load.at[i]) for i in range(len(TABLES))
    ]
    density_fill = pltpu.make_async_copy(density_in, density, d_load)
    fetch = pltpu.make_async_copy(images, held, load)
    fills[0].start()
    density_fill.start()
    fetch.start()
    for fill in fills[1:]:
        fill.start()
    exchange = Exchange(x_ref, a_ref, r_ref, sems[:6])
    back = Exchange(x_back, a_back, out_ref, sems[6:])
    fills[0].wait()
    density_fill.wait()

    def transform(k):
        row = (y + k) % 4
        for plane in range(4):
            out = dot(table[row], density[plane])
            for part in range(2):
                for side in range(2):
                    stage[pl.ds(plane * 4 + part * 2 + side, 64, stride=16), :] = out[
                        part * 64 : part * 64 + 64, side * 128 : side * 128 + 128
                    ]
        x_ref[row] = stage[...].astype(jnp.bfloat16).reshape(4, 8, 2, 16, 128)

    transform(1)
    entered()
    exchange.start(1)
    for k in (2, 3):
        transform(k)
        exchange.start(k)
    transform(0)

    near = orient[...] - slab * 4
    steps = lax.broadcasted_iota(jnp.int32, (16, 64), 0) - 4 - near
    squares = (steps * steps).astype(jnp.float32)
    raw = jnp.exp(-sharp[...] * squares)
    total = 1.0 + 2.0 * (
        jnp.exp(-sharp[...])
        + jnp.exp(-4.0 * sharp[...])
        + jnp.exp(-9.0 * sharp[...])
        + jnp.exp(-16.0 * sharp[...])
    )
    mixing = jnp.where(jnp.abs(steps) <= 4, raw / total, 0.0)
    high = mixing.astype(jnp.bfloat16)
    low = (mixing - high.astype(jnp.float32)).astype(jnp.bfloat16)
    factors = jnp.concatenate(
        [
            jnp.concatenate([high, high], axis=1),
            jnp.concatenate([low, jnp.zeros_like(low)], axis=1),
        ],
        axis=0,
    )
    fetch.wait()

    def mix(index, carry):
        at = index * 2
        rows = jnp.concatenate(
            [held[pl.ds(at, 64, stride=128), :], held[pl.ds(at + 1, 64, stride=128), :]], axis=1
        )
        upper = rows.astype(jnp.bfloat16)
        lower = (rows - upper.astype(jnp.float32)).astype(jnp.bfloat16)
        out = dot(factors, jnp.concatenate([upper, lower], axis=0))
        out = out[:16] + out[16:]
        parts[pl.ds(at, 16, stride=128), :] = out[:, :128]
        parts[pl.ds(at + 1, 16, stride=128), :] = out[:, 128:]
        return carry

    lax.fori_loop(0, 64, mix, 0)
    sent[...] = parts[...].astype(jnp.bfloat16).reshape(16, 128, 128)

    def gift(index, shift, turn):
        first = 4 + 4 * shift + 2 * ((image + turn) % 2)
        return pltpu.make_async_remote_copy(
            src_ref=sent.at[pl.ds(first, 2)],
            dst_ref=got.at[index],
            send_sem=c_send.at[index],
            recv_sem=c_recv.at[index],
            device_id=beside(shift, turn),
            device_id_type=MESH,
        )

    gifts = [gift(index, *move) for index, move in enumerate(moves)]
    for copy in gifts:
        copy.start()
    exchange.spread(1)
    for copy in gifts:
        copy.wait()
    padded[...] = jnp.zeros_like(padded)
    for plane in range(2):
        own = sent[4 + 2 * image + plane].astype(jnp.float32)
        for index, (shift, turn) in enumerate(moves):
            piece = got[index, plane].astype(jnp.float32)
            if shift:
                source = slab - shift
                piece = jnp.where(jnp.logical_and(source >= 0, source < 128), piece, 0.0)
            own = own + piece
        padded[plane, pl.ds(16, 128), :] = own
        for depth in range(8):
            g_ref[depth, plane, pl.ds(0, 16), :] = padded[
                plane, pl.ds(16 + 8 * depth - 4, 16), :
            ].astype(jnp.bfloat16)
            mirrored = padded[plane, pl.ds(16 + 116 - 8 * depth, 16), :]
            if depth == 0:
                mirrored = jnp.concatenate([own[63:65], mirrored[2:]], axis=0)
            g_ref[depth, plane, pl.ds(16, 16), :] = mirrored.astype(jnp.bfloat16)

    def window(step):
        depth = (z + step) % 8
        return pltpu.make_async_remote_copy(
            src_ref=g_ref.at[depth],
            dst_ref=h_ref.at[z],
            send_sem=g_send,
            recv_sem=g_recv,
            device_id=device(y, x, depth, c),
            device_id_type=MESH,
        )

    for step in (4, 1, 7, 2, 6, 3, 5):
        window(step).start()
    stay = pltpu.make_async_copy(g_ref.at[z], h_ref.at[z], g_own)
    stay.start()
    exchange.start(0)
    exchange.spread(2)
    stay.wait()
    seven = pltpu.make_async_remote_copy(
        src_ref=g_ref.at[pl.ds(0, 7)],
        dst_ref=h_ref.at[pl.ds(0, 7)],
        send_sem=g_send,
        recv_sem=g_recv,
        device_id=device(y, x, (z + 1) % 8, c),
        device_id_type=MESH,
    )
    seven.wait_send()
    seven.wait_recv()
    weights = windows[jnp.where(z == 0, 1, 0)]
    for source in range(8):
        for plane in range(2):
            made[pl.ds(source * 2 + plane, 64, stride=16), :] = dot(weights, h_ref[source, plane])
    whole_rows[...] = made[...].astype(jnp.bfloat16).reshape(32, 2, 16, 128)
    for d in range(1, 32):
        row, column, core = (y + d // 8) % 4, (x + d // 2 % 4) % 4, (c + d) % 2
        pltpu.make_async_remote_copy(
            src_ref=whole_rows.at[(row * 4 + column) * 2 + core],
            dst_ref=e_ref.at[m],
            send_sem=e_send,
            recv_sem=e_recv,
            device_id=device(row, column, z, core),
            device_id_type=MESH,
        ).start()
    kept = pltpu.make_async_copy(whole_rows.at[m], e_ref.at[m], e_own)
    kept.start()
    exchange.spread(3)
    for fill in fills[1:]:
        fill.wait()
    for total_ref in (sum_re, sum_im, sum_edge):
        total_ref[...] = jnp.zeros_like(total_ref)

    def along_x(k):
        source = exchange.arrived(k)
        stage[...] = r_ref[pl.ds(source * 8, 8)].astype(jnp.float32).reshape(1024, 128)
        real, imag = (
            jnp.concatenate(
                [stage[pl.ds(part * 2 + side, 256, stride=4), :] for side in range(2)], axis=1
            ).astype(jnp.bfloat16)
            for part in range(2)
        )
        side = source % 2
        at = pl.ds((source // 2) * 256, 256)

        @pl.when(usual)
        def _():
            sum_re[at, :] += dot(real, cos_x[side]) + dot(imag, sin_x[side])
            sum_im[at, :] += dot(imag, cos_x[side]) - dot(real, sin_x[side])

        @pl.when(both_real)
        def _():
            for part, line in enumerate((real, imag)):
                columns = pl.ds(part * 256, 256)
                sum_re[at, columns] += dot(line, cos_x[side, :, pl.ds(0, 256)])
                sum_im[at, columns] -= dot(line, sin_x[side, :, pl.ds(0, 256)])
                sum_edge[at, :] += dot(line, edge_in[part, side])

    along_x(1)
    exchange.spread(0)
    kept.wait()
    others = pltpu.make_async_remote_copy(
        src_ref=whole_rows.at[pl.ds(0, 31)],
        dst_ref=e_ref.at[pl.ds(0, 31)],
        send_sem=e_send,
        recv_sem=e_recv,
        device_id=device(y, x, (z + 1) % 8, c),
        device_id_type=MESH,
    )
    others.wait_send()
    others.wait_recv()

    def rounded_root(rows, across):
        return jnp.sqrt(scale * dot(rows, across)).astype(jnp.bfloat16).astype(jnp.float32)

    first, second = (e_ref[:, part].reshape(GZ, PIX) for part in range(2))
    first_mirror = dot(mirror[...], first).astype(jnp.bfloat16)
    second_mirror = dot(mirror[...], second).astype(jnp.bfloat16)

    @pl.when(usual)
    def _():
        amplitude[...] = 0.5 * (
            rounded_root(first, across_x[0]) + rounded_root(second_mirror, across_x[1])
        )

    @pl.when(both_real)
    def _():
        for part, (near, far) in enumerate(((first, first_mirror), (second, second_mirror))):
            amplitude[:, pl.ds(part * 256, 256)] = 0.5 * (
                rounded_root(near, across_x[0, :, pl.ds(0, 256)])
                + rounded_root(far, across_x[1, :, pl.ds(0, 256)])
            )
        amplitude_edge[...] = 0.5 * (
            rounded_root(
                jnp.concatenate([first, second], axis=1),
                jnp.concatenate([edge_across[0], edge_across[1]], axis=0),
            )
            + rounded_root(
                jnp.concatenate([first_mirror, second_mirror], axis=1),
                jnp.concatenate([edge_across[0], edge_across[1]], axis=0),
            )
        )

    along_x(2)
    along_x(3)
    along_x(0)
    line_re[...] = sum_re[...].astype(jnp.bfloat16)
    line_im[...] = sum_im[...].astype(jnp.bfloat16)
    line_edge[...] = sum_edge[...].astype(jnp.bfloat16)

    def projection(real_z, imag_z, target):
        modulus = jnp.sqrt(real_z * real_z + imag_z * imag_z)
        factor = target / jnp.maximum(modulus, least_modulus)
        return (real_z * factor).astype(jnp.bfloat16), (imag_z * factor).astype(jnp.bfloat16)

    def along_depth(block, carry):
        at = pl.ds(pl.multiple_of(block * 128, 128), 128)
        cos, sin = cos_z[block], sin_z[block]
        proj_re[at, :], proj_im[at, :] = projection(
            dot(cos, line_re[...]) + dot(sin, line_im[...]),
            dot(cos, line_im[...]) - dot(sin, line_re[...]),
            amplitude[at, :],
        )

        @pl.when(both_real)
        def _():
            edge_re[at, :], edge_im[at, :] = projection(
                dot(cos, line_edge[...]), -dot(sin, line_edge[...]), amplitude_edge[at, :]
            )

        return carry

    lax.fori_loop(0, 4, along_depth, 0)
    column = lax.broadcasted_iota(jnp.int32, (1, GX), 1) % 256
    share = 1.0 + jnp.where(column == 0, 0.0, both_real.astype(jnp.float32))

    def back_depth(half):
        cos, sin = cos_b[half], sin_b[half]
        back_re[half] = (
            share * (dot(cos, proj_re[...]) - dot(sin, proj_im[...]))
        ).astype(jnp.bfloat16)
        back_im[half] = (
            share * (dot(cos, proj_im[...]) + dot(sin, proj_re[...]))
        ).astype(jnp.bfloat16)

        @pl.when(both_real)
        def _():
            back_edge[half] = (dot(cos, edge_re[...]) - dot(sin, edge_im[...])).astype(jnp.bfloat16)

    def back_x(k):
        row = (y + k) % 4
        half, side = row // 2, row % 2

        def put(part, out):
            for column_block in range(2):
                stage[pl.ds(part * 2 + column_block, 256, stride=4), :] = out[
                    :, column_block * 128 : column_block * 128 + 128
                ]

        @pl.when(usual)
        def _():
            real, imag, cos, sin = back_re[half], back_im[half], cos_r[side], sin_r[side]
            put(0, dot(real, cos) - dot(imag, sin))
            put(1, dot(imag, cos) + dot(real, sin))

        @pl.when(both_real)
        def _():
            cos, sin = cos_r[side, pl.ds(0, 256)], sin_r[side, pl.ds(0, 256)]
            for part in range(2):
                columns = pl.ds(part * 256, 256)
                put(
                    part,
                    dot(back_re[half, :, columns], cos)
                    - dot(back_im[half, :, columns], sin)
                    + dot(back_edge[half], edge_out[part, side]),
                )

        x_back[row] = stage[...].astype(jnp.bfloat16).reshape(4, 8, 2, 16, 128)
        back.start(k)

    near_half = ((y + 1) % 4) // 2
    back_depth(near_half)
    back_x(1)
    back_depth(1 - near_half)
    for k in (2, 3, 0):
        back_x(k)
    for k in ORDER:
        back.spread(k)
    for k in ORDER:
        back.arrived(k)
    exchange.finish()
    back.finish()


def exchange_step(scale, density, orient, sharp, images):
    vmem = pl.BlockSpec(memory_space=pltpu.VMEM)
    anywhere = pl.BlockSpec(memory_space=pl.ANY)
    bfloat, single = jnp.bfloat16, jnp.float32
    one = pltpu.SemaphoreType.DMA
    tiles = (32, 8, 16, 128)
    square = (GZ, GX)
    return pl.pallas_call(
        functools.partial(step_kernel, scale),
        out_shape=jax.ShapeDtypeStruct(tiles, bfloat),
        in_specs=[vmem] * 3 + [anywhere] * (2 + len(TABLES)),
        out_specs=vmem,
        scratch_shapes=[pltpu.VMEM(t.shape, bfloat) for t in TABLES]
        + [
            pltpu.VMEM(density.shape, bfloat),
            pltpu.VMEM(tiles, bfloat),
            pltpu.VMEM((32, 2, 16, 128), bfloat),
            pltpu.VMEM(BLOCKS, bfloat),
            pltpu.VMEM(BLOCKS, bfloat),
            pltpu.VMEM((1024, 128), single),
            pltpu.VMEM((64 * 128, 128), single),
            pltpu.VMEM((16 * 128, 128), single),
            pltpu.VMEM((16, 128, 128), bfloat),
            pltpu.VMEM((5, 2, 128, 128), bfloat),
            pltpu.VMEM((2, 160, 128), single),
            pltpu.VMEM((8, 2, 32, 128), bfloat),
            pltpu.VMEM((8, 2, 32, 128), bfloat),
            pltpu.VMEM((1024, 128), single),
            pltpu.VMEM((32, 2, 16, 128), bfloat),
            pltpu.VMEM(BLOCKS, bfloat),
            pltpu.VMEM(BLOCKS, bfloat),
            pltpu.VMEM(square, single),
            pltpu.VMEM(square, single),
            pltpu.VMEM((GZ, 128), single),
            pltpu.VMEM(square, bfloat),
            pltpu.VMEM(square, bfloat),
            pltpu.VMEM((GZ, 128), bfloat),
            pltpu.VMEM(square, single),
            pltpu.VMEM((GZ, 128), single),
            pltpu.VMEM(square, bfloat),
            pltpu.VMEM(square, bfloat),
            pltpu.VMEM((GZ, 128), bfloat),
            pltpu.VMEM((GZ, 128), bfloat),
            pltpu.VMEM((2, 256, GX), bfloat),
            pltpu.VMEM((2, 256, GX), bfloat),
            pltpu.VMEM((2, 256, 128), bfloat),
            one, one((len(TABLES),)), one, one((5,)), one((5,)), one, one, one, one, one, one,
        ]
        + EXCHANGE_SEMS * 2,
        compiler_params=pltpu.CompilerParams(
            collective_id=1, has_side_effects=True, vmem_limit_bytes=52 << 20
        ),
    )(
        WINDOWS,
        orient.reshape(1, -1),
        sharp.reshape(1, -1),
        density,
        images.reshape(-1, PIX),
        *TABLES,
    )


def update_kernel(lines, table, density, support, out, wide):
    plane = pl.program_id(0)

    @pl.when(plane == 0)
    def _():
        wide[...] = lines[...].astype(jnp.float32).reshape(4096, 128)

    rows = [
        jnp.concatenate(
            [wide[pl.ds(plane * 4 + part * 2 + side, HALF, stride=16), :] for side in range(2)],
            axis=1,
        ).astype(jnp.bfloat16)
        for part in range(2)
    ]
    projected = dot(table[...], jnp.concatenate(rows, axis=0))
    previous = density[0].astype(jnp.float32)
    out[0] = jnp.where(support[0] == 1, projected, previous - feedback * projected)


def update(lines, density, support):
    depth, rows, columns = density.shape
    vmem = pl.BlockSpec(memory_space=pltpu.VMEM)
    block = pl.BlockSpec((1, rows, columns), lambda plane: (plane, 0, 0))
    return pl.pallas_call(
        update_kernel,
        grid=(depth,),
        out_shape=jax.ShapeDtypeStruct(density.shape, jnp.float32),
        in_specs=[vmem, vmem, block, block],
        out_specs=block,
        scratch_shapes=[pltpu.VMEM((4096, 128), jnp.float32)],
        compiler_params=pltpu.CompilerParams(vmem_limit_bytes=32 << 20),
    )(lines, BACK_Y, density, support)


def body(images, orient, sharp, density, support):
    depth = density.shape[0]
    scale = depth / (images.shape[0] * lax.axis_size("img"))
    lines = exchange_step(scale, density, orient, sharp, images)
    return update(lines, density, support)


def solution(mesh):
    placed = (
        P(("img", "slab"), None, None),
        P(("img", "slab")),
        P(("img", "slab")),
        P("slab", None, "img"),
        P("slab", None, "img"),
    )
    return jax.shard_map(
        body, mesh=mesh, in_specs=placed, out_specs=P("slab", None, "img"), check_vma=False
    )
```

```python
import functools
import math

import jax
import jax.numpy as jnp
import ml_dtypes
import numpy as np
from jax import lax
from jax.experimental import pallas as pl
from jax.experimental.pallas import tpu as pltpu
from jax.sharding import PartitionSpec as P

GZ = 512
GY = 512
GX = 512
PIX = 128

least_modulus = 0.5
feedback = 0.9


def dft_tables(length):
    index = np.arange(length, dtype=np.int64)
    product = (index[:, None] * index[None, :]) % length
    angles = product.astype(np.float32) * np.float32(2.0 * math.pi / length)
    factor = np.float32(1.0 / math.sqrt(length))
    return (
        (np.cos(angles) * factor).astype(ml_dtypes.bfloat16),
        (np.sin(angles) * factor).astype(ml_dtypes.bfloat16),
    )


def interpolation(cells, pixels):
    grid = np.arange(cells, dtype=np.float32)
    detector = np.arange(pixels, dtype=np.float32)
    position = (grid + np.float32(0.5)) * np.float32(pixels / cells) - np.float32(0.5)
    return np.maximum(
        np.float32(0.0), np.float32(1.0) - np.abs(position[:, None] - detector[None, :])
    )


def bf(table):
    return np.asarray(table).astype(ml_dtypes.bfloat16)


COS, SIN = dft_tables(GY)
HALF = GY // 2
_y, _x, _z, _c = np.meshgrid(np.arange(4), np.arange(4), np.arange(8), np.arange(2), indexing="ij")
ROW_OF = 32 * _z + 8 * _y + 2 * _x + _c
_imag = np.concatenate([COS[HALF : HALF + 1], -SIN[1:HALF]])
FORWARD_Y = np.stack(
    [COS[:HALF][ROW_OF.reshape(4, 64)], _imag[ROW_OF.reshape(4, 64)]], axis=1
).reshape(4, 128, GY)
_two = 2.0 * COS[:, :HALF].astype(np.float32)
_two[:, 0] = COS[:, 0]
_sin = -2.0 * SIN[:, :HALF].astype(np.float32)
_sin[:, 0] = COS[:, HALF]
BACK_Y = np.stack([bf(t.reshape(GY, 8, 32).transpose(0, 2, 1)) for t in (_two, _sin)], axis=1)
BACK_Y = BACK_Y.reshape(GY, 2, 2, 128).transpose(2, 0, 1, 3).reshape(2, GY, 256)


def quarters(upper_left, upper_right, lower_left, lower_right):
    return np.concatenate(
        [
            np.concatenate([upper_left, upper_right], axis=1),
            np.concatenate([lower_left, lower_right], axis=1),
        ],
        axis=0,
    )


FORWARD_X = np.zeros((2, 2 * GX, 2 * GX), ml_dtypes.bfloat16)
FORWARD_X[0] = quarters(COS, -SIN, SIN, COS)
BACK_X = np.zeros((2, 2, 2 * GX, GX), ml_dtypes.bfloat16)
_low = GX // 2
_pair = np.where(np.arange(_low) == 0, 1.0, 2.0)[:, None]
for _e in range(2):
    _columns = slice(_e * _low, (_e + 1) * _low)
    _in = -SIN[:, :_low]
    _in[:, 0] = COS[:, _low]
    FORWARD_X[1, _e * GX : (_e + 1) * GX, _columns] = COS[:, :_low]
    FORWARD_X[1, _e * GX : (_e + 1) * GX, GX + _e * _low : GX + (_e + 1) * _low] = _in
    BACK_X[0, _e] = quarters(COS[:, _columns], SIN[:, _columns], -SIN[:, _columns], COS[:, _columns])
    _out_re = bf(COS[:_low].astype(np.float32) * _pair)
    _out_im = bf(-SIN[:_low].astype(np.float32) * _pair)
    _out_im[0] = COS[_low]
    for _side in range(2):
        _half = slice(_side * _low, (_side + 1) * _low)
        BACK_X[1, _side, _columns, _columns] = _out_re[:, _half]
        BACK_X[1, _side, GX + _e * _low : GX + (_e + 1) * _low, _columns] = _out_im[:, _half]
_across = interpolation(GY, PIX)
_mirror = (-np.arange(GY)) % GY
ACROSS_X = np.zeros((2, 2, 2 * PIX, GX), np.float32)
ACROSS_X[0, 0, :PIX] = _across.T
ACROSS_X[0, 1, PIX:] = _across[_mirror].T
EDGE_ACROSS = np.zeros((2 * PIX, 2 * PIX), np.float32)
for _e in range(2):
    _rows, _columns = slice(_e * PIX, (_e + 1) * PIX), slice(_e * _low, (_e + 1) * _low)
    ACROSS_X[1, 0, _rows, _columns] = _across[:_low].T
    ACROSS_X[1, 1, _rows, _columns] = _across[_mirror][:_low].T
    EDGE_ACROSS[_rows, _e * PIX] = _across[_low]
ACROSS_X, EDGE_ACROSS = bf(ACROSS_X), bf(EDGE_ACROSS)
_yh, _xx, _cc, _zz, _z4 = np.meshgrid(
    np.arange(2), np.arange(4), np.arange(2), np.arange(8), np.arange(4), indexing="ij"
)
Z_ORDER = (4 * (64 * _yh + 16 * _xx + 2 * _zz + _cc) + _z4).reshape(-1)
_yh, _yl, _xx, _cc, _zz, _p2 = np.meshgrid(
    np.arange(2), np.arange(2), np.arange(4), np.arange(2), np.arange(8), np.arange(2), indexing="ij"
)
K_ORDER = (4 * (64 * _yh + 16 * _xx + 2 * _zz + _cc) + 2 * _yl + _p2).reshape(-1)
FORWARD_Z = np.stack(
    [
        np.concatenate([t[K_ORDER][:, Z_ORDER[h * 256 : h * 256 + 256]] for t in (COS, SIN)], axis=1)
        for h in range(2)
    ]
)
BACK_Z = np.concatenate([COS[:, K_ORDER], SIN[:, K_ORDER]], axis=1).reshape(2, 256, 2 * GZ)
MIRROR = bf(K_ORDER[None, :] == _mirror[K_ORDER][:, None])
WINDOWS = np.zeros((2, 32, 2, 2, 16), np.float32)
for _m in range(32):
    for _r in range(16):
        WINDOWS[:, _m, 0, 0, _r] = max(0.0, 1.0 - abs(_m / 4 + 3.625 - _r))
        WINDOWS[:, _m, 1, 1, _r] = max(0.0, 1.0 - abs(11.625 - _m / 4 - _r))
WINDOWS[1, 0, 1, 1, :] = 0.0
WINDOWS[1, 0, 1, 1, 0:2] = (0.375, 0.625)
WINDOWS = bf(WINDOWS.reshape(2, 64, 32))

MESH = pl.DeviceIdType.MESH


def dot(first, second):
    return jnp.dot(first, second, preferred_element_type=jnp.float32)


def place():
    slab = lax.axis_index("slab")
    return (slab // 64) * 2 + lax.axis_index("img"), (slab // 16) % 4, (slab // 2) % 8, slab % 2


def device(y, x, z, c):
    return (y % 2, (y // 2) * 64 + x * 16 + z * 2 + c)


def greet(others):
    barrier = pltpu.get_barrier_semaphore()
    for other in others:
        pl.semaphore_signal(barrier, inc=1, device_id=other, device_id_type=MESH)
    return lambda: pl.semaphore_wait(barrier, len(others))


def across(y, k):
    return (y, y + 1 - 2 * (y % 2), (y + 2) % 4, 3 - y)[k]


class Exchange:
    def __init__(self, x_ref, a_ref, r_ref, sems):
        self.x_ref, self.a_ref, self.r_ref = x_ref, a_ref, r_ref
        self.local, self.z_send, self.z_recv, self.p_send, self.p_recv, self.own = sems
        self.y, self.x, self.z, self.c = place()
        self.m = (self.y * 4 + self.x) * 2 + self.c

    def along_z(self, k, step):
        row, depth = across(self.y, k), (self.z + step) % 8
        return pltpu.make_async_remote_copy(
            src_ref=self.x_ref.at[row, :, depth],
            dst_ref=self.a_ref.at[row, :, self.z],
            send_sem=self.z_send.at[k],
            recv_sem=self.z_recv.at[k],
            device_id=device(self.y, self.x, depth, self.c),
            device_id_type=MESH,
        )

    def keep(self, k):
        row = across(self.y, k)
        return pltpu.make_async_copy(
            self.x_ref.at[row, :, self.z], self.a_ref.at[row, :, self.z], self.local.at[k]
        )

    def whole(self, k):
        row = across(self.y, k)
        return pltpu.make_async_remote_copy(
            src_ref=self.x_ref.at[row, :, pl.ds(0, 7)],
            dst_ref=self.a_ref.at[row, :, pl.ds(0, 7)],
            send_sem=self.z_send.at[k],
            recv_sem=self.z_recv.at[k],
            device_id=device(self.y, self.x, (self.z + 1) % 8, self.c),
            device_id_type=MESH,
        )

    def start(self, k):
        for step in (4, 1, 7, 2, 6, 3, 5):
            self.along_z(k, step).start()
        self.keep(k).start()

    def spread(self, k):
        self.keep(k).wait()
        self.whole(k).wait_recv()
        row = across(self.y, k)
        for dx in (2, 1, 3, 0):
            for dc in (0, 1):
                if (k, dx, dc) == (0, 0, 0):
                    self.mine().start()
                    continue
                column, core = (self.x + dx) % 4, (self.c + dc) % 2
                pltpu.make_async_remote_copy(
                    src_ref=self.a_ref.at[row, column, :, core],
                    dst_ref=self.r_ref.at[self.m],
                    send_sem=self.p_send,
                    recv_sem=self.p_recv.at[k],
                    device_id=device(row, column, self.z, core),
                    device_id_type=MESH,
                ).start()

    def mine(self):
        return pltpu.make_async_copy(
            self.a_ref.at[self.y, self.x, :, self.c], self.r_ref.at[self.m], self.own
        )

    def arrived(self, k):
        count = 8 if k else 7
        if not k:
            self.mine().wait()
        pltpu.make_async_remote_copy(
            src_ref=self.r_ref.at[pl.ds(0, count)],
            dst_ref=self.r_ref.at[pl.ds(0, count)],
            send_sem=self.p_send,
            recv_sem=self.p_recv.at[k],
            device_id=device(self.y, self.x, (self.z + 1) % 8, self.c),
            device_id_type=MESH,
        ).wait_recv()

    def finish(self):
        for k in range(4):
            self.whole(k).wait_send()
        pltpu.make_async_remote_copy(
            src_ref=self.r_ref.at[pl.ds(0, 31)],
            dst_ref=self.r_ref.at[pl.ds(0, 31)],
            send_sem=self.p_send,
            recv_sem=self.p_recv.at[0],
            device_id=device(self.y, self.x, (self.z + 1) % 8, self.c),
            device_id_type=MESH,
        ).wait_send()


EXCHANGE_SEMS = [
    pltpu.SemaphoreType.DMA((4,)),
    pltpu.SemaphoreType.DMA((4,)),
    pltpu.SemaphoreType.DMA((4,)),
    pltpu.SemaphoreType.DMA,
    pltpu.SemaphoreType.DMA((4,)),
    pltpu.SemaphoreType.DMA,
]
BLOCKS = (4, 4, 8, 2, 16, 128)
ORDER = (2, 3, 1, 0)


def partners():
    y, x, z, c = place()
    return [device(y, x, (z + d) % 8, c) for d in range(1, 8)] + [
        device((y + d // 8) % 4, (x + d // 2 % 4) % 4, z, (c + d) % 2) for d in range(1, 32)
    ]


TABLES = (FORWARD_Y, WINDOWS, FORWARD_X, FORWARD_Z, MIRROR, ACROSS_X, EDGE_ACROSS, BACK_Z, BACK_X, BACK_Y)
CHOSEN = (2, 5, 8)


def step_kernel(scale, orient_in, sharp_in, density_in, images, *rest):
    count = len(TABLES)
    sources, out_ref, rest = rest[:count], rest[count], rest[count + 1 :]
    tables, rest = rest[:count], rest[count:]
    (
        orient, sharp, density, r_ref, e_ref,
        x_ref, a_ref, stage, held, parts, sent, got, padded, g_ref, h_ref, made, whole_rows,
        x_back, a_back, r_back, wide, lines, spectrum, edges, depth_sum, edge_sum, amplitude, amplitude_edge,
        projected, projected_edge, final,
        d_load, t_load, load, o_send, c_send, c_recv, g_send, g_recv, g_own, e_send, e_recv, e_own, *sems,
    ) = rest
    (
        table, windows, forward_x, forward_z, mirror, across_x, edge_across, back_z, back_x_table, back_y,
    ) = tables
    y, x, z, c = place()
    image = lax.axis_index("img")
    slab = lax.axis_index("slab")
    m = (y * 4 + x) * 2 + c
    special = jnp.where(slab + image == 0, 1, 0)
    both_real = special == 1

    def beside(shift, turn):
        return ((image + turn) % 2, (slab + shift + 128) % 128)

    moves = [(shift, turn) for shift in (-1, 0, 1) for turn in (0, 1) if (shift, turn) != (0, 0)]
    entered = greet(partners() + [beside(*move) for move in moves])
    fills = [
        pltpu.make_async_copy(
            sources[i].at[special] if i in CHOSEN else sources[i], tables[i], t_load.at[i]
        )
        for i in range(len(TABLES))
    ]
    first_fills = [
        fills[0],
        pltpu.make_async_copy(density_in, density, d_load.at[0]),
        pltpu.make_async_copy(orient_in, orient, d_load.at[1]),
        pltpu.make_async_copy(sharp_in, sharp, d_load.at[2]),
    ]
    fetch = pltpu.make_async_copy(images, held, load)
    for fill in first_fills:
        fill.start()
    fetch.start()
    for fill in fills[1:]:
        fill.start()
    exchange = Exchange(x_ref, a_ref, r_ref, sems[:6])
    back = Exchange(x_back, a_back, r_back, sems[6:])
    for fill in first_fills:
        fill.wait()

    def transform(k):
        row = across(y, k)
        for plane in range(4):
            out = dot(table[row], density[plane])
            for part in range(2):
                for side in range(2):
                    stage[pl.ds(plane * 4 + part * 2 + side, 64, stride=16), :] = out[
                        part * 64 : part * 64 + 64, side * 128 : side * 128 + 128
                    ]
        x_ref[row] = stage[...].astype(jnp.bfloat16).reshape(4, 8, 2, 16, 128)

    transform(2)
    entered()
    exchange.start(2)
    for k in (3, 1):
        transform(k)
        exchange.start(k)
    transform(0)

    near = orient[...] - slab * 4
    steps = lax.broadcasted_iota(jnp.int32, (16, 64), 0) - 4 - near
    squares = (steps * steps).astype(jnp.float32)
    raw = jnp.exp(-sharp[...] * squares)
    total = 1.0 + 2.0 * (
        jnp.exp(-sharp[...])
        + jnp.exp(-4.0 * sharp[...])
        + jnp.exp(-9.0 * sharp[...])
        + jnp.exp(-16.0 * sharp[...])
    )
    mixing = jnp.where(jnp.abs(steps) <= 4, raw / total, 0.0)
    high = mixing.astype(jnp.bfloat16)
    low = (mixing - high.astype(jnp.float32)).astype(jnp.bfloat16)
    factors = jnp.concatenate(
        [
            jnp.concatenate([high, high], axis=1),
            jnp.concatenate([low, jnp.zeros_like(low)], axis=1),
        ],
        axis=0,
    )
    fetch.wait()

    def mix(index, carry):
        at = index * 2
        rows = jnp.concatenate(
            [held[pl.ds(at, 64, stride=128), :], held[pl.ds(at + 1, 64, stride=128), :]], axis=1
        )
        upper = rows.astype(jnp.bfloat16)
        lower = (rows - upper.astype(jnp.float32)).astype(jnp.bfloat16)
        out = dot(factors, jnp.concatenate([upper, lower], axis=0))
        out = out[:16] + out[16:]
        parts[pl.ds(at, 16, stride=128), :] = out[:, :128]
        parts[pl.ds(at + 1, 16, stride=128), :] = out[:, 128:]
        return carry

    lax.fori_loop(0, 64, mix, 0)
    sent[...] = parts[...].astype(jnp.bfloat16).reshape(16, 128, 128)

    def gift(index, shift, turn):
        first = 4 + 4 * shift + 2 * ((image + turn) % 2)
        return pltpu.make_async_remote_copy(
            src_ref=sent.at[pl.ds(first, 2)],
            dst_ref=got.at[index],
            send_sem=c_send.at[index],
            recv_sem=c_recv.at[index],
            device_id=beside(shift, turn),
            device_id_type=MESH,
        )

    gifts = [gift(index, *move) for index, move in enumerate(moves)]
    for copy in gifts:
        copy.start()
    exchange.spread(2)
    for copy in gifts:
        copy.wait()
    padded[...] = jnp.zeros_like(padded)
    for plane in range(2):
        own = sent[4 + 2 * image + plane].astype(jnp.float32)
        for index, (shift, turn) in enumerate(moves):
            piece = got[index, plane].astype(jnp.float32)
            if shift:
                source = slab - shift
                piece = jnp.where(jnp.logical_and(source >= 0, source < 128), piece, 0.0)
            own = own + piece
        padded[plane, pl.ds(16, 128), :] = own
        for depth in range(8):
            g_ref[depth, plane, pl.ds(0, 16), :] = padded[
                plane, pl.ds(16 + 8 * depth - 4, 16), :
            ].astype(jnp.bfloat16)
            mirrored = padded[plane, pl.ds(16 + 116 - 8 * depth, 16), :]
            if depth == 0:
                mirrored = jnp.concatenate([own[63:65], mirrored[2:]], axis=0)
            g_ref[depth, plane, pl.ds(16, 16), :] = mirrored.astype(jnp.bfloat16)

    def window(step):
        depth = (z + step) % 8
        return pltpu.make_async_remote_copy(
            src_ref=g_ref.at[depth],
            dst_ref=h_ref.at[z],
            send_sem=g_send,
            recv_sem=g_recv,
            device_id=device(y, x, depth, c),
            device_id_type=MESH,
        )

    for step in (4, 1, 7, 2, 6, 3, 5):
        window(step).start()
    stay = pltpu.make_async_copy(g_ref.at[z], h_ref.at[z], g_own)
    stay.start()
    exchange.start(0)
    exchange.spread(3)
    for fill in fills[1:]:
        fill.wait()

    def along_x(half):
        for side in range(2):
            wide[pl.ds(side * 1024, 1024), :] = (
                r_ref[pl.ds((half * 2 + side) * 8, 8)].astype(jnp.float32).reshape(1024, 128)
            )
        for part in range(2):
            for side in range(2):
                for block in range(2):
                    at = part * 512 + side * 256 + block * 128
                    lines[:, pl.ds(at, 128)] = wide[
                        pl.ds(side * 1024 + part * 2 + block, 256, stride=4), :
                    ].astype(jnp.bfloat16)
        both = dot(lines[...], forward_x[...]).astype(jnp.bfloat16)
        spectrum[pl.ds(0, 256), :] = both
        spectrum[pl.ds(256, 256), pl.ds(0, GX)] = both[:, GX:]
        spectrum[pl.ds(256, 256), pl.ds(GX, GX)] = -both[:, :GX]

        @pl.when(both_real)
        def _():
            first_lane = lax.broadcasted_iota(jnp.int32, (256, 128), 1) == 0
            zero = jnp.zeros((256, 128), jnp.bfloat16)
            edges[...] = jnp.zeros_like(edges)
            for part in range(2):
                mixed = spectrum[pl.ds(0, 256), pl.ds(GX + part * 256, 128)].astype(jnp.float32)
                edge = jnp.where(first_lane, mixed, 0.0)
                kept_part = (mixed - edge).astype(jnp.bfloat16)
                edge = edge.astype(jnp.bfloat16)
                spectrum[pl.ds(0, 256), pl.ds(GX + part * 256, 128)] = kept_part
                spectrum[pl.ds(256, 256), pl.ds(part * 256, 128)] = kept_part
                edges[pl.ds(0, 256), pl.ds(part * 128, 128)] = edge
                edges[pl.ds(256, 256), pl.ds(256 + part * 128, 128)] = zero - edge

    def block_of(block):
        return pl.ds(pl.multiple_of(block * 128, 128), 128)

    other_half, own_half = 1 - y // 2, y // 2
    exchange.arrived(2)
    exchange.arrived(3)
    along_x(other_half)

    def first_depth(block, carry):
        at = block_of(block)
        weights = forward_z[other_half, at, :]
        depth_sum[at, :] = dot(weights, spectrum[...])

        @pl.when(both_real)
        def _():
            edge_sum[at, :] = dot(weights, edges[...])

        return carry

    lax.fori_loop(0, 4, first_depth, 0)
    exchange.spread(1)
    stay.wait()
    seven = pltpu.make_async_remote_copy(
        src_ref=g_ref.at[pl.ds(0, 7)],
        dst_ref=h_ref.at[pl.ds(0, 7)],
        send_sem=g_send,
        recv_sem=g_recv,
        device_id=device(y, x, (z + 1) % 8, c),
        device_id_type=MESH,
    )
    seven.wait_send()
    seven.wait_recv()
    weights = windows[jnp.where(z == 0, 1, 0)]
    for source in range(8):
        for plane in range(2):
            made[pl.ds(source * 2 + plane, 64, stride=16), :] = dot(weights, h_ref[source, plane])
    whole_rows[...] = made[...].astype(jnp.bfloat16).reshape(32, 2, 16, 128)
    for d in range(1, 32):
        row, column, core = (y + d // 8) % 4, (x + d // 2 % 4) % 4, (c + d) % 2
        pltpu.make_async_remote_copy(
            src_ref=whole_rows.at[(row * 4 + column) * 2 + core],
            dst_ref=e_ref.at[m],
            send_sem=e_send,
            recv_sem=e_recv,
            device_id=device(row, column, z, core),
            device_id_type=MESH,
        ).start()
    kept = pltpu.make_async_copy(whole_rows.at[m], e_ref.at[m], e_own)
    kept.start()
    exchange.spread(0)
    kept.wait()
    others = pltpu.make_async_remote_copy(
        src_ref=whole_rows.at[pl.ds(0, 31)],
        dst_ref=e_ref.at[pl.ds(0, 31)],
        send_sem=e_send,
        recv_sem=e_recv,
        device_id=device(y, x, (z + 1) % 8, c),
        device_id_type=MESH,
    )
    others.wait_send()
    others.wait_recv()

    def rounded_root(rows, across_table):
        return jnp.sqrt(scale * dot(rows, across_table)).astype(jnp.bfloat16).astype(jnp.float32)

    near = jnp.concatenate([e_ref[:, part].reshape(GZ, PIX) for part in range(2)], axis=1)
    far = dot(mirror[...], near).astype(jnp.bfloat16)
    amplitude[...] = 0.5 * (rounded_root(near, across_x[0]) + rounded_root(far, across_x[1]))

    @pl.when(both_real)
    def _():
        amplitude_edge[...] = 0.5 * (
            rounded_root(near, edge_across[...]) + rounded_root(far, edge_across[...])
        )

    exchange.arrived(1)
    exchange.arrived(0)
    along_x(own_half)

    def projection(real_z, imag_z, target):
        inverse = lax.rsqrt(real_z * real_z + imag_z * imag_z)
        factor = target * jnp.minimum(inverse, 1.0 / least_modulus)
        return (real_z * factor).astype(jnp.bfloat16), (imag_z * factor).astype(jnp.bfloat16)

    def along_depth(block, carry):
        at = block_of(block)
        below = pl.ds(pl.multiple_of(GZ + block * 128, 128), 128)
        weights = forward_z[own_half, at, :]
        total = depth_sum[at, :] + dot(weights, spectrum[...])
        real, imag = projection(total[:, :GX], total[:, GX:], amplitude[at, :])
        projected[at, pl.ds(0, GX)] = real
        projected[at, pl.ds(GX, GX)] = imag
        projected[below, pl.ds(0, GX)] = -imag
        projected[below, pl.ds(GX, GX)] = real

        @pl.when(both_real)
        def _():
            total = edge_sum[at, :] + dot(weights, edges[...])
            real, imag = projection(total[:, :256], total[:, 256:], amplitude_edge[at, :])
            projected_edge[at, :] = real
            projected_edge[below, :] = -imag

        return carry

    lax.fori_loop(0, 4, along_depth, 0)

    def back_depth(half):
        lines[...] = dot(back_z[half], projected[...]).astype(jnp.bfloat16)

        @pl.when(both_real)
        def _():
            first_lane = lax.broadcasted_iota(jnp.int32, (256, 128), 1) == 0
            edge = dot(back_z[half], projected_edge[...])
            for part in range(2):
                at = pl.ds(GX + part * 256, 128)
                lines[:, at] = jnp.where(
                    first_lane,
                    edge[:, part * 128 : part * 128 + 128],
                    lines[:, at].astype(jnp.float32),
                ).astype(jnp.bfloat16)

    def back_x(k):
        row = across(y, k)
        out = dot(lines[...], back_x_table[row % 2])
        for block in range(4):
            stage[pl.ds(block, 256, stride=4), :] = out[:, block * 128 : block * 128 + 128]
        x_back[row] = stage[...].astype(jnp.bfloat16).reshape(4, 8, 2, 16, 128)
        back.start(k)

    back_depth(other_half)
    back_x(2)
    back_x(3)
    back_depth(own_half)
    back_x(1)
    back_x(0)

    def along_y(half, last):
        wide[...] = r_back[pl.ds(half * 16, 16)].astype(jnp.float32).reshape(2048, 128)
        for plane in range(4):
            rows = [
                jnp.concatenate(
                    [
                        wide[pl.ds(plane * 4 + part * 2 + side, 128, stride=16), :]
                        for side in range(2)
                    ],
                    axis=1,
                ).astype(jnp.bfloat16)
                for part in range(2)
            ]
            out = dot(back_y[half], jnp.concatenate(rows, axis=0))
            if last:
                final[plane] += out
                pltpu.make_async_copy(final.at[plane], out_ref.at[plane], o_send.at[plane]).start()
            else:
                final[plane] = out

    for k in ORDER:
        back.spread(k)
        if k == 1:
            back.arrived(2)
            back.arrived(3)
            along_y(other_half, False)
    back.arrived(1)
    back.arrived(0)
    along_y(own_half, True)
    exchange.finish()
    back.finish()
    for plane in range(4):
        pltpu.make_async_copy(final.at[plane], out_ref.at[plane], o_send.at[plane]).wait()


def exchange_step(scale, density, orient, sharp, images):
    far = pl.BlockSpec(memory_space=pltpu.HBM)
    bfloat, single = jnp.bfloat16, jnp.float32
    one = pltpu.SemaphoreType.DMA
    tiles = (32, 8, 16, 128)
    return pl.pallas_call(
        functools.partial(step_kernel, scale),
        out_shape=jax.ShapeDtypeStruct(density.shape, single),
        in_specs=[far] * (4 + len(TABLES)),
        out_specs=far,
        scratch_shapes=[
            pltpu.VMEM(t.shape[1:] if i in CHOSEN else t.shape, bfloat) for i, t in enumerate(TABLES)
        ]
        + [
            pltpu.VMEM((1, 64), jnp.int32),
            pltpu.VMEM((1, 64), single),
            pltpu.VMEM(density.shape, bfloat),
            pltpu.VMEM(tiles, bfloat),
            pltpu.VMEM((32, 2, 16, 128), bfloat),
            pltpu.VMEM(BLOCKS, bfloat),
            pltpu.VMEM(BLOCKS, bfloat),
            pltpu.VMEM((1024, 128), single),
            pltpu.VMEM((64 * 128, 128), single),
            pltpu.VMEM((16 * 128, 128), single),
            pltpu.VMEM((16, 128, 128), bfloat),
            pltpu.VMEM((5, 2, 128, 128), bfloat),
            pltpu.VMEM((2, 160, 128), single),
            pltpu.VMEM((8, 2, 32, 128), bfloat),
            pltpu.VMEM((8, 2, 32, 128), bfloat),
            pltpu.VMEM((1024, 128), single),
            pltpu.VMEM((32, 2, 16, 128), bfloat),
            pltpu.VMEM(BLOCKS, bfloat),
            pltpu.VMEM(BLOCKS, bfloat),
            pltpu.VMEM(tiles, bfloat),
            pltpu.VMEM((2048, 128), single),
            pltpu.VMEM((256, 2 * GX), bfloat),
            pltpu.VMEM((512, 2 * GX), bfloat),
            pltpu.VMEM((512, 512), bfloat),
            pltpu.VMEM((GZ, 2 * GX), single),
            pltpu.VMEM((GZ, 512), single),
            pltpu.VMEM((GZ, GX), single),
            pltpu.VMEM((GZ, 256), single),
            pltpu.VMEM((2 * GZ, 2 * GX), bfloat),
            pltpu.VMEM((2 * GZ, 256), bfloat),
            pltpu.VMEM(density.shape, single),
            one((3,)), one((len(TABLES),)), one, one((4,)), one((5,)), one((5,)), one, one, one, one, one, one,
        ]
        + EXCHANGE_SEMS * 2,
        compiler_params=pltpu.CompilerParams(
            collective_id=1, has_side_effects=True, vmem_limit_bytes=50 << 20
        ),
    )(
        orient.reshape(1, -1),
        sharp.reshape(1, -1),
        density,
        images.reshape(-1, PIX),
        *TABLES,
    )


def body(images, orient, sharp, density, support):
    depth = density.shape[0]
    scale = depth / (images.shape[0] * lax.axis_size("img"))
    projected = exchange_step(scale, density, orient, sharp, images)
    previous = density.astype(jnp.float32)
    return jnp.where(support == 1, projected, previous - feedback * projected)


def solution(mesh):
    placed = (
        P(("img", "slab"), None, None),
        P(("img", "slab")),
        P(("img", "slab")),
        P("slab", None, "img"),
        P("slab", None, "img"),
    )
    return jax.shard_map(
        body, mesh=mesh, in_specs=placed, out_specs=P("slab", None, "img"), check_vma=False
    )
```

```python
import functools
import math

import jax
import jax.numpy as jnp
import ml_dtypes
import numpy as np
from jax import lax
from jax.experimental import pallas as pl
from jax.experimental.pallas import tpu as pltpu
from jax.sharding import PartitionSpec as P

GZ = 512
GY = 512
GX = 512
PIX = 128

least_modulus = 0.5
feedback = 0.9


def dft_tables(length):
    index = np.arange(length, dtype=np.int64)
    product = (index[:, None] * index[None, :]) % length
    angles = product.astype(np.float32) * np.float32(2.0 * math.pi / length)
    factor = np.float32(1.0 / math.sqrt(length))
    return (
        (np.cos(angles) * factor).astype(ml_dtypes.bfloat16),
        (np.sin(angles) * factor).astype(ml_dtypes.bfloat16),
    )


def interpolation(cells, pixels):
    grid = np.arange(cells, dtype=np.float32)
    detector = np.arange(pixels, dtype=np.float32)
    position = (grid + np.float32(0.5)) * np.float32(pixels / cells) - np.float32(0.5)
    return np.maximum(
        np.float32(0.0), np.float32(1.0) - np.abs(position[:, None] - detector[None, :])
    )


def bf(table):
    return np.asarray(table).astype(ml_dtypes.bfloat16)


COS, SIN = dft_tables(GY)
HALF = GY // 2
_y, _x, _z, _c = np.meshgrid(np.arange(4), np.arange(4), np.arange(8), np.arange(2), indexing="ij")
ROW_OF = 32 * _z + 8 * _y + 2 * _x + _c
_imag = np.concatenate([COS[HALF : HALF + 1], -SIN[1:HALF]])
FORWARD_Y = np.stack(
    [COS[:HALF][ROW_OF.reshape(4, 64)], _imag[ROW_OF.reshape(4, 64)]], axis=1
).reshape(4, 128, GY)
_two = 2.0 * COS[:, :HALF].astype(np.float32)
_two[:, 0] = COS[:, 0]
_sin = -2.0 * SIN[:, :HALF].astype(np.float32)
_sin[:, 0] = COS[:, HALF]
BACK_Y = np.stack([bf(t.reshape(GY, 8, 32).transpose(0, 2, 1)) for t in (_two, _sin)], axis=1)
BACK_Y = BACK_Y.reshape(GY, 2, 2, 128).transpose(2, 0, 1, 3).reshape(2, GY, 256)


def quarters(upper_left, upper_right, lower_left, lower_right):
    return np.concatenate(
        [
            np.concatenate([upper_left, upper_right], axis=1),
            np.concatenate([lower_left, lower_right], axis=1),
        ],
        axis=0,
    )


FORWARD_X = np.zeros((2, 2 * GX, 2 * GX), ml_dtypes.bfloat16)
FORWARD_X[0] = quarters(COS, -SIN, SIN, COS)
BACK_X = np.zeros((2, 2, 2 * GX, GX), ml_dtypes.bfloat16)
_low = GX // 2
_pair = np.where(np.arange(_low) == 0, 1.0, 2.0)[:, None]
for _e in range(2):
    _columns = slice(_e * _low, (_e + 1) * _low)
    _in = -SIN[:, :_low]
    _in[:, 0] = COS[:, _low]
    FORWARD_X[1, _e * GX : (_e + 1) * GX, _columns] = COS[:, :_low]
    FORWARD_X[1, _e * GX : (_e + 1) * GX, GX + _e * _low : GX + (_e + 1) * _low] = _in
    BACK_X[0, _e] = quarters(COS[:, _columns], SIN[:, _columns], -SIN[:, _columns], COS[:, _columns])
    _out_re = bf(COS[:_low].astype(np.float32) * _pair)
    _out_im = bf(-SIN[:_low].astype(np.float32) * _pair)
    _out_im[0] = COS[_low]
    for _side in range(2):
        _half = slice(_side * _low, (_side + 1) * _low)
        BACK_X[1, _side, _columns, _columns] = _out_re[:, _half]
        BACK_X[1, _side, GX + _e * _low : GX + (_e + 1) * _low, _columns] = _out_im[:, _half]
_across = interpolation(GY, PIX)
_mirror = (-np.arange(GY)) % GY
ACROSS_X = np.zeros((2, 2, 2 * PIX, GX), np.float32)
ACROSS_X[0, 0, :PIX] = _across.T
ACROSS_X[0, 1, PIX:] = _across[_mirror].T
EDGE_ACROSS = np.zeros((2 * PIX, 2 * PIX), np.float32)
for _e in range(2):
    _rows, _columns = slice(_e * PIX, (_e + 1) * PIX), slice(_e * _low, (_e + 1) * _low)
    ACROSS_X[1, 0, _rows, _columns] = _across[:_low].T
    ACROSS_X[1, 1, _rows, _columns] = _across[_mirror][:_low].T
    EDGE_ACROSS[_rows, _e * PIX] = _across[_low]
ACROSS_X, EDGE_ACROSS = bf(ACROSS_X), bf(EDGE_ACROSS)
_yh, _xx, _cc, _zz, _z4 = np.meshgrid(
    np.arange(2), np.arange(4), np.arange(2), np.arange(8), np.arange(4), indexing="ij"
)
Z_ORDER = (4 * (64 * _yh + 16 * _xx + 2 * _zz + _cc) + _z4).reshape(-1)
_yh, _yl, _xx, _cc, _zz, _p2 = np.meshgrid(
    np.arange(2), np.arange(2), np.arange(4), np.arange(2), np.arange(8), np.arange(2), indexing="ij"
)
K_ORDER = (4 * (64 * _yh + 16 * _xx + 2 * _zz + _cc) + 2 * _yl + _p2).reshape(-1)
FORWARD_Z = np.stack(
    [
        np.concatenate([t[K_ORDER][:, Z_ORDER[h * 256 : h * 256 + 256]] for t in (COS, SIN)], axis=1)
        for h in range(2)
    ]
)
BACK_Z = np.concatenate([COS[:, K_ORDER], SIN[:, K_ORDER]], axis=1).reshape(2, 256, 2 * GZ)
MIRROR = bf(K_ORDER[None, :] == _mirror[K_ORDER][:, None])
WINDOWS = np.zeros((2, 32, 2, 2, 16), np.float32)
for _m in range(32):
    for _r in range(16):
        WINDOWS[:, _m, 0, 0, _r] = max(0.0, 1.0 - abs(_m / 4 + 3.625 - _r))
        WINDOWS[:, _m, 1, 1, _r] = max(0.0, 1.0 - abs(11.625 - _m / 4 - _r))
WINDOWS[1, 0, 1, 1, :] = 0.0
WINDOWS[1, 0, 1, 1, 0:2] = (0.375, 0.625)
WINDOWS = bf(WINDOWS.reshape(2, 64, 32))

MESH = pl.DeviceIdType.MESH


def dot(first, second):
    return jnp.dot(first, second, preferred_element_type=jnp.float32)


def place():
    slab = lax.axis_index("slab")
    return (slab // 64) * 2 + lax.axis_index("img"), (slab // 16) % 4, (slab // 2) % 8, slab % 2


def device(y, x, z, c):
    return (y % 2, (y // 2) * 64 + x * 16 + z * 2 + c)


def greet(others):
    barrier = pltpu.get_barrier_semaphore()
    for other in others:
        pl.semaphore_signal(barrier, inc=1, device_id=other, device_id_type=MESH)
    return lambda: pl.semaphore_wait(barrier, len(others))


def across(y, k):
    return (y, y + 1 - 2 * (y % 2), (y + 2) % 4, 3 - y)[k]


class Exchange:
    def __init__(self, x_ref, a_ref, r_ref, sems):
        self.x_ref, self.a_ref, self.r_ref = x_ref, a_ref, r_ref
        self.local, self.z_send, self.z_recv, self.p_send, self.p_recv, self.own = sems
        self.y, self.x, self.z, self.c = place()
        self.m = (self.y * 4 + self.x) * 2 + self.c

    def along_z(self, k, step):
        row, depth = across(self.y, k), (self.z + step) % 8
        return pltpu.make_async_remote_copy(
            src_ref=self.x_ref.at[row, :, depth],
            dst_ref=self.a_ref.at[row, :, self.z],
            send_sem=self.z_send.at[k],
            recv_sem=self.z_recv.at[k],
            device_id=device(self.y, self.x, depth, self.c),
            device_id_type=MESH,
        )

    def keep(self, k):
        row = across(self.y, k)
        return pltpu.make_async_copy(
            self.x_ref.at[row, :, self.z], self.a_ref.at[row, :, self.z], self.local.at[k]
        )

    def whole(self, k):
        row = across(self.y, k)
        return pltpu.make_async_remote_copy(
            src_ref=self.x_ref.at[row, :, pl.ds(0, 7)],
            dst_ref=self.a_ref.at[row, :, pl.ds(0, 7)],
            send_sem=self.z_send.at[k],
            recv_sem=self.z_recv.at[k],
            device_id=device(self.y, self.x, (self.z + 1) % 8, self.c),
            device_id_type=MESH,
        )

    def start(self, k):
        for step in (4, 1, 7, 2, 6, 3, 5):
            self.along_z(k, step).start()
        self.keep(k).start()

    def spread(self, k):
        self.keep(k).wait()
        self.whole(k).wait_recv()
        row = across(self.y, k)
        for dx in (2, 1, 3, 0):
            for dc in (0, 1):
                if (k, dx, dc) == (0, 0, 0):
                    self.mine().start()
                    continue
                column, core = (self.x + dx) % 4, (self.c + dc) % 2
                pltpu.make_async_remote_copy(
                    src_ref=self.a_ref.at[row, column, :, core],
                    dst_ref=self.r_ref.at[self.m],
                    send_sem=self.p_send,
                    recv_sem=self.p_recv.at[k],
                    device_id=device(row, column, self.z, core),
                    device_id_type=MESH,
                ).start()

    def mine(self):
        return pltpu.make_async_copy(
            self.a_ref.at[self.y, self.x, :, self.c], self.r_ref.at[self.m], self.own
        )

    def arrived(self, k):
        count = 8 if k else 7
        if not k:
            self.mine().wait()
        pltpu.make_async_remote_copy(
            src_ref=self.r_ref.at[pl.ds(0, count)],
            dst_ref=self.r_ref.at[pl.ds(0, count)],
            send_sem=self.p_send,
            recv_sem=self.p_recv.at[k],
            device_id=device(self.y, self.x, (self.z + 1) % 8, self.c),
            device_id_type=MESH,
        ).wait_recv()

    def finish(self):
        for k in range(4):
            self.whole(k).wait_send()
        pltpu.make_async_remote_copy(
            src_ref=self.r_ref.at[pl.ds(0, 31)],
            dst_ref=self.r_ref.at[pl.ds(0, 31)],
            send_sem=self.p_send,
            recv_sem=self.p_recv.at[0],
            device_id=device(self.y, self.x, (self.z + 1) % 8, self.c),
            device_id_type=MESH,
        ).wait_send()


EXCHANGE_SEMS = [
    pltpu.SemaphoreType.DMA((4,)),
    pltpu.SemaphoreType.DMA((4,)),
    pltpu.SemaphoreType.DMA((4,)),
    pltpu.SemaphoreType.DMA,
    pltpu.SemaphoreType.DMA((4,)),
    pltpu.SemaphoreType.DMA,
]
BLOCKS = (4, 4, 8, 2, 16, 128)
ORDER = (2, 3, 1, 0)


def partners():
    y, x, z, c = place()
    return [device(y, x, (z + d) % 8, c) for d in range(1, 8)] + [
        device((y + d // 8) % 4, (x + d // 2 % 4) % 4, z, (c + d) % 2) for d in range(1, 32)
    ]


TABLES = (FORWARD_Y, WINDOWS, FORWARD_X, FORWARD_Z, MIRROR, ACROSS_X, EDGE_ACROSS, BACK_Z, BACK_X, BACK_Y)
CHOSEN = (2, 5, 8)


def step_kernel(scale, orient_in, sharp_in, density_in, images, support_in, *rest):
    count = len(TABLES)
    sources, out_ref, rest = rest[:count], rest[count], rest[count + 1 :]
    tables, rest = rest[:count], rest[count:]
    (
        orient, sharp, density, r_ref, e_ref,
        x_ref, a_ref, stage, held, parts, sent, got, padded, g_ref, h_ref, made, whole_rows,
        x_back, a_back, r_back, wide, lines, spectrum, edges, depth_sum, edge_sum, amplitude, amplitude_edge,
        projected, projected_edge, final,
        support, d_load, t_load, load, o_send, c_send, c_recv, g_send, g_recv, g_own, e_send, e_recv, e_own, *sems,
    ) = rest
    (
        table, windows, forward_x, forward_z, mirror, across_x, edge_across, back_z, back_x_table, back_y,
    ) = tables
    y, x, z, c = place()
    image = lax.axis_index("img")
    slab = lax.axis_index("slab")
    m = (y * 4 + x) * 2 + c
    special = jnp.where(slab + image == 0, 1, 0)
    both_real = special == 1

    def beside(shift, turn):
        return ((image + turn) % 2, (slab + shift + 128) % 128)

    moves = [(shift, turn) for shift in (-1, 0, 1) for turn in (0, 1) if (shift, turn) != (0, 0)]
    entered = greet(partners() + [beside(*move) for move in moves])
    fills = [
        pltpu.make_async_copy(
            sources[i].at[special] if i in CHOSEN else sources[i], tables[i], t_load.at[i]
        )
        for i in range(len(TABLES))
    ]
    first_fills = [
        fills[0],
        pltpu.make_async_copy(density_in, density, d_load.at[0]),
        pltpu.make_async_copy(orient_in, orient, d_load.at[1]),
        pltpu.make_async_copy(sharp_in, sharp, d_load.at[2]),
    ]
    fetch = pltpu.make_async_copy(images, held, load)
    for fill in first_fills:
        fill.start()
    fetch.start()
    fills.append(pltpu.make_async_copy(support_in, support, d_load.at[3]))
    for fill in fills[1:]:
        fill.start()
    exchange = Exchange(x_ref, a_ref, r_ref, sems[:6])
    back = Exchange(x_back, a_back, r_back, sems[6:])
    for fill in first_fills:
        fill.wait()

    def transform(k):
        row = across(y, k)
        for plane in range(4):
            out = dot(table[row], density[plane])
            for part in range(2):
                for side in range(2):
                    stage[pl.ds(plane * 4 + part * 2 + side, 64, stride=16), :] = out[
                        part * 64 : part * 64 + 64, side * 128 : side * 128 + 128
                    ]
        x_ref[row] = stage[...].astype(jnp.bfloat16).reshape(4, 8, 2, 16, 128)

    transform(2)
    entered()
    exchange.start(2)
    transform(3)
    exchange.start(3)

    near = orient[...] - slab * 4
    steps = lax.broadcasted_iota(jnp.int32, (16, 64), 0) - 4 - near
    squares = (steps * steps).astype(jnp.float32)
    raw = jnp.exp(-sharp[...] * squares)
    total = 1.0 + 2.0 * (
        jnp.exp(-sharp[...])
        + jnp.exp(-4.0 * sharp[...])
        + jnp.exp(-9.0 * sharp[...])
        + jnp.exp(-16.0 * sharp[...])
    )
    mixing = jnp.where(jnp.abs(steps) <= 4, raw / total, 0.0)
    high = mixing.astype(jnp.bfloat16)
    low = (mixing - high.astype(jnp.float32)).astype(jnp.bfloat16)
    factors = jnp.concatenate(
        [
            jnp.concatenate([high, high], axis=1),
            jnp.concatenate([low, jnp.zeros_like(low)], axis=1),
        ],
        axis=0,
    )
    fetch.wait()

    def mix(index, carry):
        at = index * 2
        rows = jnp.concatenate(
            [held[pl.ds(at, 64, stride=128), :], held[pl.ds(at + 1, 64, stride=128), :]], axis=1
        )
        upper = rows.astype(jnp.bfloat16)
        lower = (rows - upper.astype(jnp.float32)).astype(jnp.bfloat16)
        out = dot(factors, jnp.concatenate([upper, lower], axis=0))
        out = out[:16] + out[16:]
        parts[pl.ds(at, 16, stride=128), :] = out[:, :128]
        parts[pl.ds(at + 1, 16, stride=128), :] = out[:, 128:]
        return carry

    lax.fori_loop(0, 64, mix, 0, unroll=8)
    sent[...] = parts[...].astype(jnp.bfloat16).reshape(16, 128, 128)


    def gift(index, shift, turn):
        first = 4 + 4 * shift + 2 * ((image + turn) % 2)
        return pltpu.make_async_remote_copy(
            src_ref=sent.at[pl.ds(first, 2)],
            dst_ref=got.at[index],
            send_sem=c_send.at[index],
            recv_sem=c_recv.at[index],
            device_id=beside(shift, turn),
            device_id_type=MESH,
        )

    gifts = [gift(index, *move) for index, move in enumerate(moves)]
    for copy in gifts:
        copy.start()
    transform(1)
    exchange.start(1)
    transform(0)
    exchange.spread(2)
    for copy in gifts:
        copy.wait()
    padded[...] = jnp.zeros_like(padded)
    for plane in range(2):
        own = sent[4 + 2 * image + plane].astype(jnp.float32)
        for index, (shift, turn) in enumerate(moves):
            piece = got[index, plane].astype(jnp.float32)
            if shift:
                source = slab - shift
                piece = jnp.where(jnp.logical_and(source >= 0, source < 128), piece, 0.0)
            own = own + piece
        padded[plane, pl.ds(16, 128), :] = own
        for depth in range(8):
            g_ref[depth, plane, pl.ds(0, 16), :] = padded[
                plane, pl.ds(16 + 8 * depth - 4, 16), :
            ].astype(jnp.bfloat16)
            mirrored = padded[plane, pl.ds(16 + 116 - 8 * depth, 16), :]
            if depth == 0:
                mirrored = jnp.concatenate([own[63:65], mirrored[2:]], axis=0)
            g_ref[depth, plane, pl.ds(16, 16), :] = mirrored.astype(jnp.bfloat16)

    def window(step):
        depth = (z + step) % 8
        return pltpu.make_async_remote_copy(
            src_ref=g_ref.at[depth],
            dst_ref=h_ref.at[z],
            send_sem=g_send,
            recv_sem=g_recv,
            device_id=device(y, x, depth, c),
            device_id_type=MESH,
        )

    for step in (4, 1, 7, 2, 6, 3, 5):
        window(step).start()
    stay = pltpu.make_async_copy(g_ref.at[z], h_ref.at[z], g_own)
    stay.start()
    exchange.start(0)
    exchange.spread(3)
    for fill in fills[1:]:
        fill.wait()

    def along_x(half):
        for side in range(2):
            wide[pl.ds(side * 1024, 1024), :] = (
                r_ref[pl.ds((half * 2 + side) * 8, 8)].astype(jnp.float32).reshape(1024, 128)
            )
        for part in range(2):
            for side in range(2):
                for block in range(2):
                    at = part * 512 + side * 256 + block * 128
                    lines[:, pl.ds(at, 128)] = wide[
                        pl.ds(side * 1024 + part * 2 + block, 256, stride=4), :
                    ].astype(jnp.bfloat16)
        both = dot(lines[...], forward_x[...]).astype(jnp.bfloat16)
        spectrum[pl.ds(0, 256), :] = both
        spectrum[pl.ds(256, 256), pl.ds(0, GX)] = both[:, GX:]
        spectrum[pl.ds(256, 256), pl.ds(GX, GX)] = -both[:, :GX]

        @pl.when(both_real)
        def _():
            first_lane = lax.broadcasted_iota(jnp.int32, (256, 128), 1) == 0
            zero = jnp.zeros((256, 128), jnp.bfloat16)
            edges[...] = jnp.zeros_like(edges)
            for part in range(2):
                mixed = spectrum[pl.ds(0, 256), pl.ds(GX + part * 256, 128)].astype(jnp.float32)
                edge = jnp.where(first_lane, mixed, 0.0)
                kept_part = (mixed - edge).astype(jnp.bfloat16)
                edge = edge.astype(jnp.bfloat16)
                spectrum[pl.ds(0, 256), pl.ds(GX + part * 256, 128)] = kept_part
                spectrum[pl.ds(256, 256), pl.ds(part * 256, 128)] = kept_part
                edges[pl.ds(0, 256), pl.ds(part * 128, 128)] = edge
                edges[pl.ds(256, 256), pl.ds(256 + part * 128, 128)] = zero - edge

    def block_of(block):
        return pl.ds(pl.multiple_of(block * 128, 128), 128)

    other_half, own_half = 1 - y // 2, y // 2
    exchange.arrived(2)
    exchange.arrived(3)
    along_x(other_half)

    def first_depth(block, carry):
        at = block_of(block)
        weights = forward_z[other_half, at, :]
        depth_sum[at, :] = dot(weights, spectrum[...])

        @pl.when(both_real)
        def _():
            edge_sum[at, :] = dot(weights, edges[...])

        return carry

    lax.fori_loop(0, 4, first_depth, 0)
    exchange.spread(1)
    stay.wait()
    seven = pltpu.make_async_remote_copy(
        src_ref=g_ref.at[pl.ds(0, 7)],
        dst_ref=h_ref.at[pl.ds(0, 7)],
        send_sem=g_send,
        recv_sem=g_recv,
        device_id=device(y, x, (z + 1) % 8, c),
        device_id_type=MESH,
    )
    seven.wait_send()
    seven.wait_recv()
    weights = windows[jnp.where(z == 0, 1, 0)]
    for source in range(8):
        for plane in range(2):
            made[pl.ds(source * 2 + plane, 64, stride=16), :] = dot(weights, h_ref[source, plane])
    whole_rows[...] = made[...].astype(jnp.bfloat16).reshape(32, 2, 16, 128)
    for d in range(1, 32):
        row, column, core = (y + d // 8) % 4, (x + d // 2 % 4) % 4, (c + d) % 2
        pltpu.make_async_remote_copy(
            src_ref=whole_rows.at[(row * 4 + column) * 2 + core],
            dst_ref=e_ref.at[m],
            send_sem=e_send,
            recv_sem=e_recv,
            device_id=device(row, column, z, core),
            device_id_type=MESH,
        ).start()
    kept = pltpu.make_async_copy(whole_rows.at[m], e_ref.at[m], e_own)
    kept.start()
    exchange.spread(0)
    kept.wait()
    others = pltpu.make_async_remote_copy(
        src_ref=whole_rows.at[pl.ds(0, 31)],
        dst_ref=e_ref.at[pl.ds(0, 31)],
        send_sem=e_send,
        recv_sem=e_recv,
        device_id=device(y, x, (z + 1) % 8, c),
        device_id_type=MESH,
    )
    others.wait_send()
    others.wait_recv()

    def rounded_root(rows, across_table):
        return jnp.sqrt(scale * dot(rows, across_table)).astype(jnp.bfloat16).astype(jnp.float32)

    near = jnp.concatenate([e_ref[:, part].reshape(GZ, PIX) for part in range(2)], axis=1)
    far = dot(mirror[...], near).astype(jnp.bfloat16)
    amplitude[...] = 0.5 * (rounded_root(near, across_x[0]) + rounded_root(far, across_x[1]))

    @pl.when(both_real)
    def _():
        amplitude_edge[...] = 0.5 * (
            rounded_root(near, edge_across[...]) + rounded_root(far, edge_across[...])
        )

    exchange.arrived(1)
    exchange.arrived(0)
    along_x(own_half)

    def projection(real_z, imag_z, target):
        inverse = lax.rsqrt(real_z * real_z + imag_z * imag_z)
        factor = target * jnp.minimum(inverse, 1.0 / least_modulus)
        return (real_z * factor).astype(jnp.bfloat16), (imag_z * factor).astype(jnp.bfloat16)

    def along_depth(block, carry):
        at = block_of(block)
        below = pl.ds(pl.multiple_of(GZ + block * 128, 128), 128)
        weights = forward_z[own_half, at, :]
        total = depth_sum[at, :] + dot(weights, spectrum[...])
        real, imag = projection(total[:, :GX], total[:, GX:], amplitude[at, :])
        projected[at, pl.ds(0, GX)] = real
        projected[at, pl.ds(GX, GX)] = imag
        projected[below, pl.ds(0, GX)] = -imag
        projected[below, pl.ds(GX, GX)] = real

        @pl.when(both_real)
        def _():
            total = edge_sum[at, :] + dot(weights, edges[...])
            real, imag = projection(total[:, :256], total[:, 256:], amplitude_edge[at, :])
            projected_edge[at, :] = real
            projected_edge[below, :] = -imag

        return carry

    lax.fori_loop(0, 4, along_depth, 0)

    def back_depth(half):
        lines[...] = dot(back_z[half], projected[...]).astype(jnp.bfloat16)

        @pl.when(both_real)
        def _():
            first_lane = lax.broadcasted_iota(jnp.int32, (256, 128), 1) == 0
            edge = dot(back_z[half], projected_edge[...])
            for part in range(2):
                at = pl.ds(GX + part * 256, 128)
                lines[:, at] = jnp.where(
                    first_lane,
                    edge[:, part * 128 : part * 128 + 128],
                    lines[:, at].astype(jnp.float32),
                ).astype(jnp.bfloat16)

    def back_x(k):
        row = across(y, k)
        out = dot(lines[...], back_x_table[row % 2])
        for block in range(4):
            stage[pl.ds(block, 256, stride=4), :] = out[:, block * 128 : block * 128 + 128]
        x_back[row] = stage[...].astype(jnp.bfloat16).reshape(4, 8, 2, 16, 128)
        back.start(k)

    back_depth(other_half)
    back_x(2)
    back_x(3)
    back_depth(own_half)
    back_x(1)
    back_x(0)

    def along_y(half, last):
        wide[...] = r_back[pl.ds(half * 16, 16)].astype(jnp.float32).reshape(2048, 128)
        for plane in range(4):
            rows = [
                jnp.concatenate(
                    [
                        wide[pl.ds(plane * 4 + part * 2 + side, 128, stride=16), :]
                        for side in range(2)
                    ],
                    axis=1,
                ).astype(jnp.bfloat16)
                for part in range(2)
            ]
            out = dot(back_y[half], jnp.concatenate(rows, axis=0))
            if last:
                out = final[plane] + out
                previous = density[plane].astype(jnp.float32)
                final[plane] = jnp.where(support[plane] == 1, out, previous - feedback * out)
                pltpu.make_async_copy(final.at[plane], out_ref.at[plane], o_send.at[plane]).start()
            else:
                final[plane] = out

    for k in ORDER:
        back.spread(k)
        if k == 1:
            back.arrived(2)
            back.arrived(3)
            along_y(other_half, False)
    back.arrived(1)
    back.arrived(0)
    along_y(own_half, True)
    exchange.finish()
    back.finish()
    for plane in range(4):
        pltpu.make_async_copy(final.at[plane], out_ref.at[plane], o_send.at[plane]).wait()


def exchange_step(scale, density, orient, sharp, images, support):
    far = pl.BlockSpec(memory_space=pltpu.HBM)
    bfloat, single = jnp.bfloat16, jnp.float32
    one = pltpu.SemaphoreType.DMA
    tiles = (32, 8, 16, 128)
    return pl.pallas_call(
        functools.partial(step_kernel, scale),
        out_shape=jax.ShapeDtypeStruct(density.shape, single),
        in_specs=[far] * (5 + len(TABLES)),
        out_specs=far,
        scratch_shapes=[
            pltpu.VMEM(t.shape[1:] if i in CHOSEN else t.shape, bfloat) for i, t in enumerate(TABLES)
        ]
        + [
            pltpu.VMEM((1, 64), jnp.int32),
            pltpu.VMEM((1, 64), single),
            pltpu.VMEM(density.shape, bfloat),
            pltpu.VMEM(tiles, bfloat),
            pltpu.VMEM((32, 2, 16, 128), bfloat),
            pltpu.VMEM(BLOCKS, bfloat),
            pltpu.VMEM(BLOCKS, bfloat),
            pltpu.VMEM((1024, 128), single),
            pltpu.VMEM((64 * 128, 128), single),
            pltpu.VMEM((16 * 128, 128), single),
            pltpu.VMEM((16, 128, 128), bfloat),
            pltpu.VMEM((5, 2, 128, 128), bfloat),
            pltpu.VMEM((2, 160, 128), single),
            pltpu.VMEM((8, 2, 32, 128), bfloat),
            pltpu.VMEM((8, 2, 32, 128), bfloat),
            pltpu.VMEM((1024, 128), single),
            pltpu.VMEM((32, 2, 16, 128), bfloat),
            pltpu.VMEM(BLOCKS, bfloat),
            pltpu.VMEM(BLOCKS, bfloat),
            pltpu.VMEM(tiles, bfloat),
            pltpu.VMEM((2048, 128), single),
            pltpu.VMEM((256, 2 * GX), bfloat),
            pltpu.VMEM((512, 2 * GX), bfloat),
            pltpu.VMEM((512, 512), bfloat),
            pltpu.VMEM((GZ, 2 * GX), single),
            pltpu.VMEM((GZ, 512), single),
            pltpu.VMEM((GZ, GX), single),
            pltpu.VMEM((GZ, 256), single),
            pltpu.VMEM((2 * GZ, 2 * GX), bfloat),
            pltpu.VMEM((2 * GZ, 256), bfloat),
            pltpu.VMEM(density.shape, single),
            pltpu.VMEM(density.shape, jnp.int32),
            one((4,)), one((len(TABLES),)), one, one((4,)), one((5,)), one((5,)), one, one, one, one, one, one,
        ]
        + EXCHANGE_SEMS * 2,
        compiler_params=pltpu.CompilerParams(
            collective_id=1, has_side_effects=True, vmem_limit_bytes=63 << 20
        ),
    )(
        orient.reshape(1, -1),
        sharp.reshape(1, -1),
        density,
        images.reshape(-1, PIX),
        support,
        *TABLES,
    )


def body(images, orient, sharp, density, support):
    depth = density.shape[0]
    scale = depth / (images.shape[0] * lax.axis_size("img"))
    return exchange_step(scale, density, orient, sharp, images, support)


def solution(mesh):
    placed = (
        P(("img", "slab"), None, None),
        P(("img", "slab")),
        P(("img", "slab")),
        P("slab", None, "img"),
        P("slab", None, "img"),
    )
    return jax.shard_map(
        body, mesh=mesh, in_specs=placed, out_specs=P("slab", None, "img"), check_vma=False
    )
```

```python
import functools
import math

import jax
import jax.numpy as jnp
import ml_dtypes
import numpy as np
from jax import lax
from jax.experimental import pallas as pl
from jax.experimental.pallas import tpu as pltpu
from jax.sharding import PartitionSpec as P

GZ = 512
GY = 512
GX = 512
PIX = 128

least_modulus = 0.5
feedback = 0.9


def dft_tables(length):
    index = np.arange(length, dtype=np.int64)
    product = (index[:, None] * index[None, :]) % length
    angles = product.astype(np.float32) * np.float32(2.0 * math.pi / length)
    factor = np.float32(1.0 / math.sqrt(length))
    return (
        (np.cos(angles) * factor).astype(ml_dtypes.bfloat16),
        (np.sin(angles) * factor).astype(ml_dtypes.bfloat16),
    )


def interpolation(cells, pixels):
    grid = np.arange(cells, dtype=np.float32)
    detector = np.arange(pixels, dtype=np.float32)
    position = (grid + np.float32(0.5)) * np.float32(pixels / cells) - np.float32(0.5)
    return np.maximum(
        np.float32(0.0), np.float32(1.0) - np.abs(position[:, None] - detector[None, :])
    )


def bf(table):
    return np.asarray(table).astype(ml_dtypes.bfloat16)


COS, SIN = dft_tables(GY)
HALF = GY // 2
_y, _x, _z, _s = np.meshgrid(np.arange(4), np.arange(4), np.arange(8), np.arange(2), indexing="ij")
ROW_OF = 32 * _z + 8 * _y + 2 * _x + _s
_imag = np.concatenate([COS[HALF : HALF + 1], -SIN[1:HALF]])
FORWARD_Y = np.stack(
    [
        [
            np.concatenate([t[ROW_OF[2 * h : 2 * h + 2, :, :, e].reshape(-1)] for t in (COS, _imag)])
            for h in range(2)
        ]
        for e in range(2)
    ]
)
_two = 2.0 * COS[:, :HALF].astype(np.float32)
_two[:, 0] = COS[:, 0]
_sin = -2.0 * SIN[:, :HALF].astype(np.float32)
_sin[:, 0] = COS[:, HALF]
BACK_Y = np.concatenate(
    [
        bf(t.reshape(GY, 8, 16, 2).transpose(3, 0, 2, 1).reshape(2, GY, 128))
        for t in (_two, _sin)
    ],
    axis=2,
)


def quarters(upper_left, upper_right, lower_left, lower_right):
    return np.concatenate(
        [
            np.concatenate([upper_left, upper_right], axis=1),
            np.concatenate([lower_left, lower_right], axis=1),
        ],
        axis=0,
    )


FORWARD_X = np.zeros((2, 2 * GX, 2 * GX), ml_dtypes.bfloat16)
BACK_X = np.zeros((2, 2, 2 * GX, GX), ml_dtypes.bfloat16)
_low = GX // 2
_pair = np.where(np.arange(_low) == 0, 1.0, 2.0)[:, None]
_in = -SIN[:, :_low]
_in[:, 0] = COS[:, _low]
_out_re = bf(COS[:_low].astype(np.float32) * _pair)
_out_im = bf(-SIN[:_low].astype(np.float32) * _pair)
_out_im[0] = COS[_low]
for _e in range(2):
    _half = slice(_e * _low, (_e + 1) * _low)
    _place = slice(_e * GX, (_e + 1) * GX)
    FORWARD_X[0, :, _place] = quarters(COS[:, _half], -SIN[:, _half], SIN[:, _half], COS[:, _half])
    FORWARD_X[1, _place, _place] = np.concatenate([COS[:, :_low], _in], axis=1)
    for _side in range(2):
        _to = slice(_side * _low, (_side + 1) * _low)
        _cos, _sine = COS[_half, _to], SIN[_half, _to]
        BACK_X[0, _side, _place] = quarters(_cos, _sine, -_sine, _cos)
        BACK_X[1, _side, _place, _half] = np.concatenate([_out_re[:, _to], _out_im[:, _to]])
_across = interpolation(GY, PIX)
_mirror = (-np.arange(GY)) % GY
ACROSS_X = np.zeros((4, 2, 2 * PIX, _low), np.float32)
EDGE_ACROSS = np.zeros((2, 2 * PIX, PIX), np.float32)
for _e in range(2):
    _half, _rows = slice(_e * _low, (_e + 1) * _low), slice(_e * PIX, (_e + 1) * PIX)
    ACROSS_X[_e, 0, :PIX] = _across[_half].T
    ACROSS_X[_e, 1, PIX:] = _across[_mirror][_half].T
    ACROSS_X[2 + _e, 0, _rows] = _across[:_low].T
    ACROSS_X[2 + _e, 1, _rows] = _across[_mirror][:_low].T
    EDGE_ACROSS[_e, _rows, 0] = _across[_low]
ACROSS_X, EDGE_ACROSS = bf(ACROSS_X), bf(EDGE_ACROSS)
_yh, _xx, _cc, _zz, _z4 = np.meshgrid(
    np.arange(2), np.arange(4), np.arange(2), np.arange(8), np.arange(4), indexing="ij"
)
Z_ORDER = (4 * (64 * _yh + 16 * _xx + 2 * _zz + _cc) + _z4).reshape(-1)
_yh, _yl, _xx, _cc, _zz, _p2 = np.meshgrid(
    np.arange(2), np.arange(2), np.arange(4), np.arange(2), np.arange(8), np.arange(2), indexing="ij"
)
K_ORDER = (4 * (64 * _yh + 16 * _xx + 2 * _zz + _cc) + 2 * _yl + _p2).reshape(-1)
FORWARD_Z = np.concatenate([t[K_ORDER][:, Z_ORDER] for t in (COS, SIN)], axis=1)
BACK_Z = np.concatenate([COS[:, K_ORDER], SIN[:, K_ORDER]], axis=1).reshape(2, 256, 2 * GZ)
MIRROR = bf(K_ORDER[None, :] == _mirror[K_ORDER][:, None])
WINDOWS = np.zeros((2, 32, 2, 2, 16), np.float32)
for _m in range(32):
    for _r in range(16):
        WINDOWS[:, _m, 0, 0, _r] = max(0.0, 1.0 - abs(_m / 4 + 3.625 - _r))
        WINDOWS[:, _m, 1, 1, _r] = max(0.0, 1.0 - abs(11.625 - _m / 4 - _r))
WINDOWS[1, 0, 1, 1, :] = 0.0
WINDOWS[1, 0, 1, 1, 0:2] = (0.375, 0.625)
WINDOWS = bf(WINDOWS.reshape(2, 64, 32))

MESH = pl.DeviceIdType.MESH


def dot(first, second):
    return jnp.dot(first, second, preferred_element_type=jnp.float32)


def place():
    slab = lax.axis_index("slab")
    return (slab // 64) * 2 + lax.axis_index("img"), (slab // 16) % 4, (slab // 2) % 8, slab % 2


def device(y, x, z, c):
    return (y % 2, (y // 2) * 64 + x * 16 + z * 2 + c)


def greet(others):
    barrier = pltpu.get_barrier_semaphore()
    for other in others:
        pl.semaphore_signal(barrier, inc=1, device_id=other, device_id_type=MESH)
    return lambda: pl.semaphore_wait(barrier, len(others))


def across(y, k):
    return (y, y + 1 - 2 * (y % 2), (y + 2) % 4, 3 - y)[k]


class Exchange:
    def __init__(self, x_ref, a_ref, r_ref, sems):
        self.x_ref, self.a_ref, self.r_ref = x_ref, a_ref, r_ref
        self.local, self.z_send, self.z_recv, self.p_send, self.p_recv, self.own = sems
        self.y, self.x, self.z, self.c = place()
        self.within = self.c == self.y // 2

    def move(self, source, target, send, recv, where):
        return pltpu.make_async_remote_copy(
            src_ref=source,
            dst_ref=target,
            send_sem=send,
            recv_sem=recv,
            device_id=device(*where),
            device_id_type=MESH,
        )

    def start(self, part, k):
        row, index = self.row(k), part * self.parts + k
        for step in (4, 1, 7, 2, 6, 3, 5):
            depth = (self.z + step) % 8
            self.move(
                self.x_ref.at[part, row, :, depth],
                self.a_ref.at[part, row, :, self.z],
                self.z_send.at[index],
                self.z_recv.at[index],
                (self.y, self.x, depth, self.c),
            ).start()
        self.keep(part, k).start()

    def keep(self, part, k):
        row = self.row(k)
        return pltpu.make_async_copy(
            self.x_ref.at[part, row, :, self.z],
            self.a_ref.at[part, row, :, self.z],
            self.local.at[part * self.parts + k],
        )

    def whole(self, part, k):
        row, index = self.row(k), part * self.parts + k
        return self.move(
            self.x_ref.at[part, row, :, pl.ds(0, 7)],
            self.a_ref.at[part, row, :, pl.ds(0, 7)],
            self.z_send.at[index],
            self.z_recv.at[index],
            (self.y, self.x, (self.z + 1) % 8, self.c),
        )

    def spread(self, part, k):
        self.keep(part, k).wait()
        self.whole(part, k).wait_recv()
        for source, where, mine in self.targets(part, k):
            target = self.r_ref.at[part, self.slot()]
            copy = self.move(source, target, self.p_send, self.p_recv.at[part], where)
            if mine:
                pl.when(self.within)(pltpu.make_async_copy(source, target, self.own.at[part]).start)
                pl.when(jnp.logical_not(self.within))(copy.start)
            else:
                copy.start()

    def blocks(self, part, count):
        piece = self.r_ref.at[part, pl.ds(0, count)]
        where = (self.y, self.x, (self.z + 1) % 8, self.c)
        return self.move(piece, piece, self.p_send, self.p_recv.at[part], where)

    def arrived(self, part):
        @pl.when(self.within)
        def _():
            source = self.r_ref.at[part, 0]
            pltpu.make_async_copy(source, self.r_ref.at[part, self.slot()], self.own.at[part]).wait()
            self.blocks(part, 15).wait_recv()

        @pl.when(jnp.logical_not(self.within))
        def _():
            self.blocks(part, 16).wait_recv()

    def finish(self):
        for part in range(2):
            for k in range(self.parts):
                self.whole(part, k).wait_send()

            @pl.when(self.within)
            def _():
                self.blocks(part, 15).wait_send()

            @pl.when(jnp.logical_not(self.within))
            def _():
                self.blocks(part, 16).wait_send()


class Forward(Exchange):
    parts = 4

    def row(self, k):
        return across(self.y, k)

    def slot(self):
        return (self.y % 2 * 4 + self.x) * 2 + self.c

    def targets(self, part, k):
        row = self.row(k)
        for dx in (2, 1, 3, 0):
            column = (self.x + dx) % 4
            where = (row, column, self.z, self.y // 2)
            yield self.a_ref.at[part, row, column], where, k == 0 and dx == 0


class Back(Exchange):
    parts = 2

    def row(self, k):
        return (self.y + k) % 2

    def slot(self):
        return self.y * 4 + self.x

    def targets(self, part, k):
        row = self.row(k)
        for dx in (2, 1, 3, 0):
            for dc in (0, 1):
                column, core = (self.x + dx) % 4, (self.c + dc) % 2
                where = (2 * self.c + row, column, self.z, core)
                yield self.a_ref.at[part, row, column, :, core], where, (k, dx, dc) == (0, 0, 0)


def exchange_sems(parts):
    one = pltpu.SemaphoreType.DMA
    return [one((2 * parts,)), one((2 * parts,)), one((2 * parts,)), one, one((2,)), one((2,))]


FORWARD_TILES = (2, 4, 4, 8, 16, 128)
BACK_TILES = (2, 2, 4, 8, 2, 16, 128)
LANDED_TILES = (2, 16, 8, 16, 128)
ORDER = (2, 3, 1, 0)


def partners():
    y, x, z, c = place()
    return [device(y, x, (z + d) % 8, c) for d in range(1, 8)] + [
        device((y + d // 8) % 4, (x + d // 2 % 4) % 4, z, (c + d) % 2) for d in range(1, 32)
    ]


TABLES = (
    FORWARD_Y, WINDOWS, FORWARD_X, FORWARD_Z, MIRROR, ACROSS_X, EDGE_ACROSS, BACK_Z, BACK_X, BACK_Y,
)
BY_SET, BY_SET_AND_CORE, BY_CORE = (2, 8), (5,), (6,)


def held_shape(index, table):
    if index in BY_SET + BY_SET_AND_CORE:
        return (2,) + table.shape[1:]
    return table.shape[1:] if index in BY_CORE else table.shape


def step_kernel(scale, orient_in, sharp_in, density_in, images, support_in, *rest):
    count = len(TABLES)
    sources, out_ref, rest = rest[:count], rest[count], rest[count + 1 :]
    tables, rest = rest[:count], rest[count:]
    (
        orient, sharp, density, r_ref, e_ref,
        x_ref, a_ref, stage, held, parts, sent, got, padded, g_ref, h_ref, made, whole_rows,
        x_back, a_back, r_back, wide, lines, halves, landed, spectrum, edges, amplitude, amplitude_edge,
        projected, projected_edge, half_out, half_in, final,
        support, d_load, t_load, load, o_send, c_send, c_recv, g_send, g_recv, g_own, e_send, e_recv, e_own,
        x_send, x_recv, *sems,
    ) = rest
    (
        table, windows, forward_x, forward_z, mirror, across_x, edge_across, back_z, back_x_table, back_y,
    ) = tables
    y, x, z, c = place()
    image = lax.axis_index("img")
    slab = lax.axis_index("slab")
    m = (y * 4 + x) * 2 + c
    special = jnp.where(slab // 2 + image == 0, 1, 0)
    both_real = special == 1

    def beside(shift, turn):
        return ((image + turn) % 2, (slab + shift + 128) % 128)

    moves = [(shift, turn) for shift in (-1, 0, 1) for turn in (0, 1) if (shift, turn) != (0, 0)]
    entered = greet(partners() + [beside(*move) for move in moves])
    fills = []

    def fill(source, target):
        fills.append(pltpu.make_async_copy(source, target, t_load.at[len(fills)]))

    for index, (source, target) in enumerate(zip(sources, tables)):
        if index in BY_SET:
            fill(source.at[special], target.at[0])
            fill(source.at[0], target.at[1])
        elif index in BY_SET_AND_CORE:
            fill(source.at[special * 2 + c], target.at[0])
            fill(source.at[c], target.at[1])
        else:
            fill(source.at[c] if index in BY_CORE else source, target)
    first_fills = [
        fills[0],
        pltpu.make_async_copy(density_in, density, d_load.at[0]),
        pltpu.make_async_copy(orient_in, orient, d_load.at[1]),
        pltpu.make_async_copy(sharp_in, sharp, d_load.at[2]),
    ]
    fetch = pltpu.make_async_copy(images, held, load)
    for fill in first_fills:
        fill.start()
    fetch.start()
    fills.append(pltpu.make_async_copy(support_in, support, d_load.at[3]))
    for fill in fills[1:]:
        fill.start()
    forward = Forward(x_ref, a_ref, r_ref, sems[:6])
    back = Back(x_back, a_back, r_back, sems[6:])
    for fill in first_fills:
        fill.wait()

    def transform(part, half):
        for plane in range(4):
            out = dot(table[part, half], density[plane])
            for piece in range(2):
                for side in range(2):
                    stage[pl.ds(plane * 4 + piece * 2 + side, 64, stride=16), :] = out[
                        piece * 64 : piece * 64 + 64, side * 128 : side * 128 + 128
                    ]
        x_ref[part, pl.ds(half * 2, 2)] = stage[...].astype(jnp.bfloat16).reshape(2, 4, 8, 16, 128)

    other_half, own_half = 1 - y // 2, y // 2
    transform(0, other_half)
    entered()
    forward.start(0, 2)
    forward.start(0, 3)

    near = orient[...] - slab * 4
    steps = lax.broadcasted_iota(jnp.int32, (16, 64), 0) - 4 - near
    squares = (steps * steps).astype(jnp.float32)
    raw = jnp.exp(-sharp[...] * squares)
    total = 1.0 + 2.0 * (
        jnp.exp(-sharp[...])
        + jnp.exp(-4.0 * sharp[...])
        + jnp.exp(-9.0 * sharp[...])
        + jnp.exp(-16.0 * sharp[...])
    )
    mixing = jnp.where(jnp.abs(steps) <= 4, raw / total, 0.0)
    high = mixing.astype(jnp.bfloat16)
    low = (mixing - high.astype(jnp.float32)).astype(jnp.bfloat16)
    factors = jnp.concatenate(
        [
            jnp.concatenate([high, high], axis=1),
            jnp.concatenate([low, jnp.zeros_like(low)], axis=1),
        ],
        axis=0,
    )
    fetch.wait()

    def mix(index, carry):
        at = index * 2
        rows = jnp.concatenate(
            [held[pl.ds(at, 64, stride=128), :], held[pl.ds(at + 1, 64, stride=128), :]], axis=1
        )
        upper = rows.astype(jnp.bfloat16)
        lower = (rows - upper.astype(jnp.float32)).astype(jnp.bfloat16)
        out = dot(factors, jnp.concatenate([upper, lower], axis=0))
        out = out[:16] + out[16:]
        parts[pl.ds(at, 16, stride=128), :] = out[:, :128]
        parts[pl.ds(at + 1, 16, stride=128), :] = out[:, 128:]
        return carry

    lax.fori_loop(0, 64, mix, 0, unroll=8)
    sent[...] = parts[...].astype(jnp.bfloat16).reshape(16, 128, 128)


    def gift(index, shift, turn):
        first = 4 + 4 * shift + 2 * ((image + turn) % 2)
        return pltpu.make_async_remote_copy(
            src_ref=sent.at[pl.ds(first, 2)],
            dst_ref=got.at[index],
            send_sem=c_send.at[index],
            recv_sem=c_recv.at[index],
            device_id=beside(shift, turn),
            device_id_type=MESH,
        )

    gifts = [gift(index, *move) for index, move in enumerate(moves)]
    for copy in gifts:
        copy.start()
    transform(0, own_half)
    forward.start(0, 1)
    forward.start(0, 0)
    transform(1, other_half)
    transform(1, own_half)
    forward.spread(0, 2)
    for copy in gifts:
        copy.wait()
    padded[...] = jnp.zeros_like(padded)
    for plane in range(2):
        own = sent[4 + 2 * image + plane].astype(jnp.float32)
        for index, (shift, turn) in enumerate(moves):
            piece = got[index, plane].astype(jnp.float32)
            if shift:
                source = slab - shift
                piece = jnp.where(jnp.logical_and(source >= 0, source < 128), piece, 0.0)
            own = own + piece
        padded[plane, pl.ds(16, 128), :] = own
        for depth in range(8):
            g_ref[depth, plane, pl.ds(0, 16), :] = padded[
                plane, pl.ds(16 + 8 * depth - 4, 16), :
            ].astype(jnp.bfloat16)
            mirrored = padded[plane, pl.ds(16 + 116 - 8 * depth, 16), :]
            if depth == 0:
                mirrored = jnp.concatenate([own[63:65], mirrored[2:]], axis=0)
            g_ref[depth, plane, pl.ds(16, 16), :] = mirrored.astype(jnp.bfloat16)

    def window(step):
        depth = (z + step) % 8
        return pltpu.make_async_remote_copy(
            src_ref=g_ref.at[depth],
            dst_ref=h_ref.at[z],
            send_sem=g_send,
            recv_sem=g_recv,
            device_id=device(y, x, depth, c),
            device_id_type=MESH,
        )

    for step in (4, 1, 7, 2, 6, 3, 5):
        window(step).start()
    stay = pltpu.make_async_copy(g_ref.at[z], h_ref.at[z], g_own)
    stay.start()
    for k in ORDER:
        forward.start(1, k)
    forward.spread(0, 3)
    for fill in fills[1:]:
        fill.wait()
    forward.spread(0, 1)
    forward.spread(0, 0)
    stay.wait()
    seven = pltpu.make_async_remote_copy(
        src_ref=g_ref.at[pl.ds(0, 7)],
        dst_ref=h_ref.at[pl.ds(0, 7)],
        send_sem=g_send,
        recv_sem=g_recv,
        device_id=device(y, x, (z + 1) % 8, c),
        device_id_type=MESH,
    )
    seven.wait_send()
    seven.wait_recv()
    weights = windows[jnp.where(z == 0, 1, 0)]
    for source in range(8):
        for plane in range(2):
            made[pl.ds(source * 2 + plane, 64, stride=16), :] = dot(weights, h_ref[source, plane])
    whole_rows[...] = made[...].astype(jnp.bfloat16).reshape(16, 2, 2, 16, 128)
    for d in range(1, 32):
        row, column, core = (y + d // 8) % 4, (x + d // 2 % 4) % 4, (c + d) % 2
        pltpu.make_async_remote_copy(
            src_ref=whole_rows.at[row * 4 + column],
            dst_ref=e_ref.at[m],
            send_sem=e_send,
            recv_sem=e_recv,
            device_id=device(row, column, z, core),
            device_id_type=MESH,
        ).start()
    kept = pltpu.make_async_copy(whole_rows.at[y * 4 + x], e_ref.at[m], e_own)
    kept.start()

    def cross(index, source, target):
        return pltpu.make_async_remote_copy(
            src_ref=source,
            dst_ref=target,
            send_sem=x_send.at[index],
            recv_sem=x_recv.at[index],
            device_id=device(y, x, z, 1 - c),
            device_id_type=MESH,
        )

    def cross_forward(part):
        return cross(part, halves.at[part, 1 - c], landed.at[part, c])

    def cross_back(part):
        return cross(2 + part, half_out.at[part], half_in.at[part, c])

    def along_x(part):
        forward.arrived(part)
        wide[...] = r_ref[part].astype(jnp.float32).reshape(2048, 128)
        for piece in range(2):
            for side in range(2):
                for block in range(2):
                    at = piece * 512 + side * 256 + block * 128
                    lines[:, pl.ds(at, 128)] = wide[
                        pl.ds(side * 1024 + piece * 2 + block, 256, stride=4), :
                    ].astype(jnp.bfloat16)
        both = dot(lines[...], forward_x[part]).astype(jnp.bfloat16)
        for half in range(2):
            halves[part, half] = both[:, half * GX : half * GX + GX]
        cross_forward(part).start()
        landed[part, c] = halves[part, c]

    def rounded_root(rows, across_table):
        return jnp.sqrt(scale * dot(rows, across_table)).astype(jnp.bfloat16).astype(jnp.float32)

    def amplitudes(part):
        near = jnp.concatenate([e_ref[:, part, row].reshape(GZ, PIX) for row in range(2)], axis=1)
        far = dot(mirror[...], near).astype(jnp.bfloat16)
        amplitude[part] = 0.5 * (
            rounded_root(near, across_x[part, 0]) + rounded_root(far, across_x[part, 1])
        )
        if part == 0:

            @pl.when(both_real)
            def _():
                amplitude_edge[...] = 0.5 * (
                    rounded_root(near, edge_across[...]) + rounded_root(far, edge_across[...])
                )

    def projection(real_z, imag_z, target):
        inverse = lax.rsqrt(real_z * real_z + imag_z * imag_z)
        factor = target * jnp.minimum(inverse, 1.0 / least_modulus)
        return (real_z * factor).astype(jnp.bfloat16), (imag_z * factor).astype(jnp.bfloat16)

    def along_z(part):
        cross_forward(part).wait()
        half_x = GX // 2
        for half in range(2):
            top = pl.ds(half * 256, 256)
            low = pl.ds(GZ + half * 256, 256)
            spectrum[top, :] = landed[part, half]
            if part == 0:

                @pl.when(both_real)
                def _():
                    at = pl.ds(half_x, 128)
                    first_lane = lax.broadcasted_iota(jnp.int32, (256, 128), 1) == 0
                    mixed = spectrum[top, at].astype(jnp.float32)
                    edge = jnp.where(first_lane, mixed, 0.0)
                    spectrum[top, at] = (mixed - edge).astype(jnp.bfloat16)
                    zero = jnp.zeros((256, 128), jnp.bfloat16)
                    edges[top, :] = jnp.concatenate([edge.astype(jnp.bfloat16), zero], axis=1)
                    edges[low, :] = jnp.concatenate([zero, (-edge).astype(jnp.bfloat16)], axis=1)

            spectrum[low, pl.ds(0, half_x)] = spectrum[top, pl.ds(half_x, half_x)]
            spectrum[low, pl.ds(half_x, half_x)] = -spectrum[top, pl.ds(0, half_x)]

        def block_of_planes(block, carry):
            at = pl.ds(pl.multiple_of(block * 128, 128), 128)
            low = pl.ds(pl.multiple_of(GZ + block * 128, 128), 128)
            weights = forward_z[at, :]
            total = dot(weights, spectrum[...])
            real, imag = projection(total[:, :half_x], total[:, half_x:], amplitude[part, at, :])
            projected[at, pl.ds(0, half_x)] = real
            projected[at, pl.ds(half_x, half_x)] = imag
            projected[low, pl.ds(0, half_x)] = -imag
            projected[low, pl.ds(half_x, half_x)] = real
            if part == 0:

                @pl.when(both_real)
                def _():
                    total = dot(weights, edges[...])
                    real, imag = projection(total[:, :128], total[:, 128:], amplitude_edge[at, :])
                    projected_edge[at, :] = real
                    projected_edge[low, :] = -imag

            return carry

        lax.fori_loop(0, 4, block_of_planes, 0)

        def inverse(half, target):
            target[...] = dot(back_z[half], projected[...]).astype(jnp.bfloat16)
            if part == 0:

                @pl.when(both_real)
                def _():
                    first_lane = lax.broadcasted_iota(jnp.int32, (256, 128), 1) == 0
                    edge = dot(back_z[half], projected_edge[...])
                    at = pl.ds(half_x, 128)
                    target[:, at] = jnp.where(
                        first_lane, edge, target[:, at].astype(jnp.float32)
                    ).astype(jnp.bfloat16)

        inverse(1 - c, half_out.at[part])
        cross_back(part).start()
        inverse(c, half_in.at[part, c])

    def back_x(part):
        cross_back(part).wait()
        for half in range(2):
            lines[:, pl.ds(half * GX, GX)] = half_in[part, half]
        for k in (1, 0):
            row = (y + k) % 2
            out = dot(lines[...], back_x_table[part, row])
            for block in range(4):
                stage[pl.ds(block, 256, stride=4), :] = out[:, block * 128 : block * 128 + 128]
            x_back[part, row] = stage[...].astype(jnp.bfloat16).reshape(4, 8, 2, 16, 128)
            back.start(part, k)

    def along_y(part):
        back.arrived(part)
        wide[...] = r_back[part].astype(jnp.float32).reshape(2048, 128)
        for plane in range(4):
            rows = [
                jnp.concatenate(
                    [
                        wide[pl.ds(plane * 4 + piece * 2 + side, 128, stride=16), :]
                        for side in range(2)
                    ],
                    axis=1,
                ).astype(jnp.bfloat16)
                for piece in range(2)
            ]
            out = dot(back_y[part], jnp.concatenate(rows, axis=0))
            if part:
                out = final[plane] + out
                previous = density[plane].astype(jnp.float32)
                final[plane] = jnp.where(support[plane] == 1, out, previous - feedback * out)
                pltpu.make_async_copy(final.at[plane], out_ref.at[plane], o_send.at[plane]).start()
            else:
                final[plane] = out

    along_x(0)
    forward.spread(1, 2)
    kept.wait()
    others = pltpu.make_async_remote_copy(
        src_ref=e_ref.at[pl.ds(0, 31)],
        dst_ref=e_ref.at[pl.ds(0, 31)],
        send_sem=e_send,
        recv_sem=e_recv,
        device_id=device(y, x, (z + 1) % 8, c),
        device_id_type=MESH,
    )
    others.wait_send()
    others.wait_recv()
    amplitudes(0)
    along_z(0)
    forward.spread(1, 3)
    forward.spread(1, 1)
    back_x(0)
    amplitudes(1)
    forward.spread(1, 0)
    along_x(1)
    along_z(1)
    back_x(1)
    back.spread(0, 1)
    back.spread(0, 0)
    along_y(0)
    back.spread(1, 1)
    back.spread(1, 0)
    along_y(1)
    forward.finish()
    back.finish()
    for plane in range(4):
        pltpu.make_async_copy(final.at[plane], out_ref.at[plane], o_send.at[plane]).wait()


def exchange_step(scale, density, orient, sharp, images, support):
    far = pl.BlockSpec(memory_space=pltpu.HBM)
    bfloat, single = jnp.bfloat16, jnp.float32
    one = pltpu.SemaphoreType.DMA
    buffers = [
        ((1, 64), jnp.int32),
        ((1, 64), single),
        (density.shape, bfloat),
        (LANDED_TILES, bfloat),
        ((32, 2, 2, 16, 128), bfloat),
        (FORWARD_TILES, bfloat),
        (FORWARD_TILES, bfloat),
        ((1024, 128), single),
        ((64 * 128, 128), single),
        ((16 * 128, 128), single),
        ((16, 128, 128), bfloat),
        ((5, 2, 128, 128), bfloat),
        ((2, 160, 128), single),
        ((8, 2, 32, 128), bfloat),
        ((8, 2, 32, 128), bfloat),
        ((1024, 128), single),
        ((16, 2, 2, 16, 128), bfloat),
        (BACK_TILES, bfloat),
        (BACK_TILES, bfloat),
        (LANDED_TILES, bfloat),
        ((2048, 128), single),
        ((256, 2 * GX), bfloat),
        ((2, 2, 256, GX), bfloat),
        ((2, 2, 256, GX), bfloat),
        ((2 * GZ, GX), bfloat),
        ((2 * GZ, 256), bfloat),
        ((2, GZ, GX // 2), single),
        ((GZ, 128), single),
        ((2 * GZ, GX), bfloat),
        ((2 * GZ, 128), bfloat),
        ((2, 256, GX), bfloat),
        ((2, 2, 256, GX), bfloat),
        (density.shape, single),
        (density.shape, jnp.int32),
    ]
    fill_count = len(TABLES) + len(BY_SET + BY_SET_AND_CORE)
    return pl.pallas_call(
        functools.partial(step_kernel, scale),
        out_shape=jax.ShapeDtypeStruct(density.shape, single),
        in_specs=[far] * (5 + len(TABLES)),
        out_specs=far,
        scratch_shapes=[pltpu.VMEM(held_shape(i, t), bfloat) for i, t in enumerate(TABLES)]
        + [pltpu.VMEM(*buffer) for buffer in buffers]
        + [one((4,)), one((fill_count,)), one, one((4,)), one((5,)), one((5,)), one, one, one, one, one, one]
        + [one((4,)), one((4,))]
        + exchange_sems(4)
        + exchange_sems(2),
        compiler_params=pltpu.CompilerParams(
            collective_id=1, has_side_effects=True, vmem_limit_bytes=63 << 20
        ),
    )(
        orient.reshape(1, -1),
        sharp.reshape(1, -1),
        density,
        images.reshape(-1, PIX),
        support,
        *TABLES,
    )


def body(images, orient, sharp, density, support):
    depth = density.shape[0]
    scale = depth / (images.shape[0] * lax.axis_size("img"))
    return exchange_step(scale, density, orient, sharp, images, support)


def solution(mesh):
    placed = (
        P(("img", "slab"), None, None),
        P(("img", "slab")),
        P(("img", "slab")),
        P("slab", None, "img"),
        P("slab", None, "img"),
    )
    return jax.shard_map(
        body, mesh=mesh, in_specs=placed, out_specs=P("slab", None, "img"), check_vma=False
    )
```

```python
import functools
import math

import jax
import jax.numpy as jnp
import ml_dtypes
import numpy as np
from jax import lax
from jax.experimental import pallas as pl
from jax.experimental.pallas import tpu as pltpu
from jax.sharding import PartitionSpec as P

GZ = 512
GY = 512
GX = 512
PIX = 128

least_modulus = 0.5
feedback = 0.9


def dft_tables(length):
    index = np.arange(length, dtype=np.int64)
    product = (index[:, None] * index[None, :]) % length
    angles = product.astype(np.float32) * np.float32(2.0 * math.pi / length)
    factor = np.float32(1.0 / math.sqrt(length))
    return (
        (np.cos(angles) * factor).astype(ml_dtypes.bfloat16),
        (np.sin(angles) * factor).astype(ml_dtypes.bfloat16),
    )


def interpolation(cells, pixels):
    grid = np.arange(cells, dtype=np.float32)
    detector = np.arange(pixels, dtype=np.float32)
    position = (grid + np.float32(0.5)) * np.float32(pixels / cells) - np.float32(0.5)
    return np.maximum(
        np.float32(0.0), np.float32(1.0) - np.abs(position[:, None] - detector[None, :])
    )


def bf(table):
    return np.asarray(table).astype(ml_dtypes.bfloat16)


COS, SIN = dft_tables(GY)
HALF = GY // 2
_y, _x, _z, _s = np.meshgrid(np.arange(4), np.arange(4), np.arange(8), np.arange(2), indexing="ij")
ROW_OF = 32 * _z + 8 * _y + 2 * _x + _s
_imag = np.concatenate([COS[HALF : HALF + 1], -SIN[1:HALF]])
FORWARD_Y = np.stack(
    [
        [
            np.concatenate([t[ROW_OF[2 * h : 2 * h + 2, :, :, e].reshape(-1)] for t in (COS, _imag)])
            for h in range(2)
        ]
        for e in range(2)
    ]
)
_two = 2.0 * COS[:, :HALF].astype(np.float32)
_two[:, 0] = COS[:, 0]
_sin = -2.0 * SIN[:, :HALF].astype(np.float32)
_sin[:, 0] = COS[:, HALF]
BACK_Y = np.concatenate(
    [
        bf(t.reshape(GY, 8, 16, 2).transpose(3, 0, 2, 1).reshape(2, GY, 128))
        for t in (_two, _sin)
    ],
    axis=2,
)


def quarters(upper_left, upper_right, lower_left, lower_right):
    return np.concatenate(
        [
            np.concatenate([upper_left, upper_right], axis=1),
            np.concatenate([lower_left, lower_right], axis=1),
        ],
        axis=0,
    )


FORWARD_X = np.zeros((2, 2 * GX, 2 * GX), ml_dtypes.bfloat16)
BACK_X = np.zeros((2, 2, 2 * GX, GX), ml_dtypes.bfloat16)
_low = GX // 2
_pair = np.where(np.arange(_low) == 0, 1.0, 2.0)[:, None]
_in = -SIN[:, :_low]
_in[:, 0] = COS[:, _low]
_out_re = bf(COS[:_low].astype(np.float32) * _pair)
_out_im = bf(-SIN[:_low].astype(np.float32) * _pair)
_out_im[0] = COS[_low]
for _e in range(2):
    _half = slice(_e * _low, (_e + 1) * _low)
    _place = slice(_e * GX, (_e + 1) * GX)
    FORWARD_X[0, :, _place] = quarters(COS[:, _half], -SIN[:, _half], SIN[:, _half], COS[:, _half])
    FORWARD_X[1, _place, _place] = np.concatenate([COS[:, :_low], _in], axis=1)
    for _side in range(2):
        _to = slice(_side * _low, (_side + 1) * _low)
        _cos, _sine = COS[_half, _to], SIN[_half, _to]
        BACK_X[0, _side, _place] = quarters(_cos, _sine, -_sine, _cos)
        BACK_X[1, _side, _place, _half] = np.concatenate([_out_re[:, _to], _out_im[:, _to]])
_across = interpolation(GY, PIX)
_mirror = (-np.arange(GY)) % GY
ACROSS_X = np.zeros((4, 2, 2 * PIX, _low), np.float32)
EDGE_ACROSS = np.zeros((2, 2 * PIX, PIX), np.float32)
for _e in range(2):
    _half, _rows = slice(_e * _low, (_e + 1) * _low), slice(_e * PIX, (_e + 1) * PIX)
    ACROSS_X[_e, 0, :PIX] = _across[_half].T
    ACROSS_X[_e, 1, PIX:] = _across[_mirror][_half].T
    ACROSS_X[2 + _e, 0, _rows] = _across[:_low].T
    ACROSS_X[2 + _e, 1, _rows] = _across[_mirror][:_low].T
    EDGE_ACROSS[_e, _rows, 0] = _across[_low]
ACROSS_X, EDGE_ACROSS = bf(ACROSS_X), bf(EDGE_ACROSS)
_yh, _xx, _cc, _zz, _z4 = np.meshgrid(
    np.arange(2), np.arange(4), np.arange(2), np.arange(8), np.arange(4), indexing="ij"
)
Z_ORDER = (4 * (64 * _yh + 16 * _xx + 2 * _zz + _cc) + _z4).reshape(-1)
_yh, _yl, _xx, _cc, _zz, _p2 = np.meshgrid(
    np.arange(2), np.arange(2), np.arange(4), np.arange(2), np.arange(8), np.arange(2), indexing="ij"
)
K_ORDER = (4 * (64 * _yh + 16 * _xx + 2 * _zz + _cc) + 2 * _yl + _p2).reshape(-1)
FORWARD_Z = np.concatenate([t[K_ORDER][:, Z_ORDER] for t in (COS, SIN)], axis=1)
BACK_Z = np.concatenate([COS[:, K_ORDER], SIN[:, K_ORDER]], axis=1).reshape(2, 256, 2 * GZ)
MIRROR = bf(K_ORDER[None, :] == _mirror[K_ORDER][:, None])
WINDOWS = np.zeros((2, 2, 32, 2, 48), np.float32)
for _p in range(2):
    for _m in range(32):
        for _r in range(10):
            WINDOWS[:, _p, _m, 0, 20 * _p + _r] = max(0.0, 1.0 - abs(_m / 4 + 0.625 - _r))
            WINDOWS[:, _p, _m, 1, 20 * _p + 10 + _r] = max(0.0, 1.0 - abs(8.625 - _m / 4 - _r))
    WINDOWS[1, _p, 0, 1, :] = 0.0
    WINDOWS[1, _p, 0, 1, 40 + 2 * _p : 42 + 2 * _p] = (0.375, 0.625)
WINDOWS = bf(WINDOWS.reshape(2, 128, 48))

MESH = pl.DeviceIdType.MESH


def dot(first, second):
    return jnp.dot(first, second, preferred_element_type=jnp.float32)


def place():
    slab = lax.axis_index("slab")
    return (slab // 64) * 2 + lax.axis_index("img"), (slab // 16) % 4, (slab // 2) % 8, slab % 2


def device(y, x, z, c):
    return (y % 2, (y // 2) * 64 + x * 16 + z * 2 + c)


def greet(others):
    barrier = pltpu.get_barrier_semaphore()
    for other in others:
        pl.semaphore_signal(barrier, inc=1, device_id=other, device_id_type=MESH)
    return lambda: pl.semaphore_wait(barrier, len(others))


def across(y, k):
    return (y, y + 1 - 2 * (y % 2), (y + 2) % 4, 3 - y)[k]


class Exchange:
    def __init__(self, x_ref, a_ref, r_ref, sems):
        self.x_ref, self.a_ref, self.r_ref = x_ref, a_ref, r_ref
        self.local, self.z_send, self.z_recv, self.p_send, self.p_recv, self.own = sems
        self.y, self.x, self.z, self.c = place()
        self.within = self.c == self.y // 2

    def move(self, source, target, send, recv, where):
        return pltpu.make_async_remote_copy(
            src_ref=source,
            dst_ref=target,
            send_sem=send,
            recv_sem=recv,
            device_id=device(*where),
            device_id_type=MESH,
        )

    def start(self, part, k):
        row, index = self.row(k), part * self.parts + k
        for step in (4, 1, 7, 2, 6, 3, 5):
            depth = (self.z + step) % 8
            self.move(
                self.x_ref.at[part, row, :, depth],
                self.a_ref.at[part, row, :, self.z],
                self.z_send.at[index],
                self.z_recv.at[index],
                (self.y, self.x, depth, self.c),
            ).start()
        self.keep(part, k).start()

    def keep(self, part, k):
        row = self.row(k)
        return pltpu.make_async_copy(
            self.x_ref.at[part, row, :, self.z],
            self.a_ref.at[part, row, :, self.z],
            self.local.at[part * self.parts + k],
        )

    def whole(self, part, k):
        row, index = self.row(k), part * self.parts + k
        return self.move(
            self.x_ref.at[part, row, :, pl.ds(0, 7)],
            self.a_ref.at[part, row, :, pl.ds(0, 7)],
            self.z_send.at[index],
            self.z_recv.at[index],
            (self.y, self.x, (self.z + 1) % 8, self.c),
        )

    def spread(self, part, k):
        self.keep(part, k).wait()
        self.whole(part, k).wait_recv()
        for source, where, mine in self.targets(part, k):
            target = self.r_ref.at[part, self.slot()]
            copy = self.move(source, target, self.p_send, self.p_recv.at[part], where)
            if mine:
                pl.when(self.within)(pltpu.make_async_copy(source, target, self.own.at[part]).start)
                pl.when(jnp.logical_not(self.within))(copy.start)
            else:
                copy.start()

    def blocks(self, part, count):
        piece = self.r_ref.at[part, pl.ds(0, count)]
        where = (self.y, self.x, (self.z + 1) % 8, self.c)
        return self.move(piece, piece, self.p_send, self.p_recv.at[part], where)

    def arrived(self, part):
        @pl.when(self.within)
        def _():
            source = self.r_ref.at[part, 0]
            pltpu.make_async_copy(source, self.r_ref.at[part, self.slot()], self.own.at[part]).wait()
            self.blocks(part, 15).wait_recv()

        @pl.when(jnp.logical_not(self.within))
        def _():
            self.blocks(part, 16).wait_recv()

    def finish(self):
        for part in range(2):
            for k in range(self.parts):
                self.whole(part, k).wait_send()

            @pl.when(self.within)
            def _():
                self.blocks(part, 15).wait_send()

            @pl.when(jnp.logical_not(self.within))
            def _():
                self.blocks(part, 16).wait_send()


class Forward(Exchange):
    parts = 4

    def row(self, k):
        return across(self.y, k)

    def slot(self):
        return (self.y % 2 * 4 + self.x) * 2 + self.c

    def targets(self, part, k):
        row = self.row(k)
        for dx in (2, 1, 3, 0):
            column = (self.x + dx) % 4
            where = (row, column, self.z, self.y // 2)
            yield self.a_ref.at[part, row, column], where, k == 0 and dx == 0


class Back(Exchange):
    parts = 2

    def row(self, k):
        return (self.y + k) % 2

    def slot(self):
        return self.y * 4 + self.x

    def targets(self, part, k):
        row = self.row(k)
        for dx in (2, 1, 3, 0):
            for dc in (0, 1):
                column, core = (self.x + dx) % 4, (self.c + dc) % 2
                where = (2 * self.c + row, column, self.z, core)
                yield self.a_ref.at[part, row, column, :, core], where, (k, dx, dc) == (0, 0, 0)


def exchange_sems(parts):
    one = pltpu.SemaphoreType.DMA
    return [one((2 * parts,)), one((2 * parts,)), one((2 * parts,)), one, one((2,)), one((2,))]


FORWARD_TILES = (2, 4, 4, 8, 16, 128)
BACK_TILES = (2, 2, 4, 8, 2, 16, 128)
LANDED_TILES = (2, 16, 8, 16, 128)
ORDER = (2, 3, 1, 0)


def partners():
    y, x, z, c = place()
    return [device(y, x, (z + d) % 8, c) for d in range(1, 8)] + [
        device((y + d // 8) % 4, (x + d // 2 % 4) % 4, z, (c + d) % 2) for d in range(1, 32)
    ]


TABLES = (
    FORWARD_Y, WINDOWS, FORWARD_X, FORWARD_Z, MIRROR, ACROSS_X, EDGE_ACROSS, BACK_Z, BACK_X, BACK_Y,
)
BY_SET, BY_SET_AND_CORE, BY_CORE = (2, 8), (5,), (6,)


def held_shape(index, table):
    if index in BY_SET + BY_SET_AND_CORE:
        return (2,) + table.shape[1:]
    return table.shape[1:] if index in BY_CORE else table.shape


def step_kernel(scale, orient_in, sharp_in, density_in, images, support_in, *rest):
    count = len(TABLES)
    sources, out_ref, rest = rest[:count], rest[count], rest[count + 1 :]
    tables, rest = rest[:count], rest[count:]
    (
        orient, sharp, density, r_ref, e_ref,
        x_ref, a_ref, stage, held, sent, got, padded, g_ref, h_ref, made, whole_rows,
        x_back, a_back, r_back, wide, lines, halves, landed, spectrum, edges, amplitude, amplitude_edge,
        projected, projected_edge, half_out, half_in, final,
        support, d_load, t_load, load, o_send, c_send, c_recv, g_send, g_recv, g_own, e_send, e_recv, e_own,
        x_send, x_recv, *sems,
    ) = rest
    (
        table, windows, forward_x, forward_z, mirror, across_x, edge_across, back_z, back_x_table, back_y,
    ) = tables
    y, x, z, c = place()
    image = lax.axis_index("img")
    slab = lax.axis_index("slab")
    m = (y * 4 + x) * 2 + c
    special = jnp.where(slab // 2 + image == 0, 1, 0)
    both_real = special == 1

    def beside(shift, turn):
        return ((image + turn) % 2, (slab + shift + 128) % 128)

    moves = [(shift, turn) for shift in (-1, 0, 1) for turn in (0, 1) if (shift, turn) != (0, 0)]
    entered = greet(partners() + [beside(*move) for move in moves])
    fills = []

    def fill(source, target):
        fills.append(pltpu.make_async_copy(source, target, t_load.at[len(fills)]))

    for index, (source, target) in enumerate(zip(sources, tables)):
        if index in BY_SET:
            fill(source.at[special], target.at[0])
            fill(source.at[0], target.at[1])
        elif index in BY_SET_AND_CORE:
            fill(source.at[special * 2 + c], target.at[0])
            fill(source.at[c], target.at[1])
        else:
            fill(source.at[c] if index in BY_CORE else source, target)
    first_fills = [
        fills[0],
        pltpu.make_async_copy(density_in, density, d_load.at[0]),
        pltpu.make_async_copy(orient_in, orient, d_load.at[1]),
        pltpu.make_async_copy(sharp_in, sharp, d_load.at[2]),
    ]
    fetch = pltpu.make_async_copy(images, held, load)
    for fill in first_fills:
        fill.start()
    fetch.start()
    fills.append(pltpu.make_async_copy(support_in, support, d_load.at[3]))
    for fill in fills[1:]:
        fill.start()
    forward = Forward(x_ref, a_ref, r_ref, sems[:6])
    back = Back(x_back, a_back, r_back, sems[6:])
    for fill in first_fills:
        fill.wait()

    def transform(part, half):
        for plane in range(4):
            out = dot(table[part, half], density[plane])
            for piece in range(2):
                for side in range(2):
                    stage[pl.ds(plane * 4 + piece * 2 + side, 64, stride=16), :] = out[
                        piece * 64 : piece * 64 + 64, side * 128 : side * 128 + 128
                    ]
        x_ref[part, pl.ds(half * 2, 2)] = stage[...].astype(jnp.bfloat16).reshape(2, 4, 8, 16, 128)

    other_half, own_half = 1 - y // 2, y // 2
    transform(0, other_half)
    entered()
    forward.start(0, 2)

    near = orient[...] - slab * 4
    steps = lax.broadcasted_iota(jnp.int32, (16, 64), 0) - 4 - near
    squares = (steps * steps).astype(jnp.float32)
    raw = jnp.exp(-sharp[...] * squares)
    total = 1.0 + 2.0 * (
        jnp.exp(-sharp[...])
        + jnp.exp(-4.0 * sharp[...])
        + jnp.exp(-9.0 * sharp[...])
        + jnp.exp(-16.0 * sharp[...])
    )
    mixing = jnp.where(jnp.abs(steps) <= 4, raw / total, 0.0)
    high = mixing.astype(jnp.bfloat16)
    low = (mixing - high.astype(jnp.float32)).astype(jnp.bfloat16)
    def iota(shape, axis):
        return lax.broadcasted_iota(jnp.int32, shape, axis)

    def within(at, group):
        return jnp.where(jnp.logical_and(at >= group * 8, at < group * 8 + 8), 1.0, 0.0).astype(
            jnp.bfloat16
        )

    by_plane = within(iota((96, 16), 0), iota((96, 16), 1))
    by_snapshot = within(iota((64, 512), 1), iota((64, 512), 0))
    agree = (iota((96, 512), 0) & 7) == (iota((96, 512), 1) & 7)

    def widened(part):
        rows = dot(by_plane, part).astype(jnp.bfloat16)
        return jnp.where(agree, dot(rows, by_snapshot), 0.0).astype(jnp.bfloat16)

    wide_high = widened(high)
    wide_both = jnp.concatenate([wide_high, widened(low)], axis=0)
    fetch.wait()

    def mix(index, carry):
        at = pl.multiple_of(index * 16, 16)
        rows = jnp.concatenate(
            [held[:, pl.ds(at + 8 * block, 8), :].reshape(512, 128) for block in range(2)], axis=1
        )
        upper = rows.astype(jnp.bfloat16)
        lower = (rows - upper.astype(jnp.float32)).astype(jnp.bfloat16)
        out = dot(wide_both, upper)
        out = out[:96] + out[96:] + dot(wide_high, lower)
        for plane in range(12):
            own = out[plane * 8 : plane * 8 + 8]
            sent[plane, pl.ds(at, 16), :] = jnp.concatenate(
                [own[:, :128], own[:, 128:]], axis=0
            ).astype(jnp.bfloat16)
        return carry

    lax.fori_loop(0, 8, mix, 0, unroll=4)

    def gift(index, shift, turn):
        first = 4 + 4 * shift + 2 * ((image + turn) % 2)
        return pltpu.make_async_remote_copy(
            src_ref=sent.at[pl.ds(first, 2)],
            dst_ref=got.at[index],
            send_sem=c_send.at[index],
            recv_sem=c_recv.at[index],
            device_id=beside(shift, turn),
            device_id_type=MESH,
        )

    gifts = [gift(index, *move) for index, move in enumerate(moves)]
    for copy in gifts:
        copy.start()
    forward.start(0, 3)
    transform(0, own_half)
    forward.start(0, 1)
    transform(1, other_half)
    forward.spread(0, 2)
    for copy in gifts:
        copy.wait()
    padded[...] = jnp.zeros_like(padded)
    for plane in range(2):
        own = sent[4 + 2 * image + plane].astype(jnp.float32)
        for index, (shift, turn) in enumerate(moves):
            piece = got[index, plane].astype(jnp.float32)
            if shift:
                source = slab - shift
                piece = jnp.where(jnp.logical_and(source >= 0, source < 128), piece, 0.0)
            own = own + piece
        padded[plane, pl.ds(16, 128), :] = own
    for depth in range(8):
        rows = [
            padded[plane, pl.ds(16 + first, 10), :]
            for plane in range(2)
            for first in (8 * depth - 1, 119 - 8 * depth)
        ]
        rows += [padded[plane, pl.ds(16 + 63, 2), :] for plane in range(2)]
        rows.append(jnp.zeros((4, PIX), jnp.float32))
        g_ref[depth] = jnp.concatenate(rows, axis=0).astype(jnp.bfloat16)

    def window(step):
        depth = (z + step) % 8
        return pltpu.make_async_remote_copy(
            src_ref=g_ref.at[depth],
            dst_ref=h_ref.at[z],
            send_sem=g_send,
            recv_sem=g_recv,
            device_id=device(y, x, depth, c),
            device_id_type=MESH,
        )

    for step in (4, 1, 7, 2, 6, 3, 5):
        window(step).start()
    stay = pltpu.make_async_copy(g_ref.at[z], h_ref.at[z], g_own)
    stay.start()
    forward.start(0, 0)
    transform(1, own_half)
    forward.spread(0, 3)
    forward.start(1, 2)
    for fill in fills[1:]:
        fill.wait()
    forward.spread(0, 1)
    forward.start(1, 3)
    stay.wait()
    seven = pltpu.make_async_remote_copy(
        src_ref=g_ref.at[pl.ds(0, 7)],
        dst_ref=h_ref.at[pl.ds(0, 7)],
        send_sem=g_send,
        recv_sem=g_recv,
        device_id=device(y, x, (z + 1) % 8, c),
        device_id_type=MESH,
    )
    seven.wait_send()
    seven.wait_recv()
    weights = windows[jnp.where(z == 0, 1, 0)]
    out = dot(weights, jnp.concatenate([h_ref[source] for source in range(8)], axis=1))
    for source in range(8):
        for plane in range(2):
            made[pl.ds(source * 2 + plane, 64, stride=16), :] = out[
                plane * 64 : plane * 64 + 64, source * 128 : source * 128 + 128
            ]
    whole_rows[...] = made[...].astype(jnp.bfloat16).reshape(16, 2, 2, 16, 128)

    def kept(part):
        return pltpu.make_async_copy(whole_rows.at[y * 4 + x, part], e_ref.at[part, m], e_own.at[part])

    def others(part):
        piece = e_ref.at[part, pl.ds(0, 31)]
        return pltpu.make_async_remote_copy(
            src_ref=piece,
            dst_ref=piece,
            send_sem=e_send.at[part],
            recv_sem=e_recv.at[part],
            device_id=device(y, x, (z + 1) % 8, c),
            device_id_type=MESH,
        )

    for part in range(2):
        for d in range(1, 32):
            row, column, core = (y + d // 8) % 4, (x + d // 2 % 4) % 4, (c + d) % 2
            pltpu.make_async_remote_copy(
                src_ref=whole_rows.at[row * 4 + column, part],
                dst_ref=e_ref.at[part, m],
                send_sem=e_send.at[part],
                recv_sem=e_recv.at[part],
                device_id=device(row, column, z, core),
                device_id_type=MESH,
            ).start()
        kept(part).start()
    forward.spread(0, 0)
    for k in (1, 0):
        forward.start(1, k)

    def cross(index, source, target):
        return pltpu.make_async_remote_copy(
            src_ref=source,
            dst_ref=target,
            send_sem=x_send.at[index],
            recv_sem=x_recv.at[index],
            device_id=device(y, x, z, 1 - c),
            device_id_type=MESH,
        )

    def cross_forward(part):
        return cross(part, halves.at[part, 1 - c], landed.at[part, c])

    def cross_back(part):
        return cross(2 + part, half_out.at[part], half_in.at[part, c])

    def along_x(part):
        forward.arrived(part)
        wide[...] = r_ref[part].astype(jnp.float32).reshape(2048, 128)
        for piece in range(2):
            for side in range(2):
                for block in range(2):
                    at = piece * 512 + side * 256 + block * 128
                    lines[:, pl.ds(at, 128)] = wide[
                        pl.ds(side * 1024 + piece * 2 + block, 256, stride=4), :
                    ].astype(jnp.bfloat16)
        both = dot(lines[...], forward_x[part]).astype(jnp.bfloat16)
        for half in range(2):
            halves[part, half] = both[:, half * GX : half * GX + GX]
        cross_forward(part).start()
        landed[part, c] = halves[part, c]

    def rounded_root(rows, across_table):
        return jnp.sqrt(scale * dot(rows, across_table)).astype(jnp.bfloat16).astype(jnp.float32)

    def amplitudes(part):
        kept(part).wait()
        others(part).wait_send()
        others(part).wait_recv()
        near = jnp.concatenate([e_ref[part, :, row].reshape(GZ, PIX) for row in range(2)], axis=1)
        far = dot(mirror[...], near).astype(jnp.bfloat16)
        amplitude[part] = 0.5 * (
            rounded_root(near, across_x[part, 0]) + rounded_root(far, across_x[part, 1])
        )
        if part == 0:

            @pl.when(both_real)
            def _():
                amplitude_edge[...] = 0.5 * (
                    rounded_root(near, edge_across[...]) + rounded_root(far, edge_across[...])
                )

    def projection(real_z, imag_z, target):
        inverse = lax.rsqrt(real_z * real_z + imag_z * imag_z)
        factor = target * jnp.minimum(inverse, 1.0 / least_modulus)
        return (real_z * factor).astype(jnp.bfloat16), (imag_z * factor).astype(jnp.bfloat16)

    def along_z(part):
        cross_forward(part).wait()
        half_x = GX // 2
        for half in range(2):
            top = pl.ds(half * 256, 256)
            low = pl.ds(GZ + half * 256, 256)
            spectrum[top, :] = landed[part, half]
            if part == 0:

                @pl.when(both_real)
                def _():
                    at = pl.ds(half_x, 128)
                    first_lane = lax.broadcasted_iota(jnp.int32, (256, 128), 1) == 0
                    mixed = spectrum[top, at].astype(jnp.float32)
                    edge = jnp.where(first_lane, mixed, 0.0)
                    spectrum[top, at] = (mixed - edge).astype(jnp.bfloat16)
                    zero = jnp.zeros((256, 128), jnp.bfloat16)
                    edges[top, :] = jnp.concatenate([edge.astype(jnp.bfloat16), zero], axis=1)
                    edges[low, :] = jnp.concatenate([zero, (-edge).astype(jnp.bfloat16)], axis=1)

            spectrum[low, pl.ds(0, half_x)] = spectrum[top, pl.ds(half_x, half_x)]
            spectrum[low, pl.ds(half_x, half_x)] = -spectrum[top, pl.ds(0, half_x)]

        def block_of_planes(block, carry):
            at = pl.ds(pl.multiple_of(block * 128, 128), 128)
            low = pl.ds(pl.multiple_of(GZ + block * 128, 128), 128)
            weights = forward_z[at, :]
            total = dot(weights, spectrum[...])
            real, imag = projection(total[:, :half_x], total[:, half_x:], amplitude[part, at, :])
            projected[at, pl.ds(0, half_x)] = real
            projected[at, pl.ds(half_x, half_x)] = imag
            projected[low, pl.ds(0, half_x)] = -imag
            projected[low, pl.ds(half_x, half_x)] = real
            if part == 0:

                @pl.when(both_real)
                def _():
                    total = dot(weights, edges[...])
                    real, imag = projection(total[:, :128], total[:, 128:], amplitude_edge[at, :])
                    projected_edge[at, :] = real
                    projected_edge[low, :] = -imag

            return carry

        lax.fori_loop(0, 4, block_of_planes, 0)

        def inverse(half, target):
            target[...] = dot(back_z[half], projected[...]).astype(jnp.bfloat16)
            if part == 0:

                @pl.when(both_real)
                def _():
                    first_lane = lax.broadcasted_iota(jnp.int32, (256, 128), 1) == 0
                    edge = dot(back_z[half], projected_edge[...])
                    at = pl.ds(half_x, 128)
                    target[:, at] = jnp.where(
                        first_lane, edge, target[:, at].astype(jnp.float32)
                    ).astype(jnp.bfloat16)

        inverse(1 - c, half_out.at[part])
        cross_back(part).start()
        inverse(c, half_in.at[part, c])

    def back_x(part):
        cross_back(part).wait()
        for half in range(2):
            lines[:, pl.ds(half * GX, GX)] = half_in[part, half]
        for k in (1, 0):
            row = (y + k) % 2
            out = dot(lines[...], back_x_table[part, row])
            for block in range(4):
                stage[pl.ds(block, 256, stride=4), :] = out[:, block * 128 : block * 128 + 128]
            x_back[part, row] = stage[...].astype(jnp.bfloat16).reshape(4, 8, 2, 16, 128)
            back.start(part, k)

    def along_y(part):
        back.arrived(part)
        wide[...] = r_back[part].astype(jnp.float32).reshape(2048, 128)
        for plane in range(4):
            rows = [
                jnp.concatenate(
                    [
                        wide[pl.ds(plane * 4 + piece * 2 + side, 128, stride=16), :]
                        for side in range(2)
                    ],
                    axis=1,
                ).astype(jnp.bfloat16)
                for piece in range(2)
            ]
            out = dot(back_y[part], jnp.concatenate(rows, axis=0))
            if part:
                out = final[plane] + out
                previous = density[plane].astype(jnp.float32)
                final[plane] = jnp.where(support[plane] == 1, out, previous - feedback * out)
                pltpu.make_async_copy(final.at[plane], out_ref.at[plane], o_send.at[plane]).start()
            else:
                final[plane] = out

    amplitudes(0)
    along_x(0)
    forward.spread(1, 2)
    along_z(0)
    forward.spread(1, 3)
    forward.spread(1, 1)
    back_x(0)
    amplitudes(1)
    forward.spread(1, 0)
    along_x(1)
    along_z(1)
    back_x(1)
    back.spread(0, 1)
    back.spread(0, 0)
    along_y(0)
    back.spread(1, 1)
    back.spread(1, 0)
    along_y(1)
    forward.finish()
    back.finish()
    for plane in range(4):
        pltpu.make_async_copy(final.at[plane], out_ref.at[plane], o_send.at[plane]).wait()


def exchange_step(scale, density, orient, sharp, images, support):
    far = pl.BlockSpec(memory_space=pltpu.HBM)
    bfloat, single = jnp.bfloat16, jnp.float32
    one = pltpu.SemaphoreType.DMA
    buffers = [
        ((1, 64), jnp.int32),
        ((1, 64), single),
        (density.shape, bfloat),
        (LANDED_TILES, bfloat),
        ((2, 32, 2, 16, 128), bfloat),
        (FORWARD_TILES, bfloat),
        (FORWARD_TILES, bfloat),
        ((1024, 128), single),
        ((64, 128, 128), single),
        ((12, 128, 128), bfloat),
        ((5, 2, 128, 128), bfloat),
        ((2, 160, 128), single),
        ((8, 48, 128), bfloat),
        ((8, 48, 128), bfloat),
        ((1024, 128), single),
        ((16, 2, 2, 16, 128), bfloat),
        (BACK_TILES, bfloat),
        (BACK_TILES, bfloat),
        (LANDED_TILES, bfloat),
        ((2048, 128), single),
        ((256, 2 * GX), bfloat),
        ((2, 2, 256, GX), bfloat),
        ((2, 2, 256, GX), bfloat),
        ((2 * GZ, GX), bfloat),
        ((2 * GZ, 256), bfloat),
        ((2, GZ, GX // 2), single),
        ((GZ, 128), single),
        ((2 * GZ, GX), bfloat),
        ((2 * GZ, 128), bfloat),
        ((2, 256, GX), bfloat),
        ((2, 2, 256, GX), bfloat),
        (density.shape, single),
        (density.shape, jnp.int32),
    ]
    fill_count = len(TABLES) + len(BY_SET + BY_SET_AND_CORE)
    return pl.pallas_call(
        functools.partial(step_kernel, scale),
        out_shape=jax.ShapeDtypeStruct(density.shape, single),
        in_specs=[far] * (5 + len(TABLES)),
        out_specs=far,
        scratch_shapes=[pltpu.VMEM(held_shape(i, t), bfloat) for i, t in enumerate(TABLES)]
        + [pltpu.VMEM(*buffer) for buffer in buffers]
        + [one((4,)), one((fill_count,)), one, one((4,)), one((5,)), one((5,)), one, one, one, one((2,)), one((2,)), one((2,))]
        + [one((4,)), one((4,))]
        + exchange_sems(4)
        + exchange_sems(2),
        compiler_params=pltpu.CompilerParams(
            collective_id=1, has_side_effects=True, vmem_limit_bytes=63 << 20
        ),
    )(
        orient.reshape(1, -1),
        sharp.reshape(1, -1),
        density,
        images,
        support,
        *TABLES,
    )


def body(images, orient, sharp, density, support):
    depth = density.shape[0]
    scale = depth / (images.shape[0] * lax.axis_size("img"))
    return exchange_step(scale, density, orient, sharp, images, support)


def solution(mesh):
    placed = (
        P(("img", "slab"), None, None),
        P(("img", "slab")),
        P(("img", "slab")),
        P("slab", None, "img"),
        P("slab", None, "img"),
    )
    return jax.shard_map(
        body, mesh=mesh, in_specs=placed, out_specs=P("slab", None, "img"), check_vma=False
    )
```

```python
import functools
import math

import jax
import jax.numpy as jnp
import ml_dtypes
import numpy as np
from jax import lax
from jax.experimental import pallas as pl
from jax.experimental.pallas import tpu as pltpu
from jax.sharding import PartitionSpec as P

GZ = 512
GY = 512
GX = 512
PIX = 128

least_modulus = 0.5
feedback = 0.9


def dft_tables(length):
    index = np.arange(length, dtype=np.int64)
    product = (index[:, None] * index[None, :]) % length
    angles = product.astype(np.float32) * np.float32(2.0 * math.pi / length)
    factor = np.float32(1.0 / math.sqrt(length))
    return (
        (np.cos(angles) * factor).astype(ml_dtypes.bfloat16),
        (np.sin(angles) * factor).astype(ml_dtypes.bfloat16),
    )


def interpolation(cells, pixels):
    grid = np.arange(cells, dtype=np.float32)
    detector = np.arange(pixels, dtype=np.float32)
    position = (grid + np.float32(0.5)) * np.float32(pixels / cells) - np.float32(0.5)
    return np.maximum(
        np.float32(0.0), np.float32(1.0) - np.abs(position[:, None] - detector[None, :])
    )


def bf(table):
    return np.asarray(table).astype(ml_dtypes.bfloat16)


COS, SIN = dft_tables(GY)
HALF = GY // 2
_y, _x, _z, _s = np.meshgrid(np.arange(4), np.arange(4), np.arange(8), np.arange(2), indexing="ij")
ROW_OF = 32 * _z + 8 * _y + 2 * _x + _s
_imag = np.concatenate([COS[HALF : HALF + 1], -SIN[1:HALF]])
FORWARD_Y = np.stack(
    [
        [
            np.concatenate([t[ROW_OF[2 * h : 2 * h + 2, :, :, e].reshape(-1)] for t in (COS, _imag)])
            for h in range(2)
        ]
        for e in range(2)
    ]
)
_two = 2.0 * COS[:, :HALF].astype(np.float32)
_two[:, 0] = COS[:, 0]
_sin = -2.0 * SIN[:, :HALF].astype(np.float32)
_sin[:, 0] = COS[:, HALF]
BACK_Y = np.concatenate(
    [
        bf(t.reshape(GY, 8, 16, 2).transpose(3, 0, 2, 1).reshape(2, GY, 128))
        for t in (_two, _sin)
    ],
    axis=2,
)


def quarters(upper_left, upper_right, lower_left, lower_right):
    return np.concatenate(
        [
            np.concatenate([upper_left, upper_right], axis=1),
            np.concatenate([lower_left, lower_right], axis=1),
        ],
        axis=0,
    )


FORWARD_X = np.zeros((2, 2 * GX, 2 * GX), ml_dtypes.bfloat16)
BACK_X = np.zeros((2, 2, 2 * GX, GX), ml_dtypes.bfloat16)
_low = GX // 2
_pair = np.where(np.arange(_low) == 0, 1.0, 2.0)[:, None]
_in = -SIN[:, :_low]
_in[:, 0] = COS[:, _low]
_out_re = bf(COS[:_low].astype(np.float32) * _pair)
_out_im = bf(-SIN[:_low].astype(np.float32) * _pair)
_out_im[0] = COS[_low]
for _e in range(2):
    _half = slice(_e * _low, (_e + 1) * _low)
    _place = slice(_e * GX, (_e + 1) * GX)
    FORWARD_X[0, :, _place] = quarters(COS[:, _half], -SIN[:, _half], SIN[:, _half], COS[:, _half])
    FORWARD_X[1, _place, _place] = np.concatenate([COS[:, :_low], _in], axis=1)
    for _side in range(2):
        _to = slice(_side * _low, (_side + 1) * _low)
        _cos, _sine = COS[_half, _to], SIN[_half, _to]
        BACK_X[0, _side, _place] = quarters(_cos, _sine, -_sine, _cos)
        BACK_X[1, _side, _place, _half] = np.concatenate([_out_re[:, _to], _out_im[:, _to]])
_across = interpolation(GY, PIX)
_mirror = (-np.arange(GY)) % GY
ACROSS_X = np.zeros((4, 2, 2 * PIX, _low), np.float32)
EDGE_ACROSS = np.zeros((2, 2 * PIX, PIX), np.float32)
for _e in range(2):
    _half, _rows = slice(_e * _low, (_e + 1) * _low), slice(_e * PIX, (_e + 1) * PIX)
    ACROSS_X[_e, 0, :PIX] = _across[_half].T
    ACROSS_X[_e, 1, PIX:] = _across[_mirror][_half].T
    ACROSS_X[2 + _e, 0, _rows] = _across[:_low].T
    ACROSS_X[2 + _e, 1, _rows] = _across[_mirror][:_low].T
    EDGE_ACROSS[_e, _rows, 0] = _across[_low]
ACROSS_X, EDGE_ACROSS = bf(ACROSS_X), bf(EDGE_ACROSS)
_yh, _xx, _cc, _zz, _z4 = np.meshgrid(
    np.arange(2), np.arange(4), np.arange(2), np.arange(8), np.arange(4), indexing="ij"
)
Z_ORDER = (4 * (64 * _yh + 16 * _xx + 2 * _zz + _cc) + _z4).reshape(-1)
_yh, _yl, _xx, _cc, _zz, _p2 = np.meshgrid(
    np.arange(2), np.arange(2), np.arange(4), np.arange(2), np.arange(8), np.arange(2), indexing="ij"
)
K_ORDER = (4 * (64 * _yh + 16 * _xx + 2 * _zz + _cc) + 2 * _yl + _p2).reshape(-1)
FORWARD_Z = np.concatenate([t[K_ORDER][:, Z_ORDER] for t in (COS, SIN)], axis=1)
BACK_Z = np.concatenate([COS[:, K_ORDER], SIN[:, K_ORDER]], axis=1).reshape(2, 256, 2 * GZ)
MIRROR = bf(K_ORDER[None, :] == _mirror[K_ORDER][:, None])
WINDOWS = np.zeros((2, 2, 32, 2, 48), np.float32)
for _p in range(2):
    for _m in range(32):
        for _r in range(10):
            WINDOWS[:, _p, _m, 0, 20 * _p + _r] = max(0.0, 1.0 - abs(_m / 4 + 0.625 - _r))
            WINDOWS[:, _p, _m, 1, 20 * _p + 10 + _r] = max(0.0, 1.0 - abs(8.625 - _m / 4 - _r))
    WINDOWS[1, _p, 0, 1, :] = 0.0
    WINDOWS[1, _p, 0, 1, 40 + 2 * _p : 42 + 2 * _p] = (0.375, 0.625)
WINDOWS = bf(WINDOWS.reshape(2, 128, 48))

MESH = pl.DeviceIdType.MESH


def dot(first, second):
    return jnp.dot(first, second, preferred_element_type=jnp.float32)


def place():
    slab = lax.axis_index("slab")
    return (slab // 64) * 2 + lax.axis_index("img"), (slab // 16) % 4, (slab // 2) % 8, slab % 2


def device(y, x, z, c):
    return (y % 2, (y // 2) * 64 + x * 16 + z * 2 + c)


def greet(others):
    barrier = pltpu.get_barrier_semaphore()
    for other in others:
        pl.semaphore_signal(barrier, inc=1, device_id=other, device_id_type=MESH)
    return lambda: pl.semaphore_wait(barrier, len(others))


def across(y, k):
    return (y, y + 1 - 2 * (y % 2), (y + 2) % 4, 3 - y)[k]


class Exchange:
    def __init__(self, x_ref, a_ref, r_ref, sems):
        self.x_ref, self.a_ref, self.r_ref = x_ref, a_ref, r_ref
        self.local, self.z_send, self.z_recv, self.p_send, self.p_recv, self.own = sems
        self.y, self.x, self.z, self.c = place()
        self.within = self.c == self.y // 2

    def move(self, source, target, send, recv, where):
        return pltpu.make_async_remote_copy(
            src_ref=source,
            dst_ref=target,
            send_sem=send,
            recv_sem=recv,
            device_id=device(*where),
            device_id_type=MESH,
        )

    def start(self, part, k):
        row, index = self.row(k), part * self.parts + k
        for step in (4, 1, 7, 2, 6, 3, 5):
            depth = (self.z + step) % 8
            self.move(
                self.x_ref.at[part, row, :, depth],
                self.a_ref.at[part, row, :, self.z],
                self.z_send.at[index],
                self.z_recv.at[index],
                (self.y, self.x, depth, self.c),
            ).start()
        self.keep(part, k).start()

    def keep(self, part, k):
        row = self.row(k)
        return pltpu.make_async_copy(
            self.x_ref.at[part, row, :, self.z],
            self.a_ref.at[part, row, :, self.z],
            self.local.at[part * self.parts + k],
        )

    def whole(self, part, k):
        row, index = self.row(k), part * self.parts + k
        return self.move(
            self.x_ref.at[part, row, :, pl.ds(0, 7)],
            self.a_ref.at[part, row, :, pl.ds(0, 7)],
            self.z_send.at[index],
            self.z_recv.at[index],
            (self.y, self.x, (self.z + 1) % 8, self.c),
        )

    def spread(self, part, k):
        self.keep(part, k).wait()
        self.whole(part, k).wait_recv()
        for source, where, mine in self.targets(part, k):
            target = self.r_ref.at[part, self.slot()]
            copy = self.move(source, target, self.p_send, self.p_recv.at[part], where)
            if mine:
                pl.when(self.within)(pltpu.make_async_copy(source, target, self.own.at[part]).start)
                pl.when(jnp.logical_not(self.within))(copy.start)
            else:
                copy.start()

    def blocks(self, part, count):
        piece = self.r_ref.at[part, pl.ds(0, count)]
        where = (self.y, self.x, (self.z + 1) % 8, self.c)
        return self.move(piece, piece, self.p_send, self.p_recv.at[part], where)

    def arrived(self, part):
        @pl.when(self.within)
        def _():
            source = self.r_ref.at[part, 0]
            pltpu.make_async_copy(source, self.r_ref.at[part, self.slot()], self.own.at[part]).wait()
            self.blocks(part, 15).wait_recv()

        @pl.when(jnp.logical_not(self.within))
        def _():
            self.blocks(part, 16).wait_recv()

    def finish(self):
        for part in range(2):
            for k in range(self.parts):
                self.whole(part, k).wait_send()

            @pl.when(self.within)
            def _():
                self.blocks(part, 15).wait_send()

            @pl.when(jnp.logical_not(self.within))
            def _():
                self.blocks(part, 16).wait_send()


class Forward(Exchange):
    parts = 4

    def row(self, k):
        return across(self.y, k)

    def slot(self):
        return (self.y % 2 * 4 + self.x) * 2 + self.c

    def targets(self, part, k):
        row = self.row(k)
        for dx in (2, 1, 3, 0):
            column = (self.x + dx) % 4
            where = (row, column, self.z, self.y // 2)
            yield self.a_ref.at[part, row, column], where, k == 0 and dx == 0


class Back(Exchange):
    parts = 2

    def row(self, k):
        return (self.y + k) % 2

    def slot(self):
        return self.y * 4 + self.x

    def targets(self, part, k):
        row = self.row(k)
        for dx in (2, 1, 3, 0):
            for dc in (0, 1):
                column, core = (self.x + dx) % 4, (self.c + dc) % 2
                where = (2 * self.c + row, column, self.z, core)
                yield self.a_ref.at[part, row, column, :, core], where, (k, dx, dc) == (0, 0, 0)


def exchange_sems(parts):
    one = pltpu.SemaphoreType.DMA
    return [one((2 * parts,)), one((2 * parts,)), one((2 * parts,)), one, one((2,)), one((2,))]


FORWARD_TILES = (2, 4, 4, 8, 16, 128)
BACK_TILES = (2, 2, 4, 8, 2, 16, 128)
LANDED_TILES = (2, 16, 8, 16, 128)
ORDER = (2, 3, 1, 0)


def partners():
    y, x, z, c = place()
    return [device(y, x, (z + d) % 8, c) for d in range(1, 8)] + [
        device((y + d // 8) % 4, (x + d // 2 % 4) % 4, z, (c + d) % 2) for d in range(1, 32)
    ]


TABLES = (
    FORWARD_Y, WINDOWS, FORWARD_X, FORWARD_Z, MIRROR, ACROSS_X, EDGE_ACROSS, BACK_Z, BACK_X, BACK_Y,
)
BY_SET, BY_SET_AND_CORE, BY_CORE = (2, 8), (5,), (6,)


def held_shape(index, table):
    if index in BY_SET + BY_SET_AND_CORE:
        return (2,) + table.shape[1:]
    return table.shape[1:] if index in BY_CORE else table.shape


def step_kernel(scale, orient_in, sharp_in, density_in, images, support_in, *rest):
    count = len(TABLES)
    sources, out_ref, rest = rest[:count], rest[count], rest[count + 1 :]
    tables, rest = rest[:count], rest[count:]
    (
        orient, sharp, density, r_ref, e_ref,
        x_ref, a_ref, stage, held, sent, got, padded, g_ref, h_ref, made, whole_rows,
        x_back, a_back, r_back, wide, lines, halves, landed, spectrum, edges, amplitude, amplitude_edge,
        depth_sum, edge_sum,
        projected, projected_edge, half_out, half_in, final,
        support, d_load, t_load, load, o_send, c_send, c_recv, g_send, g_recv, g_own, e_send, e_recv, e_own,
        x_send, x_recv, *sems,
    ) = rest
    (
        table, windows, forward_x, forward_z, mirror, across_x, edge_across, back_z, back_x_table, back_y,
    ) = tables
    y, x, z, c = place()
    image = lax.axis_index("img")
    slab = lax.axis_index("slab")
    m = (y * 4 + x) * 2 + c
    special = jnp.where(slab // 2 + image == 0, 1, 0)
    both_real = special == 1

    def beside(shift, turn):
        return ((image + turn) % 2, (slab + shift + 128) % 128)

    moves = [(shift, turn) for shift in (-1, 0, 1) for turn in (0, 1) if (shift, turn) != (0, 0)]
    entered = greet(partners() + [beside(*move) for move in moves])
    fills = []

    def fill(source, target):
        fills.append(pltpu.make_async_copy(source, target, t_load.at[len(fills)]))

    for index, (source, target) in enumerate(zip(sources, tables)):
        if index in BY_SET:
            fill(source.at[special], target.at[0])
            fill(source.at[0], target.at[1])
        elif index in BY_SET_AND_CORE:
            fill(source.at[special * 2 + c], target.at[0])
            fill(source.at[c], target.at[1])
        else:
            fill(source.at[c] if index in BY_CORE else source, target)
    first_fills = [
        fills[0],
        pltpu.make_async_copy(density_in, density, d_load.at[0]),
        pltpu.make_async_copy(orient_in, orient, d_load.at[1]),
        pltpu.make_async_copy(sharp_in, sharp, d_load.at[2]),
    ]
    fetch = pltpu.make_async_copy(images, held, load)
    for fill in first_fills:
        fill.start()
    fetch.start()
    fills.append(pltpu.make_async_copy(support_in, support, d_load.at[3]))
    forward = Forward(x_ref, a_ref, r_ref, sems[:6])
    back = Back(x_back, a_back, r_back, sems[6:])
    for fill in first_fills:
        fill.wait()

    def transform(part, half):
        for plane in range(4):
            out = dot(table[part, half], density[plane])
            for piece in range(2):
                for side in range(2):
                    stage[pl.ds(plane * 4 + piece * 2 + side, 64, stride=16), :] = out[
                        piece * 64 : piece * 64 + 64, side * 128 : side * 128 + 128
                    ]
        x_ref[part, pl.ds(half * 2, 2)] = stage[...].astype(jnp.bfloat16).reshape(2, 4, 8, 16, 128)

    other_half, own_half = 1 - y // 2, y // 2
    transform(0, other_half)
    entered()
    forward.start(0, 2)

    near = orient[...] - slab * 4
    steps = lax.broadcasted_iota(jnp.int32, (16, 64), 0) - 4 - near
    squares = (steps * steps).astype(jnp.float32)
    raw = jnp.exp(-sharp[...] * squares)
    total = 1.0 + 2.0 * (
        jnp.exp(-sharp[...])
        + jnp.exp(-4.0 * sharp[...])
        + jnp.exp(-9.0 * sharp[...])
        + jnp.exp(-16.0 * sharp[...])
    )
    mixing = jnp.where(jnp.abs(steps) <= 4, raw / total, 0.0)
    high = mixing.astype(jnp.bfloat16)
    low = (mixing - high.astype(jnp.float32)).astype(jnp.bfloat16)
    def iota(shape, axis):
        return lax.broadcasted_iota(jnp.int32, shape, axis)

    def within(at, group):
        return jnp.where(jnp.logical_and(at >= group * 8, at < group * 8 + 8), 1.0, 0.0).astype(
            jnp.bfloat16
        )

    by_plane = within(iota((96, 16), 0), iota((96, 16), 1))
    by_snapshot = within(iota((64, 512), 1), iota((64, 512), 0))
    agree = (iota((96, 512), 0) & 7) == (iota((96, 512), 1) & 7)

    def widened(part):
        rows = dot(by_plane, part).astype(jnp.bfloat16)
        return jnp.where(agree, dot(rows, by_snapshot), 0.0).astype(jnp.bfloat16)

    wide_high = widened(high)
    wide_both = jnp.concatenate([wide_high, widened(low)], axis=0)
    fetch.wait()
    for fill in fills[1:]:
        fill.start()

    def mix(index, carry):
        at = pl.multiple_of(index * 16, 16)
        rows = jnp.concatenate(
            [held[:, pl.ds(at + 8 * block, 8), :].reshape(512, 128) for block in range(2)], axis=1
        )
        upper = rows.astype(jnp.bfloat16)
        lower = (rows - upper.astype(jnp.float32)).astype(jnp.bfloat16)
        out = dot(wide_both, upper)
        out = out[:96] + out[96:] + dot(wide_high, lower)
        for plane in range(12):
            own = out[plane * 8 : plane * 8 + 8]
            sent[plane, pl.ds(at, 16), :] = jnp.concatenate(
                [own[:, :128], own[:, 128:]], axis=0
            ).astype(jnp.bfloat16)
        return carry

    lax.fori_loop(0, 8, mix, 0, unroll=4)

    def gift(index, shift, turn):
        first = 4 + 4 * shift + 2 * ((image + turn) % 2)
        return pltpu.make_async_remote_copy(
            src_ref=sent.at[pl.ds(first, 2)],
            dst_ref=got.at[index],
            send_sem=c_send.at[index],
            recv_sem=c_recv.at[index],
            device_id=beside(shift, turn),
            device_id_type=MESH,
        )

    gifts = [gift(index, *move) for index, move in enumerate(moves)]
    for copy in gifts:
        copy.start()
    forward.start(0, 3)
    transform(0, own_half)
    forward.start(0, 1)
    transform(1, other_half)
    forward.spread(0, 2)
    for copy in gifts:
        copy.wait()
    padded[...] = jnp.zeros_like(padded)
    for plane in range(2):
        own = sent[4 + 2 * image + plane].astype(jnp.float32)
        for index, (shift, turn) in enumerate(moves):
            piece = got[index, plane].astype(jnp.float32)
            if shift:
                source = slab - shift
                piece = jnp.where(jnp.logical_and(source >= 0, source < 128), piece, 0.0)
            own = own + piece
        padded[plane, pl.ds(16, 128), :] = own
    for depth in range(8):
        rows = [
            padded[plane, pl.ds(16 + first, 10), :]
            for plane in range(2)
            for first in (8 * depth - 1, 119 - 8 * depth)
        ]
        rows += [padded[plane, pl.ds(16 + 63, 2), :] for plane in range(2)]
        rows.append(jnp.zeros((4, PIX), jnp.float32))
        g_ref[depth] = jnp.concatenate(rows, axis=0).astype(jnp.bfloat16)

    def window(step):
        depth = (z + step) % 8
        return pltpu.make_async_remote_copy(
            src_ref=g_ref.at[depth],
            dst_ref=h_ref.at[z],
            send_sem=g_send,
            recv_sem=g_recv,
            device_id=device(y, x, depth, c),
            device_id_type=MESH,
        )

    for step in (4, 1, 7, 2, 6, 3, 5):
        window(step).start()
    stay = pltpu.make_async_copy(g_ref.at[z], h_ref.at[z], g_own)
    stay.start()
    forward.start(0, 0)
    transform(1, own_half)
    forward.spread(0, 3)
    forward.start(1, 2)
    for fill in fills[1:]:
        fill.wait()
    forward.spread(0, 1)
    forward.start(1, 3)
    stay.wait()
    seven = pltpu.make_async_remote_copy(
        src_ref=g_ref.at[pl.ds(0, 7)],
        dst_ref=h_ref.at[pl.ds(0, 7)],
        send_sem=g_send,
        recv_sem=g_recv,
        device_id=device(y, x, (z + 1) % 8, c),
        device_id_type=MESH,
    )
    seven.wait_send()
    seven.wait_recv()
    weights = windows[jnp.where(z == 0, 1, 0)]
    out = dot(weights, jnp.concatenate([h_ref[source] for source in range(8)], axis=1))
    for source in range(8):
        for plane in range(2):
            made[pl.ds(source * 2 + plane, 64, stride=16), :] = out[
                plane * 64 : plane * 64 + 64, source * 128 : source * 128 + 128
            ]
    whole_rows[...] = made[...].astype(jnp.bfloat16).reshape(16, 2, 2, 16, 128)

    def kept(part):
        return pltpu.make_async_copy(whole_rows.at[y * 4 + x, part], e_ref.at[part, m], e_own.at[part])

    def others(part):
        piece = e_ref.at[part, pl.ds(0, 31)]
        return pltpu.make_async_remote_copy(
            src_ref=piece,
            dst_ref=piece,
            send_sem=e_send.at[part],
            recv_sem=e_recv.at[part],
            device_id=device(y, x, (z + 1) % 8, c),
            device_id_type=MESH,
        )

    def hand_out(part):
        for d in range(1, 32):
            row, column, core = (y + d // 8) % 4, (x + d // 2 % 4) % 4, (c + d) % 2
            pltpu.make_async_remote_copy(
                src_ref=whole_rows.at[row * 4 + column, part],
                dst_ref=e_ref.at[part, m],
                send_sem=e_send.at[part],
                recv_sem=e_recv.at[part],
                device_id=device(row, column, z, core),
                device_id_type=MESH,
            ).start()
        kept(part).start()

    hand_out(0)
    forward.spread(0, 0)
    for k in (1, 0):
        forward.start(1, k)
    hand_out(1)

    def cross(index, source, target):
        return pltpu.make_async_remote_copy(
            src_ref=source,
            dst_ref=target,
            send_sem=x_send.at[index],
            recv_sem=x_recv.at[index],
            device_id=device(y, x, z, 1 - c),
            device_id_type=MESH,
        )

    def cross_forward(part):
        return cross(part, halves.at[part, 1 - c], landed.at[part, c])

    def cross_back(part):
        return cross(2 + part, half_out.at[part], half_in.at[part, c])

    def along_x(part):
        forward.arrived(part)
        wide[...] = r_ref[part].astype(jnp.float32).reshape(2048, 128)
        for piece in range(2):
            for side in range(2):
                for block in range(2):
                    at = piece * 512 + side * 256 + block * 128
                    lines[:, pl.ds(at, 128)] = wide[
                        pl.ds(side * 1024 + piece * 2 + block, 256, stride=4), :
                    ].astype(jnp.bfloat16)
        both = dot(lines[...], forward_x[part]).astype(jnp.bfloat16)
        for half in range(2):
            halves[part, half] = both[:, half * GX : half * GX + GX]
        cross_forward(part).start()
        landed[part, c] = halves[part, c]

    def rounded_root(rows, across_table):
        return jnp.sqrt(scale * dot(rows, across_table)).astype(jnp.bfloat16).astype(jnp.float32)

    def amplitudes(part):
        kept(part).wait()
        others(part).wait_send()
        others(part).wait_recv()
        near = jnp.concatenate([e_ref[part, :, row].reshape(GZ, PIX) for row in range(2)], axis=1)
        far = dot(mirror[...], near).astype(jnp.bfloat16)
        amplitude[part] = 0.5 * (
            rounded_root(near, across_x[part, 0]) + rounded_root(far, across_x[part, 1])
        )
        if part == 0:

            @pl.when(both_real)
            def _():
                amplitude_edge[...] = 0.5 * (
                    rounded_root(near, edge_across[...]) + rounded_root(far, edge_across[...])
                )

    def projection(real_z, imag_z, target):
        inverse = lax.rsqrt(real_z * real_z + imag_z * imag_z)
        factor = target * jnp.minimum(inverse, 1.0 / least_modulus)
        return (real_z * factor).astype(jnp.bfloat16), (imag_z * factor).astype(jnp.bfloat16)

    def along_z(part):
        cross_forward(part).wait()
        half_x = GX // 2
        for half in range(2):
            top = pl.ds(half * 256, 256)
            low = pl.ds(GZ + half * 256, 256)
            spectrum[top, :] = landed[part, half]
            if part == 0:

                @pl.when(both_real)
                def _():
                    at = pl.ds(half_x, 128)
                    first_lane = lax.broadcasted_iota(jnp.int32, (256, 128), 1) == 0
                    mixed = spectrum[top, at].astype(jnp.float32)
                    edge = jnp.where(first_lane, mixed, 0.0)
                    spectrum[top, at] = (mixed - edge).astype(jnp.bfloat16)
                    zero = jnp.zeros((256, 128), jnp.bfloat16)
                    edges[top, :] = jnp.concatenate([edge.astype(jnp.bfloat16), zero], axis=1)
                    edges[low, :] = jnp.concatenate([zero, (-edge).astype(jnp.bfloat16)], axis=1)

            spectrum[low, pl.ds(0, half_x)] = spectrum[top, pl.ds(half_x, half_x)]
            spectrum[low, pl.ds(half_x, half_x)] = -spectrum[top, pl.ds(0, half_x)]

    def products(block, carry):
        at = pl.ds(pl.multiple_of(block * 128, 128), 128)
        weights = forward_z[at, :]
        depth_sum[at, :] = dot(weights, spectrum[...])

        @pl.when(both_real)
        def _():
            edge_sum[at, :] = dot(weights, edges[...])

        return carry

    def project(part):
        half_x = GX // 2

        def block_of_planes(block, carry):
            at = pl.ds(pl.multiple_of(block * 128, 128), 128)
            low = pl.ds(pl.multiple_of(GZ + block * 128, 128), 128)
            total = dot(forward_z[at, :], spectrum[...]) if part else depth_sum[at, :]
            real, imag = projection(total[:, :half_x], total[:, half_x:], amplitude[part, at, :])
            projected[at, pl.ds(0, half_x)] = real
            projected[at, pl.ds(half_x, half_x)] = imag
            projected[low, pl.ds(0, half_x)] = -imag
            projected[low, pl.ds(half_x, half_x)] = real
            if part == 0:

                @pl.when(both_real)
                def _():
                    total = edge_sum[at, :]
                    real, imag = projection(total[:, :128], total[:, 128:], amplitude_edge[at, :])
                    projected_edge[at, :] = real
                    projected_edge[low, :] = -imag

            return carry

        lax.fori_loop(0, 4, block_of_planes, 0)

        def inverse(half, target):
            target[...] = dot(back_z[half], projected[...]).astype(jnp.bfloat16)
            if part == 0:

                @pl.when(both_real)
                def _():
                    first_lane = lax.broadcasted_iota(jnp.int32, (256, 128), 1) == 0
                    edge = dot(back_z[half], projected_edge[...])
                    at = pl.ds(half_x, 128)
                    target[:, at] = jnp.where(
                        first_lane, edge, target[:, at].astype(jnp.float32)
                    ).astype(jnp.bfloat16)

        inverse(1 - c, half_out.at[part])
        cross_back(part).start()
        inverse(c, half_in.at[part, c])

    def back_x(part):
        cross_back(part).wait()
        for half in range(2):
            lines[:, pl.ds(half * GX, GX)] = half_in[part, half]
        for k in (1, 0):
            row = (y + k) % 2
            out = dot(lines[...], back_x_table[part, row])
            for block in range(4):
                stage[pl.ds(block, 256, stride=4), :] = out[:, block * 128 : block * 128 + 128]
            x_back[part, row] = stage[...].astype(jnp.bfloat16).reshape(4, 8, 2, 16, 128)
            back.start(part, k)

    def along_y(part):
        back.arrived(part)
        wide[...] = r_back[part].astype(jnp.float32).reshape(2048, 128)
        for plane in range(4):
            rows = [
                jnp.concatenate(
                    [
                        wide[pl.ds(plane * 4 + piece * 2 + side, 128, stride=16), :]
                        for side in range(2)
                    ],
                    axis=1,
                ).astype(jnp.bfloat16)
                for piece in range(2)
            ]
            out = dot(back_y[part], jnp.concatenate(rows, axis=0))
            if part:
                out = final[plane] + out
                previous = density[plane].astype(jnp.float32)
                final[plane] = jnp.where(support[plane] == 1, out, previous - feedback * out)
                pltpu.make_async_copy(final.at[plane], out_ref.at[plane], o_send.at[plane]).start()
            else:
                final[plane] = out

    along_x(0)
    along_z(0)
    lax.fori_loop(0, 4, products, 0)
    forward.spread(1, 2)
    amplitudes(0)
    project(0)
    forward.spread(1, 3)
    back_x(0)
    forward.spread(1, 1)
    amplitudes(1)
    forward.spread(1, 0)
    along_x(1)
    along_z(1)
    project(1)
    back_x(1)
    back.spread(0, 1)
    back.spread(0, 0)
    along_y(0)
    back.spread(1, 1)
    back.spread(1, 0)
    along_y(1)
    forward.finish()
    back.finish()
    for plane in range(4):
        pltpu.make_async_copy(final.at[plane], out_ref.at[plane], o_send.at[plane]).wait()


def exchange_step(scale, density, orient, sharp, images, support):
    far = pl.BlockSpec(memory_space=pltpu.HBM)
    bfloat, single = jnp.bfloat16, jnp.float32
    one = pltpu.SemaphoreType.DMA
    buffers = [
        ((1, 64), jnp.int32),
        ((1, 64), single),
        (density.shape, bfloat),
        (LANDED_TILES, bfloat),
        ((2, 32, 2, 16, 128), bfloat),
        (FORWARD_TILES, bfloat),
        (FORWARD_TILES, bfloat),
        ((1024, 128), single),
        ((64, 128, 128), single),
        ((12, 128, 128), bfloat),
        ((5, 2, 128, 128), bfloat),
        ((2, 160, 128), single),
        ((8, 48, 128), bfloat),
        ((8, 48, 128), bfloat),
        ((1024, 128), single),
        ((16, 2, 2, 16, 128), bfloat),
        (BACK_TILES, bfloat),
        (BACK_TILES, bfloat),
        (LANDED_TILES, bfloat),
        ((2048, 128), single),
        ((256, 2 * GX), bfloat),
        ((2, 2, 256, GX), bfloat),
        ((2, 2, 256, GX), bfloat),
        ((2 * GZ, GX), bfloat),
        ((2 * GZ, 256), bfloat),
        ((2, GZ, GX // 2), single),
        ((GZ, 128), single),
        ((GZ, GX), single),
        ((GZ, 256), single),
        ((2 * GZ, GX), bfloat),
        ((2 * GZ, 128), bfloat),
        ((2, 256, GX), bfloat),
        ((2, 2, 256, GX), bfloat),
        (density.shape, single),
        (density.shape, jnp.int32),
    ]
    fill_count = len(TABLES) + len(BY_SET + BY_SET_AND_CORE)
    return pl.pallas_call(
        functools.partial(step_kernel, scale),
        out_shape=jax.ShapeDtypeStruct(density.shape, single),
        in_specs=[far] * (5 + len(TABLES)),
        out_specs=far,
        scratch_shapes=[pltpu.VMEM(held_shape(i, t), bfloat) for i, t in enumerate(TABLES)]
        + [pltpu.VMEM(*buffer) for buffer in buffers]
        + [one((4,)), one((fill_count,)), one, one((4,)), one((5,)), one((5,)), one, one, one, one((2,)), one((2,)), one((2,))]
        + [one((4,)), one((4,))]
        + exchange_sems(4)
        + exchange_sems(2),
        compiler_params=pltpu.CompilerParams(
            collective_id=1, has_side_effects=True, vmem_limit_bytes=63 << 20
        ),
    )(
        orient.reshape(1, -1),
        sharp.reshape(1, -1),
        density,
        images,
        support,
        *TABLES,
    )


def body(images, orient, sharp, density, support):
    depth = density.shape[0]
    scale = depth / (images.shape[0] * lax.axis_size("img"))
    return exchange_step(scale, density, orient, sharp, images, support)


def solution(mesh):
    placed = (
        P(("img", "slab"), None, None),
        P(("img", "slab")),
        P(("img", "slab")),
        P("slab", None, "img"),
        P("slab", None, "img"),
    )
    return jax.shard_map(
        body, mesh=mesh, in_specs=placed, out_specs=P("slab", None, "img"), check_vma=False
    )
```

```python
import functools
import math

import jax
import jax.numpy as jnp
import ml_dtypes
import numpy as np
from jax import lax
from jax.experimental import pallas as pl
from jax.experimental.pallas import tpu as pltpu
from jax.sharding import PartitionSpec as P

GZ = 512
GY = 512
GX = 512
PIX = 128

least_modulus = 0.5
feedback = 0.9


def dft_tables(length):
    index = np.arange(length, dtype=np.int64)
    product = (index[:, None] * index[None, :]) % length
    angles = product.astype(np.float32) * np.float32(2.0 * math.pi / length)
    factor = np.float32(1.0 / math.sqrt(length))
    return (
        (np.cos(angles) * factor).astype(ml_dtypes.bfloat16),
        (np.sin(angles) * factor).astype(ml_dtypes.bfloat16),
    )


def interpolation(cells, pixels):
    grid = np.arange(cells, dtype=np.float32)
    detector = np.arange(pixels, dtype=np.float32)
    position = (grid + np.float32(0.5)) * np.float32(pixels / cells) - np.float32(0.5)
    return np.maximum(
        np.float32(0.0), np.float32(1.0) - np.abs(position[:, None] - detector[None, :])
    )


def bf(table):
    return np.asarray(table).astype(ml_dtypes.bfloat16)


COS, SIN = dft_tables(GY)
HALF = GY // 2
_y, _x, _z, _s = np.meshgrid(np.arange(4), np.arange(4), np.arange(8), np.arange(2), indexing="ij")
ROW_OF = 32 * _z + 8 * _y + 2 * _x + _s
_imag = np.concatenate([COS[HALF : HALF + 1], -SIN[1:HALF]])
FORWARD_Y = np.stack(
    [
        [
            np.concatenate([t[ROW_OF[2 * h : 2 * h + 2, :, :, e].reshape(-1)] for t in (COS, _imag)])
            for h in range(2)
        ]
        for e in range(2)
    ]
)
_two = 2.0 * COS[:, :HALF].astype(np.float32)
_two[:, 0] = COS[:, 0]
_sin = -2.0 * SIN[:, :HALF].astype(np.float32)
_sin[:, 0] = COS[:, HALF]
BACK_Y = np.concatenate(
    [
        bf(t.reshape(GY, 8, 16, 2).transpose(3, 0, 2, 1).reshape(2, GY, 128))
        for t in (_two, _sin)
    ],
    axis=2,
)


def quarters(upper_left, upper_right, lower_left, lower_right):
    return np.concatenate(
        [
            np.concatenate([upper_left, upper_right], axis=1),
            np.concatenate([lower_left, lower_right], axis=1),
        ],
        axis=0,
    )


FORWARD_X = np.zeros((2, 2 * GX, 2 * GX), ml_dtypes.bfloat16)
BACK_X = np.zeros((2, 2, 2 * GX, GX), ml_dtypes.bfloat16)
_low = GX // 2
_pair = np.where(np.arange(_low) == 0, 1.0, 2.0)[:, None]
_in = -SIN[:, :_low]
_in[:, 0] = COS[:, _low]
_out_re = bf(COS[:_low].astype(np.float32) * _pair)
_out_im = bf(-SIN[:_low].astype(np.float32) * _pair)
_out_im[0] = COS[_low]
for _e in range(2):
    _half = slice(_e * _low, (_e + 1) * _low)
    _place = slice(_e * GX, (_e + 1) * GX)
    FORWARD_X[0, :, _place] = quarters(COS[:, _half], -SIN[:, _half], SIN[:, _half], COS[:, _half])
    FORWARD_X[1, _place, _place] = np.concatenate([COS[:, :_low], _in], axis=1)
    for _side in range(2):
        _to = slice(_side * _low, (_side + 1) * _low)
        _cos, _sine = COS[_half, _to], SIN[_half, _to]
        BACK_X[0, _side, _place] = quarters(_cos, _sine, -_sine, _cos)
        BACK_X[1, _side, _place, _half] = np.concatenate([_out_re[:, _to], _out_im[:, _to]])
_across = interpolation(GY, PIX)
_mirror = (-np.arange(GY)) % GY
ACROSS_X = np.zeros((4, 2, 2 * PIX, _low), np.float32)
EDGE_ACROSS = np.zeros((2, 2 * PIX, PIX), np.float32)
for _e in range(2):
    _half, _rows = slice(_e * _low, (_e + 1) * _low), slice(_e * PIX, (_e + 1) * PIX)
    ACROSS_X[_e, 0, :PIX] = _across[_half].T
    ACROSS_X[_e, 1, PIX:] = _across[_mirror][_half].T
    ACROSS_X[2 + _e, 0, _rows] = _across[:_low].T
    ACROSS_X[2 + _e, 1, _rows] = _across[_mirror][:_low].T
    EDGE_ACROSS[_e, _rows, 0] = _across[_low]
ACROSS_X, EDGE_ACROSS = bf(ACROSS_X), bf(EDGE_ACROSS)
_yh, _xx, _cc, _zz, _z4 = np.meshgrid(
    np.arange(2), np.arange(4), np.arange(2), np.arange(8), np.arange(4), indexing="ij"
)
Z_ORDER = (4 * (64 * _yh + 16 * _xx + 2 * _zz + _cc) + _z4).reshape(-1)
_yh, _yl, _xx, _cc, _zz, _p2 = np.meshgrid(
    np.arange(2), np.arange(2), np.arange(4), np.arange(2), np.arange(8), np.arange(2), indexing="ij"
)
K_ORDER = (4 * (64 * _yh + 16 * _xx + 2 * _zz + _cc) + 2 * _yl + _p2).reshape(-1)
FORWARD_Z = np.concatenate([t[K_ORDER][:, Z_ORDER] for t in (COS, SIN)], axis=1)
BACK_Z = np.concatenate([COS[:, K_ORDER], SIN[:, K_ORDER]], axis=1).reshape(2, 256, 2 * GZ)
MIRROR = bf(K_ORDER[None, :] == _mirror[K_ORDER][:, None])
WINDOWS = np.zeros((2, 2, 32, 2, 48), np.float32)
for _p in range(2):
    for _m in range(32):
        for _r in range(10):
            WINDOWS[:, _p, _m, 0, 20 * _p + _r] = max(0.0, 1.0 - abs(_m / 4 + 0.625 - _r))
            WINDOWS[:, _p, _m, 1, 20 * _p + 10 + _r] = max(0.0, 1.0 - abs(8.625 - _m / 4 - _r))
    WINDOWS[1, _p, 0, 1, :] = 0.0
    WINDOWS[1, _p, 0, 1, 40 + 2 * _p : 42 + 2 * _p] = (0.375, 0.625)
WINDOWS = bf(WINDOWS.reshape(2, 128, 48))

MESH = pl.DeviceIdType.MESH


def dot(first, second):
    return jnp.dot(first, second, preferred_element_type=jnp.float32)


def place():
    slab = lax.axis_index("slab")
    return (slab // 64) * 2 + lax.axis_index("img"), (slab // 16) % 4, (slab // 2) % 8, slab % 2


def device(y, x, z, c):
    return (y % 2, (y // 2) * 64 + x * 16 + z * 2 + c)


def greet(others):
    barrier = pltpu.get_barrier_semaphore()
    for other in others:
        pl.semaphore_signal(barrier, inc=1, device_id=other, device_id_type=MESH)
    return lambda: pl.semaphore_wait(barrier, len(others))


def across(y, k):
    return (y, y + 1 - 2 * (y % 2), (y + 2) % 4, 3 - y)[k]


class Exchange:
    def __init__(self, x_ref, a_ref, r_ref, sems):
        self.x_ref, self.a_ref, self.r_ref = x_ref, a_ref, r_ref
        self.local, self.z_send, self.z_recv, self.p_send, self.p_recv, self.own = sems
        self.y, self.x, self.z, self.c = place()
        self.within = self.c == self.y // 2

    def move(self, source, target, send, recv, where):
        return pltpu.make_async_remote_copy(
            src_ref=source,
            dst_ref=target,
            send_sem=send,
            recv_sem=recv,
            device_id=device(*where),
            device_id_type=MESH,
        )

    def start(self, part, k):
        row, index = self.row(k), part * self.parts + k
        for step in (4, 1, 7, 2, 6, 3, 5):
            depth = (self.z + step) % 8
            self.move(
                self.x_ref.at[part, row, :, depth],
                self.a_ref.at[part, row, :, self.z],
                self.z_send.at[index],
                self.z_recv.at[index],
                (self.y, self.x, depth, self.c),
            ).start()
        self.keep(part, k).start()

    def keep(self, part, k):
        row = self.row(k)
        return pltpu.make_async_copy(
            self.x_ref.at[part, row, :, self.z],
            self.a_ref.at[part, row, :, self.z],
            self.local.at[part * self.parts + k],
        )

    def whole(self, part, k):
        row, index = self.row(k), part * self.parts + k
        return self.move(
            self.x_ref.at[part, row, :, pl.ds(0, 7)],
            self.a_ref.at[part, row, :, pl.ds(0, 7)],
            self.z_send.at[index],
            self.z_recv.at[index],
            (self.y, self.x, (self.z + 1) % 8, self.c),
        )

    def spread(self, part, k):
        self.keep(part, k).wait()
        self.whole(part, k).wait_recv()
        for source, where, mine in self.targets(part, k):
            target = self.r_ref.at[part, self.slot()]
            copy = self.move(source, target, self.p_send, self.p_recv.at[part], where)
            if mine:
                pl.when(self.within)(pltpu.make_async_copy(source, target, self.own.at[part]).start)
                pl.when(jnp.logical_not(self.within))(copy.start)
            else:
                copy.start()

    def blocks(self, part, count):
        piece = self.r_ref.at[part, pl.ds(0, count)]
        where = (self.y, self.x, (self.z + 1) % 8, self.c)
        return self.move(piece, piece, self.p_send, self.p_recv.at[part], where)

    def arrived(self, part):
        @pl.when(self.within)
        def _():
            source = self.r_ref.at[part, 0]
            pltpu.make_async_copy(source, self.r_ref.at[part, self.slot()], self.own.at[part]).wait()
            self.blocks(part, 15).wait_recv()

        @pl.when(jnp.logical_not(self.within))
        def _():
            self.blocks(part, 16).wait_recv()

    def finish(self):
        for part in range(2):
            for k in range(self.parts):
                self.whole(part, k).wait_send()

            @pl.when(self.within)
            def _():
                self.blocks(part, 15).wait_send()

            @pl.when(jnp.logical_not(self.within))
            def _():
                self.blocks(part, 16).wait_send()


class Forward(Exchange):
    parts = 4

    def row(self, k):
        return across(self.y, k)

    def slot(self):
        return (self.y % 2 * 4 + self.x) * 2 + self.c

    def targets(self, part, k):
        row = self.row(k)
        for dx in (2, 1, 3, 0):
            column = (self.x + dx) % 4
            where = (row, column, self.z, self.y // 2)
            yield self.a_ref.at[part, row, column], where, k == 0 and dx == 0


class Back(Exchange):
    parts = 2

    def row(self, k):
        return (self.y + k) % 2

    def slot(self):
        return self.y * 4 + self.x

    def targets(self, part, k):
        row = self.row(k)
        for dx in (2, 1, 3, 0):
            for dc in (0, 1):
                column, core = (self.x + dx) % 4, (self.c + dc) % 2
                where = (2 * self.c + row, column, self.z, core)
                yield self.a_ref.at[part, row, column, :, core], where, (k, dx, dc) == (0, 0, 0)


def exchange_sems(parts):
    one = pltpu.SemaphoreType.DMA
    return [one((2 * parts,)), one((2 * parts,)), one((2 * parts,)), one, one((2,)), one((2,))]


FORWARD_TILES = (2, 4, 4, 8, 16, 128)
BACK_TILES = (2, 2, 4, 8, 2, 16, 128)
LANDED_TILES = (2, 16, 8, 16, 128)
ORDER = (2, 3, 1, 0)


def partners():
    y, x, z, c = place()
    return [device(y, x, (z + d) % 8, c) for d in range(1, 8)] + [
        device((y + d // 8) % 4, (x + d // 2 % 4) % 4, z, (c + d) % 2) for d in range(1, 32)
    ]


TABLES = (
    FORWARD_Y, WINDOWS, FORWARD_X, FORWARD_Z, MIRROR, ACROSS_X, EDGE_ACROSS, BACK_Z, BACK_X, BACK_Y,
)
BY_SET, BY_SET_AND_CORE, BY_CORE = (2, 8), (5,), (6,)


def held_shape(index, table):
    if index in BY_SET + BY_SET_AND_CORE:
        return (2,) + table.shape[1:]
    return table.shape[1:] if index in BY_CORE else table.shape


def step_kernel(scale, orient_in, sharp_in, density_in, images, support_in, *rest):
    count = len(TABLES)
    sources, out_ref, rest = rest[:count], rest[count], rest[count + 1 :]
    tables, rest = rest[:count], rest[count:]
    (
        orient, sharp, density, r_ref, e_ref,
        x_ref, a_ref, stage, held, sent, got, padded, g_ref, h_ref, made, whole_rows,
        x_back, a_back, r_back, wide, lines, halves, landed, spectrum, edges, amplitude, amplitude_edge,
        depth_sum, edge_sum,
        projected, projected_edge, half_out, half_in, final,
        support, d_load, t_load, load, o_send, c_send, c_recv, g_send, g_recv, g_own, e_send, e_recv, e_own,
        x_send, x_recv, *sems,
    ) = rest
    (
        table, windows, forward_x, forward_z, mirror, across_x, edge_across, back_z, back_x_table, back_y,
    ) = tables
    y, x, z, c = place()
    image = lax.axis_index("img")
    slab = lax.axis_index("slab")
    m = (y * 4 + x) * 2 + c
    special = jnp.where(slab // 2 + image == 0, 1, 0)
    both_real = special == 1

    def beside(shift, turn):
        return ((image + turn) % 2, (slab + shift + 128) % 128)

    moves = [(shift, turn) for shift in (-1, 0, 1) for turn in (0, 1) if (shift, turn) != (0, 0)]
    entered = greet(partners() + [beside(*move) for move in moves])
    fills = []

    def fill(source, target):
        fills.append(pltpu.make_async_copy(source, target, t_load.at[len(fills)]))

    for index, (source, target) in enumerate(zip(sources, tables)):
        if index in BY_SET:
            fill(source.at[special], target.at[0])
            fill(source.at[0], target.at[1])
        elif index in BY_SET_AND_CORE:
            fill(source.at[special * 2 + c], target.at[0])
            fill(source.at[c], target.at[1])
        else:
            fill(source.at[c] if index in BY_CORE else source, target)
    first_fills = [
        fills[0],
        pltpu.make_async_copy(density_in, density, d_load.at[0]),
        pltpu.make_async_copy(orient_in, orient, d_load.at[1]),
        pltpu.make_async_copy(sharp_in, sharp, d_load.at[2]),
    ]
    fetch = pltpu.make_async_copy(images, held, load)
    for fill in first_fills:
        fill.start()
    fetch.start()
    fills.append(pltpu.make_async_copy(support_in, support, d_load.at[3]))
    forward = Forward(x_ref, a_ref, r_ref, sems[:6])
    back = Back(x_back, a_back, r_back, sems[6:])
    for fill in first_fills:
        fill.wait()

    def transform(part, half):
        for plane in range(4):
            out = dot(table[part, half], density[plane])
            for piece in range(2):
                for side in range(2):
                    stage[pl.ds(plane * 4 + piece * 2 + side, 64, stride=16), :] = out[
                        piece * 64 : piece * 64 + 64, side * 128 : side * 128 + 128
                    ]
        x_ref[part, pl.ds(half * 2, 2)] = stage[...].astype(jnp.bfloat16).reshape(2, 4, 8, 16, 128)

    other_half, own_half = 1 - y // 2, y // 2
    transform(0, other_half)
    entered()
    forward.start(0, 2)

    near = orient[...] - slab * 4
    steps = lax.broadcasted_iota(jnp.int32, (16, 64), 0) - 4 - near
    squares = (steps * steps).astype(jnp.float32)
    raw = jnp.exp(-sharp[...] * squares)
    total = 1.0 + 2.0 * (
        jnp.exp(-sharp[...])
        + jnp.exp(-4.0 * sharp[...])
        + jnp.exp(-9.0 * sharp[...])
        + jnp.exp(-16.0 * sharp[...])
    )
    mixing = jnp.where(jnp.abs(steps) <= 4, raw / total, 0.0)
    high = mixing.astype(jnp.bfloat16)
    low = (mixing - high.astype(jnp.float32)).astype(jnp.bfloat16)
    def iota(shape, axis):
        return lax.broadcasted_iota(jnp.int32, shape, axis)

    def within(at, group):
        return jnp.where(jnp.logical_and(at >= group * 8, at < group * 8 + 8), 1.0, 0.0).astype(
            jnp.bfloat16
        )

    by_plane = within(iota((96, 16), 0), iota((96, 16), 1))
    by_snapshot = within(iota((64, 512), 1), iota((64, 512), 0))
    agree = (iota((96, 512), 0) & 7) == (iota((96, 512), 1) & 7)

    def widened(part):
        rows = dot(by_plane, part).astype(jnp.bfloat16)
        return jnp.where(agree, dot(rows, by_snapshot), 0.0).astype(jnp.bfloat16)

    wide_high = widened(high)
    wide_both = jnp.concatenate([wide_high, widened(low)], axis=0)
    fetch.wait()
    for fill in fills[1:]:
        fill.start()

    def mix(index, carry):
        at = pl.multiple_of(index * 16, 16)
        rows = jnp.concatenate(
            [held[:, pl.ds(at + 8 * block, 8), :].reshape(512, 128) for block in range(2)], axis=1
        )
        upper = rows.astype(jnp.bfloat16)
        lower = (rows - upper.astype(jnp.float32)).astype(jnp.bfloat16)
        out = dot(wide_both, upper)
        out = out[:96] + out[96:] + dot(wide_high, lower)
        for plane in range(12):
            own = out[plane * 8 : plane * 8 + 8]
            sent[plane, pl.ds(at, 16), :] = jnp.concatenate(
                [own[:, :128], own[:, 128:]], axis=0
            ).astype(jnp.bfloat16)
        return carry

    lax.fori_loop(0, 8, mix, 0, unroll=4)

    def gift(index, shift, turn):
        first = 4 + 4 * shift + 2 * ((image + turn) % 2)
        return pltpu.make_async_remote_copy(
            src_ref=sent.at[pl.ds(first, 2)],
            dst_ref=got.at[index],
            send_sem=c_send.at[index],
            recv_sem=c_recv.at[index],
            device_id=beside(shift, turn),
            device_id_type=MESH,
        )

    gifts = [gift(index, *move) for index, move in enumerate(moves)]
    for copy in gifts:
        copy.start()
    forward.start(0, 3)
    transform(0, own_half)
    forward.start(0, 1)
    transform(1, other_half)
    forward.spread(0, 2)
    for copy in gifts:
        copy.wait()
    padded[...] = jnp.zeros_like(padded)
    for plane in range(2):
        own = sent[4 + 2 * image + plane].astype(jnp.float32)
        for index, (shift, turn) in enumerate(moves):
            piece = got[index, plane].astype(jnp.float32)
            if shift:
                source = slab - shift
                piece = jnp.where(jnp.logical_and(source >= 0, source < 128), piece, 0.0)
            own = own + piece
        padded[plane, pl.ds(16, 128), :] = own
    for depth in range(8):
        rows = [
            padded[plane, pl.ds(16 + first, 10), :]
            for plane in range(2)
            for first in (8 * depth - 1, 119 - 8 * depth)
        ]
        rows += [padded[plane, pl.ds(16 + 63, 2), :] for plane in range(2)]
        rows.append(jnp.zeros((4, PIX), jnp.float32))
        g_ref[depth] = jnp.concatenate(rows, axis=0).astype(jnp.bfloat16)

    def window(step):
        depth = (z + step) % 8
        return pltpu.make_async_remote_copy(
            src_ref=g_ref.at[depth],
            dst_ref=h_ref.at[z],
            send_sem=g_send,
            recv_sem=g_recv,
            device_id=device(y, x, depth, c),
            device_id_type=MESH,
        )

    for step in (4, 1, 7, 2, 6, 3, 5):
        window(step).start()
    stay = pltpu.make_async_copy(g_ref.at[z], h_ref.at[z], g_own)
    stay.start()
    forward.start(0, 0)
    transform(1, own_half)
    forward.spread(0, 3)
    forward.start(1, 2)
    for fill in fills[1:]:
        fill.wait()
    forward.spread(0, 1)
    forward.start(1, 3)
    stay.wait()
    seven = pltpu.make_async_remote_copy(
        src_ref=g_ref.at[pl.ds(0, 7)],
        dst_ref=h_ref.at[pl.ds(0, 7)],
        send_sem=g_send,
        recv_sem=g_recv,
        device_id=device(y, x, (z + 1) % 8, c),
        device_id_type=MESH,
    )
    seven.wait_send()
    seven.wait_recv()
    weights = windows[jnp.where(z == 0, 1, 0)]
    out = dot(weights, jnp.concatenate([h_ref[source] for source in range(8)], axis=1))
    for source in range(8):
        for plane in range(2):
            made[pl.ds(source * 2 + plane, 64, stride=16), :] = out[
                plane * 64 : plane * 64 + 64, source * 128 : source * 128 + 128
            ]
    whole_rows[...] = made[...].astype(jnp.bfloat16).reshape(16, 2, 2, 16, 128)

    def kept(part):
        return pltpu.make_async_copy(whole_rows.at[y * 4 + x, part], e_ref.at[part, m], e_own.at[part])

    def others(part):
        piece = e_ref.at[part, pl.ds(0, 31)]
        return pltpu.make_async_remote_copy(
            src_ref=piece,
            dst_ref=piece,
            send_sem=e_send.at[part],
            recv_sem=e_recv.at[part],
            device_id=device(y, x, (z + 1) % 8, c),
            device_id_type=MESH,
        )

    def hand_out(part):
        for d in range(1, 32):
            row, column, core = (y + d // 8) % 4, (x + d // 2 % 4) % 4, (c + d) % 2
            pltpu.make_async_remote_copy(
                src_ref=whole_rows.at[row * 4 + column, part],
                dst_ref=e_ref.at[part, m],
                send_sem=e_send.at[part],
                recv_sem=e_recv.at[part],
                device_id=device(row, column, z, core),
                device_id_type=MESH,
            ).start()
        kept(part).start()

    hand_out(0)
    forward.spread(0, 0)
    for k in (1, 0):
        forward.start(1, k)
    hand_out(1)

    def cross(index, source, target):
        return pltpu.make_async_remote_copy(
            src_ref=source,
            dst_ref=target,
            send_sem=x_send.at[index],
            recv_sem=x_recv.at[index],
            device_id=device(y, x, z, 1 - c),
            device_id_type=MESH,
        )

    def cross_forward(part):
        return cross(part, halves.at[part, 1 - c], landed.at[part, c])

    def cross_back(part):
        return cross(2 + part, half_out.at[part], half_in.at[part, c])

    def along_x(part):
        forward.arrived(part)
        wide[...] = r_ref[part].astype(jnp.float32).reshape(2048, 128)
        for piece in range(2):
            for side in range(2):
                for block in range(2):
                    at = piece * 512 + side * 256 + block * 128
                    lines[:, pl.ds(at, 128)] = wide[
                        pl.ds(side * 1024 + piece * 2 + block, 256, stride=4), :
                    ].astype(jnp.bfloat16)
        both = dot(lines[...], forward_x[part]).astype(jnp.bfloat16)
        for half in range(2):
            halves[part, half] = both[:, half * GX : half * GX + GX]
        cross_forward(part).start()
        landed[part, c] = halves[part, c]

    def rounded_root(rows, across_table):
        return jnp.sqrt(scale * dot(rows, across_table)).astype(jnp.bfloat16).astype(jnp.float32)

    def amplitudes(part):
        kept(part).wait()
        others(part).wait_send()
        others(part).wait_recv()
        near = jnp.concatenate([e_ref[part, :, row].reshape(GZ, PIX) for row in range(2)], axis=1)
        far = dot(mirror[...], near).astype(jnp.bfloat16)
        amplitude[part] = 0.5 * (
            rounded_root(near, across_x[part, 0]) + rounded_root(far, across_x[part, 1])
        )
        if part == 0:

            @pl.when(both_real)
            def _():
                amplitude_edge[...] = 0.5 * (
                    rounded_root(near, edge_across[...]) + rounded_root(far, edge_across[...])
                )

    def projection(real_z, imag_z, target):
        inverse = lax.rsqrt(real_z * real_z + imag_z * imag_z)
        factor = target * jnp.minimum(inverse, 1.0 / least_modulus)
        return (real_z * factor).astype(jnp.bfloat16), (imag_z * factor).astype(jnp.bfloat16)

    def along_z(part):
        cross_forward(part).wait()
        half_x = GX // 2
        for half in range(2):
            top = pl.ds(half * 256, 256)
            low = pl.ds(GZ + half * 256, 256)
            spectrum[top, :] = landed[part, half]
            if part == 0:

                @pl.when(both_real)
                def _():
                    at = pl.ds(half_x, 128)
                    first_lane = lax.broadcasted_iota(jnp.int32, (256, 128), 1) == 0
                    mixed = spectrum[top, at].astype(jnp.float32)
                    edge = jnp.where(first_lane, mixed, 0.0)
                    spectrum[top, at] = (mixed - edge).astype(jnp.bfloat16)
                    zero = jnp.zeros((256, 128), jnp.bfloat16)
                    edges[top, :] = jnp.concatenate([edge.astype(jnp.bfloat16), zero], axis=1)
                    edges[low, :] = jnp.concatenate([zero, (-edge).astype(jnp.bfloat16)], axis=1)

            spectrum[low, pl.ds(0, half_x)] = spectrum[top, pl.ds(half_x, half_x)]
            spectrum[low, pl.ds(half_x, half_x)] = -spectrum[top, pl.ds(0, half_x)]

    def products(block, carry):
        at = pl.ds(pl.multiple_of(block * 128, 128), 128)
        weights = forward_z[at, :]
        depth_sum[at, :] = dot(weights, spectrum[...])

        @pl.when(both_real)
        def _():
            edge_sum[at, :] = dot(weights, edges[...])

        return carry

    def project(part):
        half_x = GX // 2

        def block_of_planes(block, carry):
            at = pl.ds(pl.multiple_of(block * 128, 128), 128)
            low = pl.ds(pl.multiple_of(GZ + block * 128, 128), 128)
            total = dot(forward_z[at, :], spectrum[...]) if part else depth_sum[at, :]
            real, imag = projection(total[:, :half_x], total[:, half_x:], amplitude[part, at, :])
            projected[at, pl.ds(0, half_x)] = real
            projected[at, pl.ds(half_x, half_x)] = imag
            projected[low, pl.ds(0, half_x)] = -imag
            projected[low, pl.ds(half_x, half_x)] = real
            if part == 0:

                @pl.when(both_real)
                def _():
                    total = edge_sum[at, :]
                    real, imag = projection(total[:, :128], total[:, 128:], amplitude_edge[at, :])
                    projected_edge[at, :] = real
                    projected_edge[low, :] = -imag

            return carry

        lax.fori_loop(0, 4, block_of_planes, 0)

        def inverse(half, target):
            target[...] = dot(back_z[half], projected[...]).astype(jnp.bfloat16)
            if part == 0:

                @pl.when(both_real)
                def _():
                    first_lane = lax.broadcasted_iota(jnp.int32, (256, 128), 1) == 0
                    edge = dot(back_z[half], projected_edge[...])
                    at = pl.ds(half_x, 128)
                    target[:, at] = jnp.where(
                        first_lane, edge, target[:, at].astype(jnp.float32)
                    ).astype(jnp.bfloat16)

        inverse(1 - c, half_out.at[part])
        cross_back(part).start()
        inverse(c, half_in.at[part, c])

    def back_x(part):
        cross_back(part).wait()
        for half in range(2):
            lines[:, pl.ds(half * GX, GX)] = half_in[part, half]
        for k in (1, 0):
            row = (y + k) % 2
            out = dot(lines[...], back_x_table[part, row])
            for block in range(4):
                stage[pl.ds(block, 256, stride=4), :] = out[:, block * 128 : block * 128 + 128]
            x_back[part, row] = stage[...].astype(jnp.bfloat16).reshape(4, 8, 2, 16, 128)
            back.start(part, k)

    def along_y(part):
        back.arrived(part)
        wide[...] = r_back[part].astype(jnp.float32).reshape(2048, 128)
        for plane in range(4):
            rows = [
                jnp.concatenate(
                    [
                        wide[pl.ds(plane * 4 + piece * 2 + side, 128, stride=16), :]
                        for side in range(2)
                    ],
                    axis=1,
                ).astype(jnp.bfloat16)
                for piece in range(2)
            ]
            out = dot(back_y[part], jnp.concatenate(rows, axis=0))
            if part:
                out = final[plane] + out
                previous = density[plane].astype(jnp.float32)
                final[plane] = jnp.where(support[plane] == 1, out, previous - feedback * out)
                pltpu.make_async_copy(final.at[plane], out_ref.at[plane], o_send.at[plane]).start()
            else:
                final[plane] = out

    along_x(0)
    along_z(0)
    lax.fori_loop(0, 4, products, 0)
    forward.spread(1, 2)
    amplitudes(0)
    project(0)
    forward.spread(1, 3)
    back_x(0)
    forward.spread(1, 1)
    forward.spread(1, 0)
    amplitudes(1)
    along_x(1)
    along_z(1)
    project(1)
    back_x(1)
    back.spread(0, 1)
    back.spread(0, 0)
    along_y(0)
    back.spread(1, 1)
    back.spread(1, 0)
    along_y(1)
    forward.finish()
    back.finish()
    for plane in range(4):
        pltpu.make_async_copy(final.at[plane], out_ref.at[plane], o_send.at[plane]).wait()


def exchange_step(scale, density, orient, sharp, images, support):
    far = pl.BlockSpec(memory_space=pltpu.HBM)
    bfloat, single = jnp.bfloat16, jnp.float32
    one = pltpu.SemaphoreType.DMA
    buffers = [
        ((1, 64), jnp.int32),
        ((1, 64), single),
        (density.shape, bfloat),
        (LANDED_TILES, bfloat),
        ((2, 32, 2, 16, 128), bfloat),
        (FORWARD_TILES, bfloat),
        (FORWARD_TILES, bfloat),
        ((1024, 128), single),
        ((64, 128, 128), single),
        ((12, 128, 128), bfloat),
        ((5, 2, 128, 128), bfloat),
        ((2, 160, 128), single),
        ((8, 48, 128), bfloat),
        ((8, 48, 128), bfloat),
        ((1024, 128), single),
        ((16, 2, 2, 16, 128), bfloat),
        (BACK_TILES, bfloat),
        (BACK_TILES, bfloat),
        (LANDED_TILES, bfloat),
        ((2048, 128), single),
        ((256, 2 * GX), bfloat),
        ((2, 2, 256, GX), bfloat),
        ((2, 2, 256, GX), bfloat),
        ((2 * GZ, GX), bfloat),
        ((2 * GZ, 256), bfloat),
        ((2, GZ, GX // 2), single),
        ((GZ, 128), single),
        ((GZ, GX), single),
        ((GZ, 256), single),
        ((2 * GZ, GX), bfloat),
        ((2 * GZ, 128), bfloat),
        ((2, 256, GX), bfloat),
        ((2, 2, 256, GX), bfloat),
        (density.shape, single),
        (density.shape, jnp.int32),
    ]
    fill_count = len(TABLES) + len(BY_SET + BY_SET_AND_CORE)
    return pl.pallas_call(
        functools.partial(step_kernel, scale),
        out_shape=jax.ShapeDtypeStruct(density.shape, single),
        in_specs=[far] * (5 + len(TABLES)),
        out_specs=far,
        scratch_shapes=[pltpu.VMEM(held_shape(i, t), bfloat) for i, t in enumerate(TABLES)]
        + [pltpu.VMEM(*buffer) for buffer in buffers]
        + [one((4,)), one((fill_count,)), one, one((4,)), one((5,)), one((5,)), one, one, one, one((2,)), one((2,)), one((2,))]
        + [one((4,)), one((4,))]
        + exchange_sems(4)
        + exchange_sems(2),
        compiler_params=pltpu.CompilerParams(
            collective_id=1, has_side_effects=True, vmem_limit_bytes=63 << 20
        ),
    )(
        orient.reshape(1, -1),
        sharp.reshape(1, -1),
        density,
        images,
        support,
        *TABLES,
    )


def hand_over_kernel(source, target, sems):
    copies = [
        pltpu.make_async_copy(
            source.at[plane, pl.ds(half * 256, 256)],
            target.at[plane, pl.ds(half * 256, 256)],
            sems.at[plane * 2 + half],
        )
        for plane in range(4)
        for half in range(2)
    ]
    for copy in copies:
        copy.start()
    for copy in copies:
        copy.wait()


def hand_over(result):
    far = pl.BlockSpec(memory_space=pltpu.HBM)
    return pl.pallas_call(
        hand_over_kernel,
        out_shape=jax.ShapeDtypeStruct(result.shape, result.dtype),
        in_specs=[far],
        out_specs=far,
        scratch_shapes=[pltpu.SemaphoreType.DMA((8,))],
        compiler_params=pltpu.CompilerParams(vmem_limit_bytes=63 << 20),
    )(result)


def body(images, orient, sharp, density, support):
    depth = density.shape[0]
    scale = depth / (images.shape[0] * lax.axis_size("img"))
    return hand_over(exchange_step(scale, density, orient, sharp, images, support))


def solution(mesh):
    placed = (
        P(("img", "slab"), None, None),
        P(("img", "slab")),
        P(("img", "slab")),
        P("slab", None, "img"),
        P("slab", None, "img"),
    )
    return jax.shard_map(
        body, mesh=mesh, in_specs=placed, out_specs=P("slab", None, "img"), check_vma=False
    )
```
